256 devices in a mesh: blk: 64 (over z, y_hi, x), grp: 4 (over y_lo, core).
Axes of the slice: x: 4, y: 4 (y_hi: 2, y_lo: 2; y = y_hi * 2 + y_lo), z: 8, core: 2. Of those that a mesh axis runs over, the one named last changes fastest.
Arguments:
- image_embed: bfloat16 [4, 8192, 1024], P('grp', 'blk'), may hold values from -2 to 2, as said below
- text_embed: bfloat16 [4, 8192, 1024], P('grp', 'blk'), may hold values from -2 to 2
- logit_scale: float32 [], replicated, may hold values from 30 to 100
- block_input: bfloat16 [256, 7, 7, 3072], P(('blk', 'grp')), may hold values from -6 to 6
- dw_kernel: bfloat16 [7, 7, 3072], replicated, may hold values from -0.875 to 0.875
- dw_bias: bfloat16 [3072], replicated, may hold values from -0.5 to 0.5
- ln_gain: bfloat16 [3072], replicated, may hold values from 0.5 to 1.5
- block_grad: bfloat16 [256, 7, 7, 3072], P(('blk', 'grp')), may hold values from -6 to 6
Outputs:
- image_grad: bfloat16 [4, 8192, 1024], P('grp', 'blk')
- text_grad: bfloat16 [4, 8192, 1024], P('grp', 'blk')
- input_grad: bfloat16 [256, 7, 7, 3072], P(('blk', 'grp'))
- kernel_grad: float32 [7, 7, 3072], replicated
- channel_grads: float32 [3, 3072], replicated
The draws below stay inside these ranges and needn't reach their ends.
Inputs may be any that keep to these rules, and one draw needn't show every extreme that they name: `image_embed`: every row is nonzero.
All inputs are finite; a program needn't handle non-finite values.
Results may differ from the reference program's by a relative error of at most 0.0079.
Values may be sent and summed in bfloat16 or wider, within the bound.
A program may use at most 128 MiB of HBM per device.

```python
import jax
import jax.numpy as jnp
from jax import lax

E = 1024
CH = 3072
GRID = 7
KS = 7
PAIRS = 8192
GROUPS = 4
IMAGES = 256


def pair_raw(key):
    full_shape = (GROUPS, PAIRS, E)
    common = jax.random.truncated_normal(jax.random.fold_in(key, 11), -4.0, 4.0, full_shape)
    noise_image = jax.random.truncated_normal(jax.random.fold_in(key, 12), -4.0, 4.0, full_shape)
    noise_text = jax.random.truncated_normal(jax.random.fold_in(key, 13), -4.0, 4.0, full_shape)
    image_part = (0.4 * common + 0.92 * noise_image) / 32.0
    text_part = (0.4 * common + 0.92 * noise_text) / 32.0
    return (image_part, text_part)


def draw_image_embed(key, part):
    image_part, text_part = pair_raw(key)
    return image_part.astype(jnp.bfloat16)


def draw_text_embed(key, part):
    image_part, text_part = pair_raw(key)
    return text_part.astype(jnp.bfloat16)


def draw_logit_scale(key, part):
    key = jax.random.fold_in(key, 3)
    return jax.random.uniform(key, (), jnp.float32, 30.0, 100.0)


def shard_levels(stream_key, extent, cuts, smallest, top_value):
    level, own = 1.0, jax.random.fold_in(stream_key, 6)
    for dim, blocks in cuts:
        steps = jnp.exp(jax.random.uniform(jax.random.fold_in(own, dim), (blocks,), jnp.float32, smallest / len(cuts), top_value / len(cuts)))
        level = level * jnp.repeat(steps, extent[dim] // blocks).reshape([-1 if axis == dim else 1 for axis in range(len(extent))])
    return level


def gaussian(own_key, dims, scale, limit, cuts=(), kind=jnp.bfloat16):
    array = jax.random.normal(own_key, dims, jnp.float32) * scale
    if len(cuts) > 0:
        array = shard_levels(own_key, dims, cuts, -0.22, 0.18) * array
    return jnp.clip(array, min=-limit, max=limit).astype(kind)


def setup_inputs(seed: int = 0) -> dict:
    key_of = jax.random.split(jax.random.key(seed), 9)
    return {
        "image_embed": draw_image_embed(jax.random.fold_in(key_of[8], 71), 0),
        "text_embed": draw_text_embed(jax.random.fold_in(key_of[8], 71), 0),
        "logit_scale": draw_logit_scale(jax.random.fold_in(key_of[8], 71), 0),
        "block_input": gaussian(key_of[3], (IMAGES, GRID, GRID, CH), 1.0, 6.0, ((0, 256),)),
        "dw_kernel": gaussian(key_of[4], (KS, KS, CH), (KS * KS) ** -0.5, 0.875),
        "dw_bias": jnp.clip(jax.random.uniform(key_of[5], (CH,), jnp.float32, -0.5, 0.5), -0.5, 0.5).astype(jnp.bfloat16),
        "ln_gain": jnp.clip(jax.random.uniform(key_of[6], (CH,), jnp.float32, 0.5, 1.5), 0.5, 1.5).astype(jnp.bfloat16),
        "block_grad": gaussian(key_of[7], (IMAGES, GRID, GRID, CH), 1.0, 6.0, ((0, 256),)),
    }


EPS = 1e-06

def normalize(raw):
    values = raw.astype(jnp.float32)
    inverse = lax.rsqrt(lax.optimization_barrier(jnp.sum(values * values, axis=-1, keepdims=True)) + EPS)
    return (values * inverse, inverse)

def project_back(grad_hat, unit_hat, inverse):
    along = lax.optimization_barrier(jnp.sum(grad_hat * unit_hat, axis=-1, keepdims=True))
    return inverse * (grad_hat - along * unit_hat)

def log_sum_exp(logits, axis):
    peak = lax.optimization_barrier(jnp.max(logits, axis=axis, keepdims=True))
    return jnp.squeeze(peak, axis) + jnp.log(lax.optimization_barrier(jnp.sum(jnp.exp(logits - peak), axis=axis)))

def contract_last(left_side, right_side):
    return lax.dot_general(left_side, right_side, (((1,), (1,)), ((), ())), preferred_element_type=jnp.float32)

def group_loss_grads(image_rows, text_rows, logit_scale):
    unit_image, inv_image = normalize(image_rows)
    unit_text, inv_text = normalize(text_rows)
    hat_image = unit_image.astype(jnp.bfloat16)
    hat_text = unit_text.astype(jnp.bfloat16)
    logits = contract_last(hat_image, hat_text) * logit_scale
    row_lse = log_sum_exp(logits, 1)
    col_lse = log_sum_exp(logits, 0)
    weights = (0.5 * (jnp.exp(logits - row_lse[:, None]) + jnp.exp(logits - col_lse[None, :]))).astype(jnp.bfloat16)
    grad_image = logit_scale * (jnp.dot(weights, hat_text, preferred_element_type=jnp.float32) - hat_text.astype(jnp.float32))
    grad_text = logit_scale * (lax.dot_general(weights, hat_image, (((0,), (0,)), ((), ())), preferred_element_type=jnp.float32) - hat_image.astype(jnp.float32))
    image_grad = project_back(grad_image, unit_image, inv_image).astype(jnp.bfloat16)
    text_grad = project_back(grad_text, unit_text, inv_text).astype(jnp.bfloat16)
    return (image_grad, text_grad)

def block_terms(image, upstream, kernel, bias, gain):
    edge = KS // 2
    padded = jnp.pad(image.astype(jnp.float32), ((edge, edge), (edge, edge), (0, 0)))
    kernel_f = kernel.astype(jnp.float32)
    conv_out = jnp.zeros(image.shape, jnp.float32) + bias.astype(jnp.float32)
    for tap_row in range(KS):
        for tap_col in range(KS):
            conv_out = conv_out + padded[tap_row:tap_row + GRID, tap_col:tap_col + GRID] * kernel_f[tap_row, tap_col]
    centre = conv_out - lax.optimization_barrier(jnp.mean(conv_out, axis=-1, keepdims=True))
    inv_std = lax.rsqrt(lax.optimization_barrier(jnp.mean(centre * centre, axis=-1, keepdims=True)) + EPS)
    normed = centre * inv_std
    upstream_f = upstream.astype(jnp.float32)
    d_normed = upstream_f * gain.astype(jnp.float32)
    d_conv = inv_std * (d_normed - lax.optimization_barrier(jnp.mean(d_normed, axis=-1, keepdims=True)) - normed * lax.optimization_barrier(jnp.mean(d_normed * normed, axis=-1, keepdims=True)))
    kernel_term = jnp.stack([lax.optimization_barrier(jnp.sum(d_conv * padded[tap_row:tap_row + GRID, tap_col:tap_col + GRID], axis=(0, 1))) for tap_row in range(KS) for tap_col in range(KS)])
    d_padded = jnp.pad(d_conv, ((edge, edge), (edge, edge), (0, 0)))
    d_input = jnp.zeros(image.shape, jnp.float32)
    for tap_row in range(KS):
        for tap_col in range(KS):
            start_row = KS - 1 - tap_row
            start_col = KS - 1 - tap_col
            d_input = d_input + d_padded[start_row:start_row + GRID, start_col:start_col + GRID] * kernel_f[tap_row, tap_col]
    channel_term = jnp.stack([lax.optimization_barrier(jnp.sum(d_conv, axis=(0, 1))), lax.optimization_barrier(jnp.sum(upstream_f * normed, axis=(0, 1))), lax.optimization_barrier(jnp.sum(upstream_f, axis=(0, 1)))])
    return (d_input.astype(jnp.bfloat16), jnp.concatenate([kernel_term, channel_term], axis=0))

def reference(image_embed, text_embed, logit_scale, block_input, dw_kernel, dw_bias, ln_gain, block_grad):
    image_grad, text_grad = lax.map(lambda pair: group_loss_grads(pair[0], pair[1], logit_scale), (image_embed, text_embed))
    input_grad, terms = jax.vmap(block_terms, in_axes=(0, 0, None, None, None))(block_input, block_grad, dw_kernel, dw_bias, ln_gain)
    totals = lax.optimization_barrier(jnp.sum(terms, axis=0)) / IMAGES
    kernel_grad = totals[:KS * KS].reshape(KS, KS, totals.shape[1])
    channel_grads = totals[KS * KS:]
    return (image_grad, text_grad, input_grad, kernel_grad, channel_grads)
```

```python
import functools
import jax
import jax.numpy as jnp
from jax import lax
from jax.experimental import pallas as pl
from jax.experimental.pallas import tpu as pltpu
from jax.sharding import PartitionSpec as P

GRID = 7
KS = 7
EPS = 1e-06
LANES = 128
TILES = 24
SPOTS = GRID * GRID
HALF = KS // 2


def spot_mean(value, count):
    folded = value[:, 0:8] + value[:, 8:16] + value[:, 16:24]
    folded = jnp.sum(folded, axis=1, keepdims=True)
    return jnp.sum(folded, axis=2, keepdims=True) * (1.0 / count)


def conv_kernel(x_ref, g_ref, k_ref, bias_ref, gain_ref, din_ref, kg_ref, cg_ref, xs, gs, ks, cs, ds, bs, acc):
    channels = TILES * LANES

    def spread(src, dst):
        for y in range(GRID):
            for t in range(TILES):
                dst[pl.ds(y * GRID * TILES + t, GRID, stride=TILES), :] = src[
                    y, :, t * LANES : (t + 1) * LANES
                ].astype(jnp.float32)

    spread(x_ref, xs)
    spread(k_ref, ks)
    spread(g_ref, gs)
    for t in range(TILES):
        bs[t : t + 1, :] = bias_ref[0:1, t * LANES : (t + 1) * LANES].astype(jnp.float32)
        bs[TILES + t : TILES + t + 1, :] = gain_ref[0:1, t * LANES : (t + 1) * LANES].astype(jnp.float32)

    def rows(part, spot):
        return pl.ds(pl.multiple_of(spot * TILES + part * 8, 8), 8)

    def gather(src, part, row):
        return [src[rows(part, row * GRID + x), :] for x in range(GRID)]

    @pl.loop(0, TILES // 8)
    def _(part):
        bias = bs[pl.ds(pl.multiple_of(part * 8, 8), 8), :]
        for y in range(GRID):
            sums = [bias] * GRID
            for a in range(KS):
                if not 0 <= y + a - HALF < GRID:
                    continue
                left = gather(xs, part, y + a - HALF)
                taps = gather(ks, part, a)
                for x in range(GRID):
                    for b in range(KS):
                        if 0 <= x + b - HALF < GRID:
                            sums[x] = sums[x] + left[x + b - HALF] * taps[b]
            for x in range(GRID):
                cs[rows(part, y * GRID + x), :] = sums[x]

    gain = bs[TILES : 2 * TILES, :][None]
    dsum = jnp.zeros((TILES, LANES), jnp.float32)
    nsum = jnp.zeros((TILES, LANES), jnp.float32)
    gsum = jnp.zeros((TILES, LANES), jnp.float32)
    for y in range(GRID):
        span = slice(y * GRID * TILES, (y + 1) * GRID * TILES)
        conv = cs[span, :].reshape(GRID, TILES, LANES)
        grad = gs[span, :].reshape(GRID, TILES, LANES)
        centre = conv - spot_mean(conv, channels)
        d_normed = grad * gain
        inv = lax.rsqrt(spot_mean(centre * centre, channels) + EPS)
        normed = centre * inv
        d_conv = inv * (
            d_normed - spot_mean(d_normed, channels) - normed * spot_mean(d_normed * normed, channels)
        )
        ds[span, :] = d_conv.reshape(GRID * TILES, LANES)
        dsum = dsum + jnp.sum(d_conv, axis=0)
        nsum = nsum + jnp.sum(grad * normed, axis=0)
        gsum = gsum + jnp.sum(grad, axis=0)
    cg_ref[0] = dsum
    cg_ref[1] = nsum
    cg_ref[2] = gsum

    @pl.loop(0, TILES // 8)
    def _(part):
        for y in range(GRID):
            sums = [None] * GRID
            for a in range(KS):
                if not 0 <= y - a + HALF < GRID:
                    continue
                left = gather(ds, part, y - a + HALF)
                taps = gather(ks, part, a)
                for x in range(GRID):
                    for b in range(KS):
                        if 0 <= x - b + HALF < GRID:
                            term = left[x - b + HALF] * taps[b]
                            sums[x] = term if sums[x] is None else sums[x] + term
            for x in range(GRID):
                cs[rows(part, y * GRID + x), :] = sums[x]
        for a in range(KS):
            sums = [None] * KS
            for y in range(GRID):
                if not 0 <= y + a - HALF < GRID:
                    continue
                left = gather(ds, part, y)
                right = gather(xs, part, y + a - HALF)
                for b in range(KS):
                    for x in range(GRID):
                        if 0 <= x + b - HALF < GRID:
                            term = left[x] * right[x + b - HALF]
                            sums[b] = term if sums[b] is None else sums[b] + term
            for b in range(KS):
                kg_ref[a * KS + b, pl.ds(pl.multiple_of(part * 8, 8), 8), :] = sums[b]

    for y in range(GRID):
        for t in range(TILES):
            din_ref[y, :, t * LANES : (t + 1) * LANES] = cs[
                pl.ds(y * GRID * TILES + t, GRID, stride=TILES), :
            ].astype(jnp.bfloat16)


def conv_block(x, g, k, bias, gain):
    f32 = jnp.float32
    big = pltpu.VMEM((SPOTS * TILES, LANES), f32)
    return pl.pallas_call(
        conv_kernel,
        out_shape=(
            jax.ShapeDtypeStruct((GRID, GRID, TILES * LANES), jnp.bfloat16),
            jax.ShapeDtypeStruct((SPOTS, TILES, LANES), f32),
            jax.ShapeDtypeStruct((3, TILES, LANES), f32),
        ),
        in_specs=[pl.BlockSpec(memory_space=pltpu.VMEM)] * 5,
        out_specs=[pl.BlockSpec(memory_space=pltpu.VMEM)] * 3,
        scratch_shapes=[big, big, big, big, big, pltpu.VMEM((2 * TILES, LANES), f32), pltpu.VMEM((8, LANES), f32)],
        compiler_params=pltpu.CompilerParams(vmem_limit_bytes=24 << 20),
        cost_estimate=pl.CostEstimate(flops=30_000_000, bytes_accessed=2_500_000, transcendentals=49),
    )(x, g, k, bias.reshape(1, -1), gain.reshape(1, -1))


AROUND = 8


def normalize(raw):
    values = raw.astype(jnp.float32)
    inverse = lax.rsqrt(jnp.sum(values * values, axis=-1, keepdims=True) + EPS)
    return (values * inverse, inverse)


def project_back(grad_hat, unit_hat, inverse):
    along = jnp.sum(grad_hat * unit_hat, axis=-1, keepdims=True)
    return inverse * (grad_hat - along * unit_hat)


def contract(left, right, dims):
    return lax.dot_general(left, right, ((dims[0], dims[1]), ((), ())), preferred_element_type=jnp.float32)


def lse_over(logits, axis, groups):
    peak = jnp.max(logits, axis=axis)
    mass = jnp.sum(jnp.exp(logits - jnp.expand_dims(peak, axis)), axis=axis)
    both = lax.all_gather(jnp.stack([peak, mass]), "blk", axis_index_groups=groups)
    top = jnp.max(both[:, 0], axis=0)
    return top + jnp.log(jnp.sum(both[:, 1] * jnp.exp(both[:, 0] - top), axis=0))


def per_device(
    image_embed, text_embed, logit_scale, block_input, dw_kernel, dw_bias, ln_gain, block_grad
):
    d_input, kterm, cterm = conv_block(block_input[0], block_grad[0], dw_kernel, dw_bias, ln_gain)
    totals = lax.psum(jnp.concatenate([kterm, cterm], axis=0), ("blk", "grp"))
    totals = totals / (lax.axis_size("blk") * lax.axis_size("grp"))
    kernel_grad = totals[:SPOTS].reshape(KS, KS, TILES * LANES)
    channel_grads = totals[SPOTS:].reshape(3, TILES * LANES)
    lines = [[z * AROUND + b for z in range(AROUND)] for b in range(AROUND)]
    sheets = [[z * AROUND + b for b in range(AROUND)] for z in range(AROUND)]
    unit_image, inv_image = normalize(image_embed[0])
    unit_text, inv_text = normalize(text_embed[0])
    hat_image = unit_image.astype(jnp.bfloat16)
    hat_text = unit_text.astype(jnp.bfloat16)
    images = lax.all_gather(hat_image, "blk", axis=0, tiled=True, axis_index_groups=sheets)
    texts = lax.all_gather(hat_text, "blk", axis=0, tiled=True, axis_index_groups=lines)
    logits = contract(images, texts, ((1,), (1,))) * logit_scale
    row_lse = lse_over(logits, 1, sheets)
    col_lse = lse_over(logits, 0, lines)
    weights = (
        0.5 * (jnp.exp(logits - row_lse[:, None]) + jnp.exp(logits - col_lse[None, :]))
    ).astype(jnp.bfloat16)
    part_image = contract(weights, texts, ((1,), (0,))).astype(jnp.bfloat16)
    part_text = contract(weights, images, ((0,), (0,))).astype(jnp.bfloat16)
    sum_image = lax.psum_scatter(part_image, "blk", axis_index_groups=sheets, tiled=True)
    sum_text = lax.psum_scatter(part_text, "blk", axis_index_groups=lines, tiled=True)
    grad_image = logit_scale * (sum_image.astype(jnp.float32) - hat_text.astype(jnp.float32))
    grad_text = logit_scale * (sum_text.astype(jnp.float32) - hat_image.astype(jnp.float32))
    image_grad = project_back(grad_image, unit_image, inv_image).astype(jnp.bfloat16)
    text_grad = project_back(grad_text, unit_text, inv_text).astype(jnp.bfloat16)
    return (image_grad[None], text_grad[None], d_input[None], kernel_grad, channel_grads)


def solution(mesh):
    placed = (
        P("grp", "blk", None),
        P("grp", "blk", None),
        P(),
        P(("blk", "grp"), None, None, None),
        P(),
        P(),
        P(),
        P(("blk", "grp"), None, None, None),
    )
    return jax.shard_map(
        per_device,
        mesh=mesh,
        in_specs=placed,
        out_specs=(
            P("grp", "blk", None),
            P("grp", "blk", None),
            P(("blk", "grp"), None, None, None),
            P(),
            P(),
        ),
        check_vma=False,
    )
```

```python
import functools
import math

import jax
import jax.numpy as jnp
from jax import lax
from jax.experimental import pallas as pl
from jax.experimental.pallas import tpu as pltpu
from jax.sharding import PartitionSpec as P

GRID = 7
KS = 7
EPS = 1e-06
LANES = 128
TILES = 24
SPOTS = GRID * GRID
HALF = KS // 2


def spot_mean(value, count):
    folded = value[:, 0:8] + value[:, 8:16] + value[:, 16:24]
    folded = jnp.sum(folded, axis=1, keepdims=True)
    return jnp.sum(folded, axis=2, keepdims=True) * (1.0 / count)


def conv_kernel(x_ref, g_ref, k_ref, bias_ref, gain_ref, din_ref, terms_ref, xs, gs, ks, cs, ds, bs):
    channels = TILES * LANES

    def spread(src, dst):
        for y in range(GRID):
            for t in range(TILES):
                dst[pl.ds(y * GRID * TILES + t, GRID, stride=TILES), :] = src[
                    y, :, t * LANES : (t + 1) * LANES
                ].astype(jnp.float32)

    spread(x_ref, xs)
    spread(k_ref, ks)
    spread(g_ref, gs)
    for t in range(TILES):
        bs[t : t + 1, :] = bias_ref[0:1, t * LANES : (t + 1) * LANES].astype(jnp.float32)
        bs[TILES + t : TILES + t + 1, :] = gain_ref[0:1, t * LANES : (t + 1) * LANES].astype(jnp.float32)

    def rows(part, spot):
        return pl.ds(pl.multiple_of(spot * TILES + part * 8, 8), 8)

    def gather(src, part, row):
        return [src[rows(part, row * GRID + x), :] for x in range(GRID)]

    @pl.loop(0, TILES // 8)
    def _(part):
        bias = bs[pl.ds(pl.multiple_of(part * 8, 8), 8), :]
        for y in range(GRID):
            sums = [bias] * GRID
            for a in range(KS):
                if not 0 <= y + a - HALF < GRID:
                    continue
                left = gather(xs, part, y + a - HALF)
                taps = gather(ks, part, a)
                for x in range(GRID):
                    for b in range(KS):
                        if 0 <= x + b - HALF < GRID:
                            sums[x] = sums[x] + left[x + b - HALF] * taps[b]
            for x in range(GRID):
                cs[rows(part, y * GRID + x), :] = sums[x]

    gain = bs[TILES : 2 * TILES, :][None]
    dsum = jnp.zeros((TILES, LANES), jnp.float32)
    nsum = jnp.zeros((TILES, LANES), jnp.float32)
    gsum = jnp.zeros((TILES, LANES), jnp.float32)
    for y in range(GRID):
        span = slice(y * GRID * TILES, (y + 1) * GRID * TILES)
        conv = cs[span, :].reshape(GRID, TILES, LANES)
        grad = gs[span, :].reshape(GRID, TILES, LANES)
        centre = conv - spot_mean(conv, channels)
        d_normed = grad * gain
        inv = lax.rsqrt(spot_mean(centre * centre, channels) + EPS)
        normed = centre * inv
        d_conv = inv * (
            d_normed - spot_mean(d_normed, channels) - normed * spot_mean(d_normed * normed, channels)
        )
        ds[span, :] = d_conv.reshape(GRID * TILES, LANES)
        dsum = dsum + jnp.sum(d_conv, axis=0)
        nsum = nsum + jnp.sum(grad * normed, axis=0)
        gsum = gsum + jnp.sum(grad, axis=0)
    first = SPOTS * TILES
    for index, total in enumerate((dsum, nsum, gsum)):
        terms_ref[first + index * TILES : first + (index + 1) * TILES, :] = total
    first = first + 3 * TILES
    terms_ref[first:SLACK, :] = jnp.zeros((SLACK - first, LANES), jnp.float32)

    @pl.loop(0, TILES // 8)
    def _(part):
        for y in range(GRID):
            sums = [None] * GRID
            for a in range(KS):
                if not 0 <= y - a + HALF < GRID:
                    continue
                left = gather(ds, part, y - a + HALF)
                taps = gather(ks, part, a)
                for x in range(GRID):
                    for b in range(KS):
                        if 0 <= x - b + HALF < GRID:
                            term = left[x - b + HALF] * taps[b]
                            sums[x] = term if sums[x] is None else sums[x] + term
            for x in range(GRID):
                cs[rows(part, y * GRID + x), :] = sums[x]
        for a in range(KS):
            sums = [None] * KS
            for y in range(GRID):
                if not 0 <= y + a - HALF < GRID:
                    continue
                left = gather(ds, part, y)
                right = gather(xs, part, y + a - HALF)
                for b in range(KS):
                    for x in range(GRID):
                        if 0 <= x + b - HALF < GRID:
                            term = left[x] * right[x + b - HALF]
                            sums[b] = term if sums[b] is None else sums[b] + term
            for b in range(KS):
                terms_ref[rows(part, a * KS + b), :] = sums[b]

    for y in range(GRID):
        for t in range(TILES):
            din_ref[y, :, t * LANES : (t + 1) * LANES] = cs[
                pl.ds(y * GRID * TILES + t, GRID, stride=TILES), :
            ].astype(jnp.bfloat16)


def conv_block(x, g, k, bias, gain):
    f32 = jnp.float32
    big = pltpu.VMEM((SPOTS * TILES, LANES), f32)
    return pl.pallas_call(
        conv_kernel,
        out_shape=(
            jax.ShapeDtypeStruct((GRID, GRID, TILES * LANES), jnp.bfloat16),
            jax.ShapeDtypeStruct((SLACK, LANES), f32),
        ),
        in_specs=[pl.BlockSpec(memory_space=pltpu.VMEM)] * 5,
        out_specs=[pl.BlockSpec(memory_space=pltpu.VMEM)] * 2,
        scratch_shapes=[big, big, big, big, big, pltpu.VMEM((2 * TILES, LANES), f32)],
        compiler_params=pltpu.CompilerParams(vmem_limit_bytes=24 << 20),
        cost_estimate=pl.CostEstimate(flops=30_000_000, bytes_accessed=2_500_000, transcendentals=49),
    )(x, g, k, bias.reshape(1, -1), gain.reshape(1, -1))


ROWS = 128
PART = 64
WIDE = 256
MESH = pl.DeviceIdType.MESH
SLACK = 1280
HIGH_SHIFT = 12.0
LOW_SHIFT = 10.0
LOW_CAP = 30.0
LOW_LIMIT = 55.0


class Geometry:
    def __init__(self, z, y_hi, x, y_lo, core, width):
        self.z, self.y_hi, self.x, self.y_lo, self.core, self.width = z, y_hi, x, y_lo, core, width
        self.sheet = y_hi * x
        self.y = y_hi * y_lo
        self.half = SLACK // core
        self.y_rows = self.half // self.y
        self.x_rows = self.y_rows // x


def dot(left, right, dims=((1,), (0,))):
    return lax.dot_general(left, right, (dims, ((), ())), preferred_element_type=jnp.float32)


def loss_kernel(
    geo, scale_ref, img_ref, txt_ref, terms_ref, ig_ref, tg_ref, kg_ref, cg_ref,
    ia, ta, ui, ut, vi, vt, probs, weights, flip, row_hi, row_lo, alpha, beta, row_all, col_all, gz, gx,
    zout, zin, xout, xin, yout, yin, l1, hsum, l2, qsum, l3, l4, fin,
    zag_s, zag_r, xag_s, xag_r, yag_s, yag_r, row_s, row_r, col_s, col_r,
    zrs_s, zrs_r, xrs_s, xrs_r, yrs_s, yrs_r,
    s1, r1, s2, r2, s3, r3, s4, r4, s5, r5, s6, r6, s7, r7,
):
    f32, bf16 = jnp.float32, jnp.bfloat16
    nz, nx, sheet = geo.z, geo.x, geo.sheet
    blk, grp = lax.axis_index("blk"), lax.axis_index("grp")
    z, b = blk // sheet, lax.rem(blk, sheet)
    yh, x = b // nx, lax.rem(b, nx)
    yl, core = grp // geo.core, lax.rem(grp, geo.core)
    y = yh * geo.y_lo + yl
    hy = 1 - yh

    def place(z_to, yh_to, x_to):
        return {"blk": z_to * sheet + yh_to * nx + x_to, "grp": grp}

    def column(y_to):
        return {
            "blk": z * sheet + (y_to // geo.y_lo) * nx + x,
            "grp": lax.rem(y_to, geo.y_lo) * geo.core + core,
        }

    def turn(value, by, size):
        return lax.rem(value + by + size, size)

    mate = {"blk": blk, "grp": yl * geo.core + (geo.core - 1 - core)}
    facing = place(z, hy, x)
    sent = []

    def copy(src, dst, send, recv, to):
        return pltpu.make_async_remote_copy(
            src_ref=src, dst_ref=dst, send_sem=send, recv_sem=recv, device_id=to, device_id_type=MESH
        )

    def start(*args):
        moving = copy(*args)
        moving.start()
        sent.append(moving)

    def arrived(dst, send, recv):
        copy(dst, dst, send, recv, facing).wait_recv()

    barrier = pltpu.get_barrier_semaphore()
    peers = [place(turn(z, o, nz), yh, x) for o in range(1, nz)]
    for q in range(2):
        for o in range(nx):
            if q or o:
                peers.append(place(z, hy if q else yh, turn(x, o, nx)))
    for o in range(1, geo.y):
        if o != geo.y_lo:
            peers.append(column(turn(y, o, geo.y)))
    peers.append(mate)
    for peer in peers:
        pl.semaphore_signal(barrier, inc=1, device_id=peer, device_id_type=MESH)

    def slot(index, part):
        return pl.ds(pl.multiple_of(index * ROWS + part * PART, PART), PART)

    def full(index):
        return pl.ds(pl.multiple_of(index * ROWS, ROWS), ROWS)

    def unit_rows(raw, unit, inverse, everyone, index):
        values = raw[...].astype(f32)
        inv = lax.rsqrt(jnp.sum(values * values, axis=-1, keepdims=True) + EPS)
        scaled = values * inv
        unit[...] = scaled
        inverse[...] = inv
        everyone[full(index), :] = scaled.astype(bf16)

    unit_rows(txt_ref, ut, vt, ta, z)
    unit_rows(img_ref, ui, vi, ia, b)
    pl.semaphore_wait(barrier, len(peers))

    def sign(d):
        return 1 - 2 * d

    def z_gather(d, k):
        rows = slot(turn(z, -sign(d) * (k // 2), nz), (k % 2) ^ d)
        to = place(turn(z, sign(d), nz), yh, x)
        start(ta.at[rows], ta.at[rows], zag_s.at[d, k], zag_r.at[d, k], to)

    def z_gathered(d, k):
        rows = slot(turn(z, -sign(d) * (k // 2 + 1), nz), (k % 2) ^ d)
        arrived(ta.at[rows], zag_s.at[d, k], zag_r.at[d, k])

    def x_gather(q, d, k):
        rows = slot((hy if q else yh) * nx + turn(x, -sign(d) * (k // 2), nx), (k % 2) ^ d)
        to = place(z, yh, turn(x, sign(d), nx))
        start(ia.at[rows], ia.at[rows], xag_s.at[q, d, k], xag_r.at[q, d, k], to)

    def x_gathered(q, d, k):
        rows = slot((hy if q else yh) * nx + turn(x, -sign(d) * (k // 2 + 1), nx), (k % 2) ^ d)
        arrived(ia.at[rows], xag_s.at[q, d, k], xag_r.at[q, d, k])

    def y_gather(c):
        start(ia.at[slot(b, c)], ia.at[slot(b, c)], yag_s.at[c], yag_r.at[c], facing)

    def y_gathered(c):
        arrived(ia.at[slot(hy * nx + x, c)], yag_s.at[c], yag_r.at[c])

    def share(first, rows):
        return pl.ds(pl.multiple_of(first, 8), rows)

    def mate_send():
        start(terms_ref.at[share((geo.core - 1 - core) * geo.half, geo.half)], l1, s1.at[0], r1.at[0], mate)

    def mate_sum():
        arrived(l1, s1.at[0], r1.at[0])
        hsum[...] = terms_ref[share(core * geo.half, geo.half), :] + l1[...]

    def y_send():
        for o in range(1, geo.y):
            to = turn(y, o, geo.y)
            start(hsum.at[share(to * geo.y_rows, geo.y_rows)], l2.at[o], s2.at[o], r2.at[o], column(to))

    def y_sum():
        total = hsum[share(y * geo.y_rows, geo.y_rows), :]
        for o in range(1, geo.y):
            arrived(l2.at[o], s2.at[o], r2.at[o])
            total = total + l2[o]
        qsum[...] = total

    def x_send():
        for o in range(1, nx):
            to = turn(x, o, nx)
            start(qsum.at[share(to * geo.x_rows, geo.x_rows)], l3.at[o], s3.at[o], r3.at[o], place(z, yh, to))

    def x_sum():
        total = qsum[share(x * geo.x_rows, geo.x_rows), :]
        for o in range(1, nx):
            arrived(l3.at[o], s3.at[o], r3.at[o])
            total = total + l3[o]
        l4[z] = total

    def z_send():
        for o in range(1, nz):
            start(l4.at[z], l4.at[z], s4.at[o], r4.at[o], place(turn(z, o, nz), yh, x))

    mine = core * geo.half + y * geo.y_rows + x * geo.x_rows

    def z_sum():
        for o in range(1, nz):
            arrived(l4.at[turn(z, -o, nz)], s4.at[o], r4.at[o])
        total = l4[0]
        for o in range(1, nz):
            total = total + l4[o]
        fin[share(mine, geo.x_rows), :] = total * (1.0 / (geo.z * geo.sheet * geo.y_lo * geo.core))

    def x_spread():
        rows = fin.at[share(mine, geo.x_rows)]
        for o in range(1, nx):
            start(rows, rows, s5.at[o], r5.at[o], place(z, yh, turn(x, o, nx)))

    def x_spread_done():
        for o in range(1, nx):
            first = core * geo.half + y * geo.y_rows + turn(x, -o, nx) * geo.x_rows
            arrived(fin.at[share(first, geo.x_rows)], s5.at[o], r5.at[o])

    def y_spread():
        rows = fin.at[share(core * geo.half + y * geo.y_rows, geo.y_rows)]
        for o in range(1, geo.y):
            start(rows, rows, s6.at[o], r6.at[o], column(turn(y, o, geo.y)))

    def y_spread_done():
        for o in range(1, geo.y):
            first = core * geo.half + turn(y, -o, geo.y) * geo.y_rows
            arrived(fin.at[share(first, geo.y_rows)], s6.at[o], r6.at[o])

    def mate_spread():
        rows = fin.at[share(core * geo.half, geo.half)]
        start(rows, rows, s7.at[0], r7.at[0], mate)

    def mate_spread_done():
        arrived(fin.at[share((geo.core - 1 - core) * geo.half, geo.half)], s7.at[0], r7.at[0])

    half_scale = scale_ref[0] * 0.5
    row_hi[...] = jnp.zeros_like(row_hi)
    row_lo[...] = jnp.zeros_like(row_lo)
    blocks = nz * ROWS // WIDE
    late = turn(z, nz // 2, nz) // (WIDE // ROWS)

    def logits_block(n):
        lanes = pl.ds(pl.multiple_of(n * WIDE, WIDE), WIDE)

        def rows_step(m, sums):
            rows = pl.ds(pl.multiple_of(m * WIDE, WIDE), WIDE)
            logits = dot(ia[rows, :], ta[lanes, :], ((1,), (1,)))
            root = jnp.exp(logits * half_scale)
            probs[rows, lanes] = root
            high = root * math.exp(-HIGH_SHIFT)
            high = high * high
            low = jnp.minimum(root * math.exp(LOW_SHIFT), math.exp(LOW_CAP))
            low = low * low
            row_hi[rows, :] += high[:, :ROWS] + high[:, ROWS:]
            row_lo[rows, :] += low[:, :ROWS] + low[:, ROWS:]
            return (
                sums[0] + jnp.sum(high.reshape(WIDE // 8, 8, WIDE), axis=0),
                sums[1] + jnp.sum(low.reshape(WIDE // 8, 8, WIDE), axis=0),
            )

        zero = jnp.zeros((8, WIDE), f32)
        high, low = lax.fori_loop(0, sheet * ROWS // WIDE, rows_step, (zero, zero))
        high = jnp.sum(high, axis=0, keepdims=True)
        low = jnp.sum(low, axis=0, keepdims=True)
        for j in range(WIDE // ROWS):
            at = n * (WIDE // ROWS) + j
            col_all[z, pl.ds(at, 1), :] = high[:, j * ROWS : (j + 1) * ROWS]
            col_all[z, pl.ds(8 + at, 1), :] = low[:, j * ROWS : (j + 1) * ROWS]

    def half_factor(total):
        high, low = total[0:8], total[8:16]
        small = low < math.exp(LOW_LIMIT)
        lse = jnp.where(small, jnp.log(low) - 2 * LOW_SHIFT, jnp.log(high) + 2 * HIGH_SHIFT)
        return jnp.exp(lse * -0.5) * math.sqrt(0.5)

    def weigh(tile):
        lanes = pl.ds(pl.multiple_of(tile * ROWS, ROWS), ROWS)

        def rows_step(m, carry):
            rows = pl.ds(pl.multiple_of(m * WIDE, WIDE), WIDE)
            root = probs[rows, lanes]
            by_row = root * alpha[rows, :]
            by_col = root * beta[pl.ds(tile, 1), :]
            weights[rows, lanes] = (by_row * by_row + by_col * by_col).astype(bf16)
            return carry

        lax.fori_loop(0, sheet * ROWS // WIDE, rows_step, 0)

    def text_part(j):
        flip[...] = weights[:, full(turn(z, j, nz))].T

        @pl.loop(0, geo.width // WIDE)
        def _(n):
            lanes = pl.ds(pl.multiple_of(n * WIDE, WIDE), WIDE)
            gz[j, :, lanes] = dot(flip[...], ia[:, lanes])

    def image_part(q, j):
        rows = full((yh if q else hy) * nx + turn(x, j, nx))

        @pl.loop(0, geo.width // WIDE)
        def _(n):
            lanes = pl.ds(pl.multiple_of(n * WIDE, WIDE), WIDE)
            gx[q * nx + j, :, lanes] = dot(weights[rows, :], ta[:, lanes])

    def ring_rows(d, k):
        part = (k % 2) ^ d
        return slice(part * PART, (part + 1) * PART)

    def ring_target(d, k, size):
        away = size // 2 - (k + 1) // 2
        return (sign(d) * away) % size

    def z_reduce(d, k):
        value = gz[ring_target(d, k, nz), ring_rows(d, k), :]
        if k >= 2:
            arrived(zin.at[d, k - 2], zrs_s.at[d, k - 2], zrs_r.at[d, k - 2])
            value = value + zin[d, k - 2].astype(f32)
        zout[d, k] = value.astype(bf16)
        to = place(turn(z, sign(d), nz), yh, x)
        start(zout.at[d, k], zin.at[d, k], zrs_s.at[d, k], zrs_r.at[d, k], to)

    def x_reduce(q, d, k):
        value = gx[q * nx + ring_target(d, k, nx), ring_rows(d, k), :]
        if k >= 2:
            arrived(xin.at[q, d, k - 2], xrs_s.at[q, d, k - 2], xrs_r.at[q, d, k - 2])
            value = value + xin[q, d, k - 2].astype(f32)
        xout[q, d, k] = value.astype(bf16)
        to = place(z, yh, turn(x, sign(d), nx))
        start(xout.at[q, d, k], xin.at[q, d, k], xrs_s.at[q, d, k], xrs_r.at[q, d, k], to)

    def ring_last(size):
        return [k for k in (size - 3, size - 2) if k >= 0]

    def x_total(q, c):
        value = gx[q * nx, c * PART : (c + 1) * PART, :]
        for d in range(2):
            for k in ring_last(nx):
                if (k % 2) ^ d == c:
                    arrived(xin.at[q, d, k], xrs_s.at[q, d, k], xrs_r.at[q, d, k])
                    value = value + xin[q, d, k].astype(f32)
        return value

    def z_total(c):
        value = gz[0, c * PART : (c + 1) * PART, :]
        for d in range(2):
            for k in ring_last(nz):
                if (k % 2) ^ d == c:
                    arrived(zin.at[d, k], zrs_s.at[d, k], zrs_r.at[d, k])
                    value = value + zin[d, k].astype(f32)
        return value

    def finish(total, other, unit, inverse, out, c):
        rows = slice(c * PART, (c + 1) * PART)
        grad = scale_ref[0] * (total - other.astype(f32))
        along = jnp.sum(grad * unit[rows, :], axis=-1, keepdims=True)
        out[rows, :] = (inverse[rows, :] * (grad - along * unit[rows, :])).astype(bf16)

    both = range(2)
    kz, kx = nz - 1, nx - 1
    for k in range(min(2, kz)):
        for d in both:
            z_gather(d, k)
    for k in range(min(2, kx)):
        for d in both:
            x_gather(0, d, k)
    for c in both:
        y_gather(c)
    mate_send()

    def z_step(k):
        if k < kz:
            for d in both:
                z_gathered(d, k)
            if k + 2 < kz:
                for d in both:
                    z_gather(d, k + 2)

    def x_step(q, k):
        if k < kx:
            for d in both:
                x_gathered(q, d, k)
            if k + 2 < kx:
                for d in both:
                    x_gather(q, d, k + 2)

    z_step(0)
    x_step(0, 0)
    mate_sum()
    y_send()
    z_step(1)
    for c in both:
        y_gathered(c)
        for k in range(min(2, kx)):
            for d in both:
                if (k % 2) ^ d == c:
                    x_gather(1, d, k)
    z_step(2)
    x_step(0, 1)
    x_step(0, 2)
    y_sum()
    x_send()
    z_step(3)
    x_step(1, 0)
    z_step(4)
    x_sum()
    z_send()
    for k in range(1, kx):
        x_step(1, k)
    for k in range(5, kz - 1):
        z_step(k)

    @pl.loop(0, blocks - 1)
    def _(i):
        logits_block(lax.rem(late + 1 + i, blocks))

    if kz - 1 >= 5:
        z_step(kz - 1)
    logits_block(late)
    for m in range(sheet):
        rows = slice(m * ROWS, (m + 1) * ROWS)
        row_all[b, m : m + 1, :] = jnp.sum(row_hi[rows, :].T, axis=0, keepdims=True)
        row_all[b, 8 + m : 9 + m, :] = jnp.sum(row_lo[rows, :].T, axis=0, keepdims=True)
    for o in range(1, nz):
        start(col_all.at[z], col_all.at[z], col_s.at[o], col_r.at[o], place(turn(z, o, nz), yh, x))
    for q in both:
        for o in range(nx):
            if q or o:
                i = q * nx + o
                to = place(z, hy if q else yh, turn(x, o, nx))
                start(row_all.at[b], row_all.at[b], row_s.at[i], row_r.at[i], to)
    z_sum()
    x_spread()
    for o in range(1, nz):
        arrived(col_all.at[turn(z, -o, nz)], col_s.at[o], col_r.at[o])
    total = col_all[0]
    for o in range(1, nz):
        total = total + col_all[o]
    beta[...] = half_factor(total)
    for q in both:
        for o in range(nx):
            if q or o:
                i = q * nx + o
                arrived(row_all.at[(hy if q else yh) * nx + turn(x, -o, nx)], row_s.at[i], row_r.at[i])
    total = row_all[0]
    for o in range(1, sheet):
        total = total + row_all[o]
    factor = half_factor(total)
    for m in range(sheet):
        rows = slice(m * ROWS, (m + 1) * ROWS)
        alpha[rows, :] = jnp.broadcast_to(factor[m : m + 1, :], (ROWS, ROWS)).T

    weigh(turn(z, nz // 2, nz))
    text_part(nz // 2)
    for d in both:
        z_reduce(d, 0)

    @pl.loop(0, nz - 1)
    def _(i):
        weigh(turn(z, nz // 2 + 1 + i, 2 * nz) % nz)

    def z_stage(k):
        if k < kz:
            for d in both:
                z_reduce(d, k)

    def x_stage(q, k):
        if k < kx:
            for d in both:
                x_reduce(q, d, k)

    def text_parts(away):
        if 0 < away < nz // 2:
            text_part(away)
            text_part(nz - away)

    def image_parts(q, away):
        if 0 < away < nx // 2:
            image_part(q, away)
            image_part(q, nx - away)

    image_part(0, nx // 2)
    x_stage(0, 0)
    text_parts(nz // 2 - 1)
    z_stage(1)
    image_parts(0, nx // 2 - 1)
    x_stage(0, 1)
    x_spread_done()
    y_spread()
    z_stage(2)
    x_stage(0, 2)
    image_part(0, 0)
    image_part(1, nx // 2)
    x_stage(1, 0)
    text_parts(nz // 2 - 2)
    z_stage(3)
    image_parts(1, nx // 2 - 1)
    x_stage(1, 1)
    for c in both:
        yout[c] = x_total(0, c).astype(bf16)
        start(yout.at[c], yin.at[c], yrs_s.at[c], yrs_r.at[c], facing)
    z_stage(4)
    x_stage(1, 2)
    y_spread_done()
    mate_spread()
    text_parts(nz // 2 - 3)
    z_stage(5)
    z_stage(6)
    image_part(1, 0)
    text_part(0)
    mate_spread_done()
    for row in range(KS):
        for t in range(TILES):
            kg_ref[row, :, t * LANES : (t + 1) * LANES] = fin[
                pl.ds(row * KS * TILES + t, KS, stride=TILES), :
            ]
    for t in range(TILES):
        cg_ref[:, t * LANES : (t + 1) * LANES] = fin[pl.ds(SPOTS * TILES + t, 3, stride=TILES), :]
    for c in both:
        value = x_total(1, c)
        arrived(yin.at[c], yrs_s.at[c], yrs_r.at[c])
        finish(value + yin[c].astype(f32), ta[slot(z, c), :], ui, vi, ig_ref, c)
    for c in both:
        finish(z_total(c), ia[slot(b, c), :], ut, vt, tg_ref, c)
    for moving in sent:
        moving.wait_send()


def loss_block(geo, scale, image_rows, text_rows, terms):
    f32, bf16 = jnp.float32, jnp.bfloat16
    vmem = pltpu.VMEM
    dma = pltpu.SemaphoreType.DMA
    images, texts, width = geo.sheet * ROWS, geo.z * ROWS, geo.width
    kz, kx = geo.z - 1, geo.x - 1
    scratch = [
        vmem((images, width), bf16), vmem((texts, width), bf16),
        vmem((ROWS, width), f32), vmem((ROWS, width), f32), vmem((ROWS, 1), f32), vmem((ROWS, 1), f32),
        vmem((images, texts), f32), vmem((images, texts), bf16), vmem((ROWS, images), bf16),
        vmem((images, ROWS), f32), vmem((images, ROWS), f32), vmem((images, ROWS), f32), vmem((8, ROWS), f32),
        vmem((geo.sheet, 16, ROWS), f32), vmem((geo.z, 16, ROWS), f32),
        vmem((geo.z, ROWS, width), f32), vmem((2 * geo.x, ROWS, width), f32),
        vmem((2, kz, PART, width), bf16), vmem((2, kz, PART, width), bf16),
        vmem((2, 2, kx, PART, width), bf16), vmem((2, 2, kx, PART, width), bf16),
        vmem((2, PART, width), bf16), vmem((2, PART, width), bf16),
        vmem((geo.half, LANES), f32), vmem((geo.half, LANES), f32),
        vmem((geo.y, geo.y_rows, LANES), f32), vmem((geo.y_rows, LANES), f32),
        vmem((geo.x, geo.x_rows, LANES), f32), vmem((geo.z, geo.x_rows, LANES), f32), vmem((SLACK, LANES), f32),
        dma((2, kz)), dma((2, kz)), dma((2, 2, kx)), dma((2, 2, kx)), dma((2,)), dma((2,)),
        dma((geo.sheet,)), dma((geo.sheet,)), dma((geo.z,)), dma((geo.z,)),
        dma((2, kz)), dma((2, kz)), dma((2, 2, kx)), dma((2, 2, kx)), dma((2,)), dma((2,)),
        dma((1,)), dma((1,)), dma((geo.y,)), dma((geo.y,)), dma((geo.x,)), dma((geo.x,)), dma((geo.z,)), dma((geo.z,)),
        dma((geo.x,)), dma((geo.x,)), dma((geo.y,)), dma((geo.y,)), dma((1,)), dma((1,)),
    ]
    return pl.pallas_call(
        functools.partial(loss_kernel, geo),
        out_shape=(
            jax.ShapeDtypeStruct((ROWS, width), bf16),
            jax.ShapeDtypeStruct((ROWS, width), bf16),
            jax.ShapeDtypeStruct((KS, KS, TILES * LANES), f32),
            jax.ShapeDtypeStruct((3, TILES * LANES), f32),
        ),
        in_specs=[pl.BlockSpec(memory_space=pltpu.SMEM)] + [pl.BlockSpec(memory_space=pltpu.VMEM)] * 3,
        out_specs=[pl.BlockSpec(memory_space=pltpu.VMEM)] * 4,
        scratch_shapes=scratch,
        compiler_params=pltpu.CompilerParams(
            collective_id=0, has_side_effects=True, vmem_limit_bytes=52 << 20
        ),
    )(scale.reshape(1), image_rows, text_rows, terms)


def per_device(
    geo, image_embed, text_embed, logit_scale, block_input, dw_kernel, dw_bias, ln_gain, block_grad
):
    d_input, terms = conv_block(block_input[0], block_grad[0], dw_kernel, dw_bias, ln_gain)
    image_grad, text_grad, kernel_grad, channel_grads = loss_block(
        geo, logit_scale, image_embed[0], text_embed[0], terms
    )
    return (image_grad[None], text_grad[None], d_input[None], kernel_grad, channel_grads)


def solution(mesh, geo=None):
    geo = geo or Geometry(8, 2, 4, 2, 2, 1024)
    placed = (
        P("grp", "blk", None),
        P("grp", "blk", None),
        P(),
        P(("blk", "grp"), None, None, None),
        P(),
        P(),
        P(),
        P(("blk", "grp"), None, None, None),
    )
    return jax.shard_map(
        functools.partial(per_device, geo),
        mesh=mesh,
        in_specs=placed,
        out_specs=(
            P("grp", "blk", None),
            P("grp", "blk", None),
            P(("blk", "grp"), None, None, None),
            P(),
            P(),
        ),
        check_vma=False,
    )
```

```python
import functools
import math

import jax
import jax.numpy as jnp
from jax import lax
from jax.experimental import pallas as pl
from jax.experimental.pallas import tpu as pltpu
from jax.sharding import PartitionSpec as P

GRID = 7
KS = 7
EPS = 1e-06
LANES = 128
TILES = 24
SPOTS = GRID * GRID
HALF = KS // 2


def spot_mean(value, count):
    folded = value[:, 0:8] + value[:, 8:16] + value[:, 16:24]
    folded = jnp.sum(folded, axis=1, keepdims=True)
    return jnp.sum(folded, axis=2, keepdims=True) * (1.0 / count)


def conv_terms(x_ref, g_ref, k_ref, bias_ref, gain_ref, din_ref, terms_ref, xs, gs, ks, cs, ds, bs):
    channels = TILES * LANES

    def spread(src, dst):
        for y in range(GRID):
            for t in range(TILES):
                dst[pl.ds(y * GRID * TILES + t, GRID, stride=TILES), :] = src[
                    y, :, t * LANES : (t + 1) * LANES
                ].astype(jnp.float32)

    spread(x_ref, xs)
    spread(k_ref, ks)
    spread(g_ref, gs)
    bs[0:TILES, :] = bias_ref[...].astype(jnp.float32).reshape(TILES, LANES)
    bs[TILES : 2 * TILES, :] = gain_ref[...].astype(jnp.float32).reshape(TILES, LANES)

    def rows(part, spot):
        return pl.ds(pl.multiple_of(spot * TILES + part * 8, 8), 8)

    def gather(src, part, row):
        return [src[rows(part, row * GRID + x), :] for x in range(GRID)]

    @pl.loop(0, TILES // 8)
    def _(part):
        bias = bs[pl.ds(pl.multiple_of(part * 8, 8), 8), :]
        for y in range(GRID):
            sums = [bias] * GRID
            for a in range(KS):
                if not 0 <= y + a - HALF < GRID:
                    continue
                left = gather(xs, part, y + a - HALF)
                taps = gather(ks, part, a)
                for x in range(GRID):
                    for b in range(KS):
                        if 0 <= x + b - HALF < GRID:
                            sums[x] = sums[x] + left[x + b - HALF] * taps[b]
            for x in range(GRID):
                cs[rows(part, y * GRID + x), :] = sums[x]

    gain = bs[TILES : 2 * TILES, :][None]
    dsum = jnp.zeros((TILES, LANES), jnp.float32)
    nsum = jnp.zeros((TILES, LANES), jnp.float32)
    gsum = jnp.zeros((TILES, LANES), jnp.float32)
    for y in range(GRID):
        span = slice(y * GRID * TILES, (y + 1) * GRID * TILES)
        conv = cs[span, :].reshape(GRID, TILES, LANES)
        grad = gs[span, :].reshape(GRID, TILES, LANES)
        centre = conv - spot_mean(conv, channels)
        d_normed = grad * gain
        inv = lax.rsqrt(spot_mean(centre * centre, channels) + EPS)
        normed = centre * inv
        d_conv = inv * (
            d_normed - spot_mean(d_normed, channels) - normed * spot_mean(d_normed * normed, channels)
        )
        ds[span, :] = d_conv.reshape(GRID * TILES, LANES)
        dsum = dsum + jnp.sum(d_conv, axis=0)
        nsum = nsum + jnp.sum(grad * normed, axis=0)
        gsum = gsum + jnp.sum(grad, axis=0)
    first = SPOTS * TILES
    for index, total in enumerate((dsum, nsum, gsum)):
        terms_ref[first + index * TILES : first + (index + 1) * TILES, :] = total
    first = first + 3 * TILES
    terms_ref[first:SLACK, :] = jnp.zeros((SLACK - first, LANES), jnp.float32)

    @pl.loop(0, TILES // 8)
    def _(part):
        for y in range(GRID):
            sums = [None] * GRID
            for a in range(KS):
                if not 0 <= y - a + HALF < GRID:
                    continue
                left = gather(ds, part, y - a + HALF)
                taps = gather(ks, part, a)
                for x in range(GRID):
                    for b in range(KS):
                        if 0 <= x - b + HALF < GRID:
                            term = left[x - b + HALF] * taps[b]
                            sums[x] = term if sums[x] is None else sums[x] + term
            for x in range(GRID):
                cs[rows(part, y * GRID + x), :] = sums[x]
        for a in range(KS):
            sums = [None] * KS
            for y in range(GRID):
                if not 0 <= y + a - HALF < GRID:
                    continue
                left = gather(ds, part, y)
                right = gather(xs, part, y + a - HALF)
                for b in range(KS):
                    for x in range(GRID):
                        if 0 <= x + b - HALF < GRID:
                            term = left[x] * right[x + b - HALF]
                            sums[b] = term if sums[b] is None else sums[b] + term
            for b in range(KS):
                terms_ref[rows(part, a * KS + b), :] = sums[b]

    for y in range(GRID):
        for t in range(TILES):
            din_ref[y, :, t * LANES : (t + 1) * LANES] = cs[
                pl.ds(y * GRID * TILES + t, GRID, stride=TILES), :
            ].astype(jnp.bfloat16)


ROWS = 128
PART = 64
WIDE = 256
MESH = pl.DeviceIdType.MESH
SLACK = 1280
HIGH_SHIFT = 12.0
LOW_SHIFT = 10.0
LOW_CAP = 30.0
LOW_LIMIT = 55.0


class Geometry:
    def __init__(self, z, y_hi, x, y_lo, core, width):
        self.z, self.y_hi, self.x, self.y_lo, self.core, self.width = z, y_hi, x, y_lo, core, width
        self.sheet = y_hi * x
        self.y = y_hi * y_lo
        self.half = SLACK // core
        self.y_rows = self.half // self.y
        self.x_rows = self.y_rows // x


def dot(left, right, dims=((1,), (0,))):
    return lax.dot_general(left, right, (dims, ((), ())), preferred_element_type=jnp.float32)


def loss_kernel(
    geo, scale_ref, img_hbm, txt_hbm, x_hbm, g_hbm, k_hbm, bias_hbm, gain_hbm,
    ig_ref, tg_ref, cg_ref, din_hbm, kg_hbm,
    din_ref, kg_ref, img_ref, txt_ref, x_ref, g_ref, k_ref, bias_ref, gain_ref, terms_ref, xs, gs, ks, cs, ds, bs, load_sem,
    ia, ta, ui, ut, vi, vt, probs, weights, flip, row_hi, row_lo, alpha, beta, row_all, col_all, gz, gx,
    zout, zin, xout, xin, yout, yin, l1, hsum, l2, qsum, l3, l4, fin,
    zag_s, zag_r, xag_s, xag_r, yag_s, yag_r, row_s, row_r, col_s, col_r,
    zrs_s, zrs_r, xrs_s, xrs_r, yrs_s, yrs_r,
    s1, r1, s2, r2, s3, r3, s4, r4, s5, r5, s6, r6, s7, r7,
):
    f32, bf16 = jnp.float32, jnp.bfloat16
    nz, nx, sheet = geo.z, geo.x, geo.sheet
    blk, grp = lax.axis_index("blk"), lax.axis_index("grp")
    z, b = blk // sheet, lax.rem(blk, sheet)
    yh, x = b // nx, lax.rem(b, nx)
    yl, core = grp // geo.core, lax.rem(grp, geo.core)
    y = yh * geo.y_lo + yl
    hy = 1 - yh

    def place(z_to, yh_to, x_to):
        return {"blk": z_to * sheet + yh_to * nx + x_to, "grp": grp}

    def column(y_to):
        return {
            "blk": z * sheet + (y_to // geo.y_lo) * nx + x,
            "grp": lax.rem(y_to, geo.y_lo) * geo.core + core,
        }

    def turn(value, by, size):
        return lax.rem(value + by + size, size)

    mate = {"blk": blk, "grp": yl * geo.core + (geo.core - 1 - core)}
    facing = place(z, hy, x)
    sent = []

    def copy(src, dst, send, recv, to):
        return pltpu.make_async_remote_copy(
            src_ref=src, dst_ref=dst, send_sem=send, recv_sem=recv, device_id=to, device_id_type=MESH
        )

    def start(*args):
        moving = copy(*args)
        moving.start()
        sent.append(moving)

    def arrived(dst, send, recv):
        copy(dst, dst, send, recv, facing).wait_recv()

    barrier = pltpu.get_barrier_semaphore()
    peers = [place(turn(z, o, nz), yh, x) for o in range(1, nz)]
    for q in range(2):
        for o in range(nx):
            if q or o:
                peers.append(place(z, hy if q else yh, turn(x, o, nx)))
    for o in range(1, geo.y):
        if o != geo.y_lo:
            peers.append(column(turn(y, o, geo.y)))
    peers.append(mate)
    for peer in peers:
        pl.semaphore_signal(barrier, inc=1, device_id=peer, device_id_type=MESH)
    operands = (txt_hbm, img_hbm, x_hbm, k_hbm, g_hbm, bias_hbm, gain_hbm)
    held = (txt_ref, img_ref, x_ref, k_ref, g_ref, bias_ref, gain_ref)
    loads = [
        pltpu.make_async_copy(src, dst, load_sem.at[i]) for i, (src, dst) in enumerate(zip(operands, held))
    ]
    for load in loads:
        load.start()

    def slot(index, part):
        return pl.ds(pl.multiple_of(index * ROWS + part * PART, PART), PART)

    def full(index):
        return pl.ds(pl.multiple_of(index * ROWS, ROWS), ROWS)

    def unit_rows(raw, unit, inverse, everyone, index):
        values = raw[...].astype(f32)
        inv = lax.rsqrt(jnp.sum(values * values, axis=-1, keepdims=True) + EPS)
        scaled = values * inv
        unit[...] = scaled
        inverse[...] = inv
        everyone[full(index), :] = scaled.astype(bf16)

    loads[0].wait()
    unit_rows(txt_ref, ut, vt, ta, z)
    loads[1].wait()
    unit_rows(img_ref, ui, vi, ia, b)
    pl.semaphore_wait(barrier, len(peers))

    def sign(d):
        return 1 - 2 * d

    def z_gather(d, k):
        rows = slot(turn(z, -sign(d) * (k // 2), nz), (k % 2) ^ d)
        to = place(turn(z, sign(d), nz), yh, x)
        start(ta.at[rows], ta.at[rows], zag_s.at[d, k], zag_r.at[d, k], to)

    def z_gathered(d, k):
        rows = slot(turn(z, -sign(d) * (k // 2 + 1), nz), (k % 2) ^ d)
        arrived(ta.at[rows], zag_s.at[d, k], zag_r.at[d, k])

    def x_gather(q, d, k):
        rows = slot((hy if q else yh) * nx + turn(x, -sign(d) * (k // 2), nx), (k % 2) ^ d)
        to = place(z, yh, turn(x, sign(d), nx))
        start(ia.at[rows], ia.at[rows], xag_s.at[q, d, k], xag_r.at[q, d, k], to)

    def x_gathered(q, d, k):
        rows = slot((hy if q else yh) * nx + turn(x, -sign(d) * (k // 2 + 1), nx), (k % 2) ^ d)
        arrived(ia.at[rows], xag_s.at[q, d, k], xag_r.at[q, d, k])

    def y_gather(c):
        start(ia.at[slot(b, c)], ia.at[slot(b, c)], yag_s.at[c], yag_r.at[c], facing)

    def y_gathered(c):
        arrived(ia.at[slot(hy * nx + x, c)], yag_s.at[c], yag_r.at[c])

    def share(first, rows):
        return pl.ds(pl.multiple_of(first, 8), rows)

    def mate_send():
        start(terms_ref.at[share((geo.core - 1 - core) * geo.half, geo.half)], l1, s1.at[0], r1.at[0], mate)

    def mate_sum():
        arrived(l1, s1.at[0], r1.at[0])
        hsum[...] = terms_ref[share(core * geo.half, geo.half), :] + l1[...]

    def y_send():
        for o in range(1, geo.y):
            to = turn(y, o, geo.y)
            start(hsum.at[share(to * geo.y_rows, geo.y_rows)], l2.at[o], s2.at[o], r2.at[o], column(to))

    def y_sum():
        total = hsum[share(y * geo.y_rows, geo.y_rows), :]
        for o in range(1, geo.y):
            arrived(l2.at[o], s2.at[o], r2.at[o])
            total = total + l2[o]
        qsum[...] = total

    def x_send():
        for o in range(1, nx):
            to = turn(x, o, nx)
            start(qsum.at[share(to * geo.x_rows, geo.x_rows)], l3.at[o], s3.at[o], r3.at[o], place(z, yh, to))

    def x_sum():
        total = qsum[share(x * geo.x_rows, geo.x_rows), :]
        for o in range(1, nx):
            arrived(l3.at[o], s3.at[o], r3.at[o])
            total = total + l3[o]
        l4[z] = total

    def z_send():
        for o in range(1, nz):
            start(l4.at[z], l4.at[z], s4.at[o], r4.at[o], place(turn(z, o, nz), yh, x))

    mine = core * geo.half + y * geo.y_rows + x * geo.x_rows

    def z_sum():
        for o in range(1, nz):
            arrived(l4.at[turn(z, -o, nz)], s4.at[o], r4.at[o])
        total = l4[0]
        for o in range(1, nz):
            total = total + l4[o]
        fin[share(mine, geo.x_rows), :] = total * (1.0 / (geo.z * geo.sheet * geo.y_lo * geo.core))

    def x_spread():
        rows = fin.at[share(mine, geo.x_rows)]
        for o in range(1, nx):
            start(rows, rows, s5.at[o], r5.at[o], place(z, yh, turn(x, o, nx)))

    def x_spread_done():
        for o in range(1, nx):
            first = core * geo.half + y * geo.y_rows + turn(x, -o, nx) * geo.x_rows
            arrived(fin.at[share(first, geo.x_rows)], s5.at[o], r5.at[o])

    def y_spread():
        rows = fin.at[share(core * geo.half + y * geo.y_rows, geo.y_rows)]
        for o in range(1, geo.y):
            start(rows, rows, s6.at[o], r6.at[o], column(turn(y, o, geo.y)))

    def y_spread_done():
        for o in range(1, geo.y):
            first = core * geo.half + turn(y, -o, geo.y) * geo.y_rows
            arrived(fin.at[share(first, geo.y_rows)], s6.at[o], r6.at[o])

    def mate_spread():
        rows = fin.at[share(core * geo.half, geo.half)]
        start(rows, rows, s7.at[0], r7.at[0], mate)

    def mate_spread_done():
        arrived(fin.at[share((geo.core - 1 - core) * geo.half, geo.half)], s7.at[0], r7.at[0])

    half_scale = scale_ref[0] * 0.5
    row_hi[...] = jnp.zeros_like(row_hi)
    row_lo[...] = jnp.zeros_like(row_lo)
    blocks = nz * ROWS // WIDE
    late = turn(z, nz // 2, nz) // (WIDE // ROWS)

    def logits_block(n):
        lanes = pl.ds(pl.multiple_of(n * WIDE, WIDE), WIDE)

        def rows_step(m, sums):
            rows = pl.ds(pl.multiple_of(m * WIDE, WIDE), WIDE)
            logits = dot(ia[rows, :], ta[lanes, :], ((1,), (1,)))
            root = jnp.exp(logits * half_scale)
            probs[rows, lanes] = root
            high = root * math.exp(-HIGH_SHIFT)
            high = high * high
            low = jnp.minimum(root * math.exp(LOW_SHIFT), math.exp(LOW_CAP))
            low = low * low
            row_hi[rows, :] += high[:, :ROWS] + high[:, ROWS:]
            row_lo[rows, :] += low[:, :ROWS] + low[:, ROWS:]
            return (
                sums[0] + jnp.sum(high.reshape(WIDE // 8, 8, WIDE), axis=0),
                sums[1] + jnp.sum(low.reshape(WIDE // 8, 8, WIDE), axis=0),
            )

        zero = jnp.zeros((8, WIDE), f32)
        high, low = lax.fori_loop(0, sheet * ROWS // WIDE, rows_step, (zero, zero))
        high = jnp.sum(high, axis=0, keepdims=True)
        low = jnp.sum(low, axis=0, keepdims=True)
        for j in range(WIDE // ROWS):
            at = n * (WIDE // ROWS) + j
            col_all[z, pl.ds(at, 1), :] = high[:, j * ROWS : (j + 1) * ROWS]
            col_all[z, pl.ds(8 + at, 1), :] = low[:, j * ROWS : (j + 1) * ROWS]

    def half_factor(total):
        high, low = total[0:8], total[8:16]
        small = low < math.exp(LOW_LIMIT)
        lse = jnp.where(small, jnp.log(low) - 2 * LOW_SHIFT, jnp.log(high) + 2 * HIGH_SHIFT)
        return jnp.exp(lse * -0.5) * math.sqrt(0.5)

    def weigh(tile):
        lanes = pl.ds(pl.multiple_of(tile * ROWS, ROWS), ROWS)

        def rows_step(m, carry):
            rows = pl.ds(pl.multiple_of(m * WIDE, WIDE), WIDE)
            root = probs[rows, lanes]
            by_row = root * alpha[rows, :]
            by_col = root * beta[pl.ds(tile, 1), :]
            weights[rows, lanes] = (by_row * by_row + by_col * by_col).astype(bf16)
            return carry

        lax.fori_loop(0, sheet * ROWS // WIDE, rows_step, 0)

    def text_part(j):
        flip[...] = weights[:, full(turn(z, j, nz))].T

        @pl.loop(0, geo.width // WIDE)
        def _(n):
            lanes = pl.ds(pl.multiple_of(n * WIDE, WIDE), WIDE)
            gz[j, :, lanes] = dot(flip[...], ia[:, lanes])

    def image_part(q, j):
        rows = full((yh if q else hy) * nx + turn(x, j, nx))

        @pl.loop(0, geo.width // WIDE)
        def _(n):
            lanes = pl.ds(pl.multiple_of(n * WIDE, WIDE), WIDE)
            gx[q * nx + j, :, lanes] = dot(weights[rows, :], ta[:, lanes])

    def ring_rows(d, k):
        part = (k % 2) ^ d
        return slice(part * PART, (part + 1) * PART)

    def ring_target(d, k, size):
        away = size // 2 - (k + 1) // 2
        return (sign(d) * away) % size

    def z_reduce(d, k):
        value = gz[ring_target(d, k, nz), ring_rows(d, k), :]
        if k >= 2:
            arrived(zin.at[d, k - 2], zrs_s.at[d, k - 2], zrs_r.at[d, k - 2])
            value = value + zin[d, k - 2].astype(f32)
        zout[d, k] = value.astype(bf16)
        to = place(turn(z, sign(d), nz), yh, x)
        start(zout.at[d, k], zin.at[d, k], zrs_s.at[d, k], zrs_r.at[d, k], to)

    def x_reduce(q, d, k):
        value = gx[q * nx + ring_target(d, k, nx), ring_rows(d, k), :]
        if k >= 2:
            arrived(xin.at[q, d, k - 2], xrs_s.at[q, d, k - 2], xrs_r.at[q, d, k - 2])
            value = value + xin[q, d, k - 2].astype(f32)
        xout[q, d, k] = value.astype(bf16)
        to = place(z, yh, turn(x, sign(d), nx))
        start(xout.at[q, d, k], xin.at[q, d, k], xrs_s.at[q, d, k], xrs_r.at[q, d, k], to)

    def ring_last(size):
        return [k for k in (size - 3, size - 2) if k >= 0]

    def x_total(q, c):
        value = gx[q * nx, c * PART : (c + 1) * PART, :]
        for d in range(2):
            for k in ring_last(nx):
                if (k % 2) ^ d == c:
                    arrived(xin.at[q, d, k], xrs_s.at[q, d, k], xrs_r.at[q, d, k])
                    value = value + xin[q, d, k].astype(f32)
        return value

    def z_total(c):
        value = gz[0, c * PART : (c + 1) * PART, :]
        for d in range(2):
            for k in ring_last(nz):
                if (k % 2) ^ d == c:
                    arrived(zin.at[d, k], zrs_s.at[d, k], zrs_r.at[d, k])
                    value = value + zin[d, k].astype(f32)
        return value

    def finish(total, other, unit, inverse, out, c):
        rows = slice(c * PART, (c + 1) * PART)
        grad = scale_ref[0] * (total - other.astype(f32))
        along = jnp.sum(grad * unit[rows, :], axis=-1, keepdims=True)
        out[rows, :] = (inverse[rows, :] * (grad - along * unit[rows, :])).astype(bf16)

    both = range(2)
    kz, kx = nz - 1, nx - 1
    for k in range(min(2, kz)):
        for d in both:
            z_gather(d, k)
    for k in range(min(2, kx)):
        for d in both:
            x_gather(0, d, k)
    for c in both:
        y_gather(c)
    for load in loads[2:]:
        load.wait()
    conv_terms(x_ref, g_ref, k_ref, bias_ref, gain_ref, din_ref, terms_ref, xs, gs, ks, cs, ds, bs)
    din_out = pltpu.make_async_copy(din_ref, din_hbm, load_sem.at[len(loads)])
    din_out.start()
    mate_send()

    def z_step(k):
        if k < kz:
            for d in both:
                z_gathered(d, k)
            if k + 2 < kz:
                for d in both:
                    z_gather(d, k + 2)

    def x_step(q, k):
        if k < kx:
            for d in both:
                x_gathered(q, d, k)
            if k + 2 < kx:
                for d in both:
                    x_gather(q, d, k + 2)

    z_step(0)
    x_step(0, 0)
    z_step(1)
    for c in both:
        y_gathered(c)
        for k in range(min(2, kx)):
            for d in both:
                if (k % 2) ^ d == c:
                    x_gather(1, d, k)
    mate_sum()
    y_send()
    x_step(0, 1)
    z_step(2)
    x_step(0, 2)
    y_sum()
    x_send()
    z_step(3)
    x_step(1, 0)
    z_step(4)
    x_sum()
    for k in range(1, kx):
        x_step(1, k)
    for k in range(5, kz - 1):
        z_step(k)

    @pl.loop(0, blocks - 1)
    def _(i):
        logits_block(lax.rem(late + 1 + i, blocks))

    if kz - 1 >= 5:
        z_step(kz - 1)
    z_send()
    logits_block(late)
    for m in range(sheet):
        rows = slice(m * ROWS, (m + 1) * ROWS)
        row_all[b, m : m + 1, :] = jnp.sum(row_hi[rows, :].T, axis=0, keepdims=True)
        row_all[b, 8 + m : 9 + m, :] = jnp.sum(row_lo[rows, :].T, axis=0, keepdims=True)
    for o in range(1, nz):
        start(col_all.at[z], col_all.at[z], col_s.at[o], col_r.at[o], place(turn(z, o, nz), yh, x))
    for q in both:
        for o in range(nx):
            if q or o:
                i = q * nx + o
                to = place(z, hy if q else yh, turn(x, o, nx))
                start(row_all.at[b], row_all.at[b], row_s.at[i], row_r.at[i], to)
    z_sum()
    x_spread()
    for o in range(1, nz):
        arrived(col_all.at[turn(z, -o, nz)], col_s.at[o], col_r.at[o])
    total = col_all[0]
    for o in range(1, nz):
        total = total + col_all[o]
    beta[...] = half_factor(total)
    for q in both:
        for o in range(nx):
            if q or o:
                i = q * nx + o
                arrived(row_all.at[(hy if q else yh) * nx + turn(x, -o, nx)], row_s.at[i], row_r.at[i])
    total = row_all[0]
    for o in range(1, sheet):
        total = total + row_all[o]
    factor = half_factor(total)
    for m in range(sheet):
        rows = slice(m * ROWS, (m + 1) * ROWS)
        alpha[rows, :] = jnp.broadcast_to(factor[m : m + 1, :], (ROWS, ROWS)).T

    def z_stage(k):
        if k < kz:
            for d in both:
                z_reduce(d, k)

    def x_stage(q, k):
        if k < kx:
            for d in both:
                x_reduce(q, d, k)

    def text_parts(away):
        if 0 < away < nz // 2:
            text_part(away)
            text_part(nz - away)

    def image_parts(q, away):
        if 0 < away < nx // 2:
            image_part(q, away)
            image_part(q, nx - away)

    half = nz // 2
    weigh(turn(z, half, nz))
    text_part(half)
    z_stage(0)
    if half > 1:
        weigh(turn(z, half - 1, nz))
        weigh(turn(z, -(half - 1), nz))
    text_parts(half - 1)
    z_stage(1)
    first = max(half - 1, 1)

    @pl.loop(0, 2 * first - 1)
    def _(i):
        weigh(turn(z, i - (first - 1), nz))

    image_part(0, nx // 2)
    x_stage(0, 0)
    image_parts(0, nx // 2 - 1)
    x_stage(0, 1)
    x_spread_done()
    y_spread()
    image_part(1, nx // 2)
    z_stage(2)
    image_parts(1, nx // 2 - 1)
    x_stage(0, 2)
    x_stage(1, 0)
    x_stage(1, 1)
    text_parts(half - 2)
    z_stage(3)
    image_part(0, 0)
    z_stage(4)
    for c in both:
        yout[c] = x_total(0, c).astype(bf16)
        start(yout.at[c], yin.at[c], yrs_s.at[c], yrs_r.at[c], facing)
    text_parts(half - 3)
    z_stage(5)
    x_stage(1, 2)
    y_spread_done()
    mate_spread()
    z_stage(6)
    image_part(1, 0)
    text_part(0)
    mate_spread_done()
    for row in range(KS):
        for t in range(TILES):
            kg_ref[row, :, t * LANES : (t + 1) * LANES] = fin[
                pl.ds(row * KS * TILES + t, KS, stride=TILES), :
            ]
    for t in range(TILES):
        cg_ref[:, t * LANES : (t + 1) * LANES] = fin[pl.ds(SPOTS * TILES + t, 3, stride=TILES), :]
    kg_out = pltpu.make_async_copy(kg_ref, kg_hbm, load_sem.at[len(loads) + 1])
    kg_out.start()
    for c in both:
        value = x_total(1, c)
        arrived(yin.at[c], yrs_s.at[c], yrs_r.at[c])
        finish(value + yin[c].astype(f32), ta[slot(z, c), :], ui, vi, ig_ref, c)
    for c in both:
        finish(z_total(c), ia[slot(b, c), :], ut, vt, tg_ref, c)
    din_out.wait()
    kg_out.wait()
    for moving in sent:
        moving.wait_send()


def loss_block(geo, scale, image_rows, text_rows, x, g, k, bias, gain):
    f32, bf16 = jnp.float32, jnp.bfloat16
    vmem = pltpu.VMEM
    dma = pltpu.SemaphoreType.DMA
    images, texts, width = geo.sheet * ROWS, geo.z * ROWS, geo.width
    kz, kx = geo.z - 1, geo.x - 1
    big = vmem((SPOTS * TILES, LANES), f32)
    maps = vmem((GRID, GRID, TILES * LANES), bf16)
    scratch = [
        maps, vmem((KS, KS, TILES * LANES), f32), vmem((ROWS, width), bf16), vmem((ROWS, width), bf16), maps, maps, maps,
        vmem((TILES * LANES,), bf16), vmem((TILES * LANES,), bf16), vmem((SLACK, LANES), f32),
        big, big, big, big, big, vmem((2 * TILES, LANES), f32), dma((9,)),
        vmem((images, width), bf16), vmem((texts, width), bf16),
        vmem((ROWS, width), f32), vmem((ROWS, width), f32), vmem((ROWS, 1), f32), vmem((ROWS, 1), f32),
        vmem((images, texts), f32), vmem((images, texts), bf16), vmem((ROWS, images), bf16),
        vmem((images, ROWS), f32), vmem((images, ROWS), f32), vmem((images, ROWS), f32), vmem((8, ROWS), f32),
        vmem((geo.sheet, 16, ROWS), f32), vmem((geo.z, 16, ROWS), f32),
        vmem((geo.z, ROWS, width), f32), vmem((2 * geo.x, ROWS, width), f32),
        vmem((2, kz, PART, width), bf16), vmem((2, kz, PART, width), bf16),
        vmem((2, 2, kx, PART, width), bf16), vmem((2, 2, kx, PART, width), bf16),
        vmem((2, PART, width), bf16), vmem((2, PART, width), bf16),
        vmem((geo.half, LANES), f32), vmem((geo.half, LANES), f32),
        vmem((geo.y, geo.y_rows, LANES), f32), vmem((geo.y_rows, LANES), f32),
        vmem((geo.x, geo.x_rows, LANES), f32), vmem((geo.z, geo.x_rows, LANES), f32), vmem((SLACK, LANES), f32),
        dma((2, kz)), dma((2, kz)), dma((2, 2, kx)), dma((2, 2, kx)), dma((2,)), dma((2,)),
        dma((geo.sheet,)), dma((geo.sheet,)), dma((geo.z,)), dma((geo.z,)),
        dma((2, kz)), dma((2, kz)), dma((2, 2, kx)), dma((2, 2, kx)), dma((2,)), dma((2,)),
        dma((1,)), dma((1,)), dma((geo.y,)), dma((geo.y,)), dma((geo.x,)), dma((geo.x,)), dma((geo.z,)), dma((geo.z,)),
        dma((geo.x,)), dma((geo.x,)), dma((geo.y,)), dma((geo.y,)), dma((1,)), dma((1,)),
    ]
    return pl.pallas_call(
        functools.partial(loss_kernel, geo),
        out_shape=(
            jax.ShapeDtypeStruct((ROWS, width), bf16),
            jax.ShapeDtypeStruct((ROWS, width), bf16),
            jax.ShapeDtypeStruct((3, TILES * LANES), f32),
            jax.ShapeDtypeStruct((GRID, GRID, TILES * LANES), bf16),
            jax.ShapeDtypeStruct((KS, KS, TILES * LANES), f32),
        ),
        in_specs=[pl.BlockSpec(memory_space=pltpu.SMEM)] + [pl.BlockSpec(memory_space=pltpu.HBM)] * 7,
        out_specs=[pl.BlockSpec(memory_space=pltpu.VMEM)] * 3 + [pl.BlockSpec(memory_space=pltpu.HBM)] * 2,
        scratch_shapes=scratch,
        compiler_params=pltpu.CompilerParams(
            collective_id=0, has_side_effects=True, vmem_limit_bytes=60 << 20
        ),
    )(scale.reshape(1), image_rows, text_rows, x, g, k, bias, gain)


def hand_out_kernel(*refs):
    count = len(refs) // 2
    sems = refs[-1]
    copies = [pltpu.make_async_copy(refs[i], refs[count + i], sems.at[i]) for i in range(count)]
    for moving in copies:
        moving.start()
    for moving in copies:
        moving.wait()


def hand_out(*arrays):
    anywhere = [pl.BlockSpec(memory_space=pl.ANY)] * 3 + [pl.BlockSpec(memory_space=pltpu.HBM)] * 2
    return pl.pallas_call(
        hand_out_kernel,
        out_shape=tuple(jax.ShapeDtypeStruct(a.shape, a.dtype) for a in arrays),
        in_specs=anywhere,
        out_specs=anywhere,
        scratch_shapes=[pltpu.SemaphoreType.DMA((len(arrays),))],
        compiler_params=pltpu.CompilerParams(vmem_limit_bytes=60 << 20),
    )(*arrays)


def per_device(
    geo, image_embed, text_embed, logit_scale, block_input, dw_kernel, dw_bias, ln_gain, block_grad
):
    image_grad, text_grad, channel_grads, d_input, kernel_grad = hand_out(
        *loss_block(
            geo, logit_scale, image_embed[0], text_embed[0],
            block_input[0], block_grad[0], dw_kernel, dw_bias, ln_gain,
        )
    )
    return (image_grad[None], text_grad[None], d_input[None], kernel_grad, channel_grads)


def solution(mesh, geo=None):
    geo = geo or Geometry(8, 2, 4, 2, 2, 1024)
    placed = (
        P("grp", "blk", None),
        P("grp", "blk", None),
        P(),
        P(("blk", "grp"), None, None, None),
        P(),
        P(),
        P(),
        P(("blk", "grp"), None, None, None),
    )
    return jax.shard_map(
        functools.partial(per_device, geo),
        mesh=mesh,
        in_specs=placed,
        out_specs=(
            P("grp", "blk", None),
            P("grp", "blk", None),
            P(("blk", "grp"), None, None, None),
            P(),
            P(),
        ),
        check_vma=False,
    )
```

```python
import functools
import math

import jax
import jax.numpy as jnp
from jax import lax
from jax.experimental import pallas as pl
from jax.experimental.pallas import tpu as pltpu
from jax.sharding import PartitionSpec as P

GRID = 7
KS = 7
EPS = 1e-06
LANES = 128
TILES = 24
SPOTS = GRID * GRID
HALF = KS // 2


def spot_mean(value, count):
    folded = value[:, 0:8] + value[:, 8:16] + value[:, 16:24]
    folded = jnp.sum(folded, axis=1, keepdims=True)
    return jnp.sum(folded, axis=2, keepdims=True) * (1.0 / count)


def conv_terms(x_ref, g_ref, k_ref, bias_ref, gain_ref, din_ref, terms_ref, xs, gs, ks, cs, ds, bs):
    channels = TILES * LANES

    def spread(src, dst):
        for y in range(GRID):
            for t in range(TILES):
                dst[pl.ds(y * GRID * TILES + t, GRID, stride=TILES), :] = src[
                    y, :, t * LANES : (t + 1) * LANES
                ].astype(jnp.float32)

    spread(x_ref, xs)
    spread(k_ref, ks)
    spread(g_ref, gs)
    bs[0:TILES, :] = bias_ref[...].astype(jnp.float32).reshape(TILES, LANES)
    bs[TILES : 2 * TILES, :] = gain_ref[...].astype(jnp.float32).reshape(TILES, LANES)

    def rows(part, spot):
        return pl.ds(pl.multiple_of(spot * TILES + part * 8, 8), 8)

    def gather(src, part, row):
        return [src[rows(part, row * GRID + x), :] for x in range(GRID)]

    @pl.loop(0, TILES // 8)
    def _(part):
        bias = bs[pl.ds(pl.multiple_of(part * 8, 8), 8), :]
        for y in range(GRID):
            sums = [bias] * GRID
            for a in range(KS):
                if not 0 <= y + a - HALF < GRID:
                    continue
                left = gather(xs, part, y + a - HALF)
                taps = gather(ks, part, a)
                for x in range(GRID):
                    for b in range(KS):
                        if 0 <= x + b - HALF < GRID:
                            sums[x] = sums[x] + left[x + b - HALF] * taps[b]
            for x in range(GRID):
                cs[rows(part, y * GRID + x), :] = sums[x]

    gain = bs[TILES : 2 * TILES, :][None]
    dsum = jnp.zeros((TILES, LANES), jnp.float32)
    nsum = jnp.zeros((TILES, LANES), jnp.float32)
    gsum = jnp.zeros((TILES, LANES), jnp.float32)
    for y in range(GRID):
        span = slice(y * GRID * TILES, (y + 1) * GRID * TILES)
        conv = cs[span, :].reshape(GRID, TILES, LANES)
        grad = gs[span, :].reshape(GRID, TILES, LANES)
        centre = conv - spot_mean(conv, channels)
        d_normed = grad * gain
        inv = lax.rsqrt(spot_mean(centre * centre, channels) + EPS)
        normed = centre * inv
        d_conv = inv * (
            d_normed - spot_mean(d_normed, channels) - normed * spot_mean(d_normed * normed, channels)
        )
        ds[span, :] = d_conv.reshape(GRID * TILES, LANES)
        dsum = dsum + jnp.sum(d_conv, axis=0)
        nsum = nsum + jnp.sum(grad * normed, axis=0)
        gsum = gsum + jnp.sum(grad, axis=0)
    first = SPOTS * TILES
    for index, total in enumerate((dsum, nsum, gsum)):
        terms_ref[first + index * TILES : first + (index + 1) * TILES, :] = total
    first = first + 3 * TILES
    terms_ref[first:SLACK, :] = jnp.zeros((SLACK - first, LANES), jnp.float32)

    @pl.loop(0, TILES // 8)
    def _(part):
        for y in range(GRID):
            sums = [None] * GRID
            for a in range(KS):
                if not 0 <= y - a + HALF < GRID:
                    continue
                left = gather(ds, part, y - a + HALF)
                taps = gather(ks, part, a)
                for x in range(GRID):
                    for b in range(KS):
                        if 0 <= x - b + HALF < GRID:
                            term = left[x - b + HALF] * taps[b]
                            sums[x] = term if sums[x] is None else sums[x] + term
            for x in range(GRID):
                cs[rows(part, y * GRID + x), :] = sums[x]
        for a in range(KS):
            sums = [None] * KS
            for y in range(GRID):
                if not 0 <= y + a - HALF < GRID:
                    continue
                left = gather(ds, part, y)
                right = gather(xs, part, y + a - HALF)
                for b in range(KS):
                    for x in range(GRID):
                        if 0 <= x + b - HALF < GRID:
                            term = left[x] * right[x + b - HALF]
                            sums[b] = term if sums[b] is None else sums[b] + term
            for b in range(KS):
                terms_ref[rows(part, a * KS + b), :] = sums[b]

    for y in range(GRID):
        for t in range(TILES):
            din_ref[y, :, t * LANES : (t + 1) * LANES] = cs[
                pl.ds(y * GRID * TILES + t, GRID, stride=TILES), :
            ].astype(jnp.bfloat16)


ROWS = 128
PART = 64
WIDE = 256
MESH = pl.DeviceIdType.MESH
SLACK = 1280
HIGH_SHIFT = 12.0
LOW_SHIFT = 10.0
LOW_CAP = 30.0
LOW_LIMIT = 55.0


class Geometry:
    def __init__(self, z, y_hi, x, y_lo, core, width):
        self.z, self.y_hi, self.x, self.y_lo, self.core, self.width = z, y_hi, x, y_lo, core, width
        self.sheet = y_hi * x
        self.y = y_hi * y_lo
        self.half = SLACK // core
        self.y_rows = self.half // self.y
        self.x_rows = self.y_rows // x


def dot(left, right, dims=((1,), (0,))):
    return lax.dot_general(left, right, (dims, ((), ())), preferred_element_type=jnp.float32)


def loss_kernel(
    geo, scale_ref, img_hbm, txt_hbm, x_hbm, g_hbm, k_hbm, bias_hbm, gain_hbm,
    ig_ref, tg_ref, cg_ref, din_hbm, kg_hbm,
    din_ref, kg_ref, img_ref, txt_ref, x_ref, g_ref, k_ref, bias_ref, gain_ref, terms_ref, xs, gs, ks, cs, ds, bs, load_sem,
    ia, ta, ui, ut, vi, vt, probs, weights, flip, row_hi, row_lo, alpha, beta, row_all, col_all, gz, gx,
    zout, zin, xout, xin, yout, yin, l1, hsum, l2, qsum, l3, l4, fin,
    zag_s, zag_r, xag_s, xag_r, yag_s, yag_r, row_s, row_r, col_s, col_r,
    zrs_s, zrs_r, xrs_s, xrs_r, yrs_s, yrs_r,
    s1, r1, s2, r2, s3, r3, s4, r4, s5, r5, s6, r6, s7, r7,
):
    f32, bf16 = jnp.float32, jnp.bfloat16
    nz, nx, sheet = geo.z, geo.x, geo.sheet
    blk, grp = lax.axis_index("blk"), lax.axis_index("grp")
    z, b = blk // sheet, lax.rem(blk, sheet)
    yh, x = b // nx, lax.rem(b, nx)
    yl, core = grp // geo.core, lax.rem(grp, geo.core)
    y = yh * geo.y_lo + yl
    hy = 1 - yh

    def place(z_to, yh_to, x_to):
        return {"blk": z_to * sheet + yh_to * nx + x_to, "grp": grp}

    def column(y_to):
        return {
            "blk": z * sheet + (y_to // geo.y_lo) * nx + x,
            "grp": lax.rem(y_to, geo.y_lo) * geo.core + core,
        }

    def turn(value, by, size):
        return lax.rem(value + by + size, size)

    mate = {"blk": blk, "grp": yl * geo.core + (geo.core - 1 - core)}
    facing = place(z, hy, x)
    sent = []

    def copy(src, dst, send, recv, to):
        return pltpu.make_async_remote_copy(
            src_ref=src, dst_ref=dst, send_sem=send, recv_sem=recv, device_id=to, device_id_type=MESH
        )

    def start(*args):
        moving = copy(*args)
        moving.start()
        sent.append(moving)

    def arrived(dst, send, recv):
        copy(dst, dst, send, recv, facing).wait_recv()

    barrier = pltpu.get_barrier_semaphore()
    peers = [place(turn(z, o, nz), yh, x) for o in range(1, nz)]
    for q in range(2):
        for o in range(nx):
            if q or o:
                peers.append(place(z, hy if q else yh, turn(x, o, nx)))
    for o in range(1, geo.y):
        if o != geo.y_lo:
            peers.append(column(turn(y, o, geo.y)))
    peers.append(mate)
    for peer in peers:
        pl.semaphore_signal(barrier, inc=1, device_id=peer, device_id_type=MESH)
    operands = (txt_hbm, img_hbm, x_hbm, k_hbm, g_hbm, bias_hbm, gain_hbm)
    held = (txt_ref, img_ref, x_ref, k_ref, g_ref, bias_ref, gain_ref)
    loads = [
        pltpu.make_async_copy(src, dst, load_sem.at[i]) for i, (src, dst) in enumerate(zip(operands, held))
    ]
    for load in loads:
        load.start()

    def slot(index, part):
        return pl.ds(pl.multiple_of(index * ROWS + part * PART, PART), PART)

    def full(index):
        return pl.ds(pl.multiple_of(index * ROWS, ROWS), ROWS)

    def unit_rows(raw, unit, inverse, everyone, index):
        values = raw[...].astype(f32)
        inv = lax.rsqrt(jnp.sum(values * values, axis=-1, keepdims=True) + EPS)
        scaled = values * inv
        unit[...] = scaled
        inverse[...] = inv
        everyone[full(index), :] = scaled.astype(bf16)

    loads[0].wait()
    unit_rows(txt_ref, ut, vt, ta, z)
    loads[1].wait()
    unit_rows(img_ref, ui, vi, ia, b)
    pl.semaphore_wait(barrier, len(peers))

    def sign(d):
        return 1 - 2 * d

    def z_gather(d, k):
        rows = slot(turn(z, -sign(d) * (k // 2), nz), (k % 2) ^ d)
        to = place(turn(z, sign(d), nz), yh, x)
        start(ta.at[rows], ta.at[rows], zag_s.at[d, k], zag_r.at[d, k], to)

    def z_gathered(d, k):
        rows = slot(turn(z, -sign(d) * (k // 2 + 1), nz), (k % 2) ^ d)
        arrived(ta.at[rows], zag_s.at[d, k], zag_r.at[d, k])

    def x_gather(q, d, k):
        rows = slot((hy if q else yh) * nx + turn(x, -sign(d) * (k // 2), nx), (k % 2) ^ d)
        to = place(z, yh, turn(x, sign(d), nx))
        start(ia.at[rows], ia.at[rows], xag_s.at[q, d, k], xag_r.at[q, d, k], to)

    def x_gathered(q, d, k):
        rows = slot((hy if q else yh) * nx + turn(x, -sign(d) * (k // 2 + 1), nx), (k % 2) ^ d)
        arrived(ia.at[rows], xag_s.at[q, d, k], xag_r.at[q, d, k])

    def y_gather(c):
        start(ia.at[slot(b, c)], ia.at[slot(b, c)], yag_s.at[c], yag_r.at[c], facing)

    def y_gathered(c):
        arrived(ia.at[slot(hy * nx + x, c)], yag_s.at[c], yag_r.at[c])

    def share(first, rows):
        return pl.ds(pl.multiple_of(first, 8), rows)

    def mate_send():
        start(terms_ref.at[share((geo.core - 1 - core) * geo.half, geo.half)], l1, s1.at[0], r1.at[0], mate)

    def mate_sum():
        arrived(l1, s1.at[0], r1.at[0])
        hsum[...] = terms_ref[share(core * geo.half, geo.half), :] + l1[...]

    def y_send():
        for o in range(1, geo.y):
            to = turn(y, o, geo.y)
            start(hsum.at[share(to * geo.y_rows, geo.y_rows)], l2.at[o], s2.at[o], r2.at[o], column(to))

    def y_sum():
        total = hsum[share(y * geo.y_rows, geo.y_rows), :]
        for o in range(1, geo.y):
            arrived(l2.at[o], s2.at[o], r2.at[o])
            total = total + l2[o]
        qsum[...] = total

    def x_send():
        for o in range(1, nx):
            to = turn(x, o, nx)
            start(qsum.at[share(to * geo.x_rows, geo.x_rows)], l3.at[o], s3.at[o], r3.at[o], place(z, yh, to))

    def x_sum():
        total = qsum[share(x * geo.x_rows, geo.x_rows), :]
        for o in range(1, nx):
            arrived(l3.at[o], s3.at[o], r3.at[o])
            total = total + l3[o]
        l4[z] = total

    def z_send():
        for o in range(1, nz):
            start(l4.at[z], l4.at[z], s4.at[o], r4.at[o], place(turn(z, o, nz), yh, x))

    mine = core * geo.half + y * geo.y_rows + x * geo.x_rows

    def z_sum():
        for o in range(1, nz):
            arrived(l4.at[turn(z, -o, nz)], s4.at[o], r4.at[o])
        total = l4[0]
        for o in range(1, nz):
            total = total + l4[o]
        fin[share(mine, geo.x_rows), :] = total * (1.0 / (geo.z * geo.sheet * geo.y_lo * geo.core))

    def x_spread():
        rows = fin.at[share(mine, geo.x_rows)]
        for o in range(1, nx):
            start(rows, rows, s5.at[o], r5.at[o], place(z, yh, turn(x, o, nx)))

    def x_spread_done():
        for o in range(1, nx):
            first = core * geo.half + y * geo.y_rows + turn(x, -o, nx) * geo.x_rows
            arrived(fin.at[share(first, geo.x_rows)], s5.at[o], r5.at[o])

    def y_spread():
        rows = fin.at[share(core * geo.half + y * geo.y_rows, geo.y_rows)]
        for o in range(1, geo.y):
            start(rows, rows, s6.at[o], r6.at[o], column(turn(y, o, geo.y)))

    def y_spread_done():
        for o in range(1, geo.y):
            first = core * geo.half + turn(y, -o, geo.y) * geo.y_rows
            arrived(fin.at[share(first, geo.y_rows)], s6.at[o], r6.at[o])

    def mate_spread():
        rows = fin.at[share(core * geo.half, geo.half)]
        start(rows, rows, s7.at[0], r7.at[0], mate)

    def mate_spread_done():
        arrived(fin.at[share((geo.core - 1 - core) * geo.half, geo.half)], s7.at[0], r7.at[0])

    half_scale = scale_ref[0] * 0.5
    row_hi[...] = jnp.zeros_like(row_hi)
    row_lo[...] = jnp.zeros_like(row_lo)
    blocks = nz * ROWS // WIDE
    late = turn(z, nz // 2, nz) // (WIDE // ROWS)

    def logits_block(n):
        lanes = pl.ds(pl.multiple_of(n * WIDE, WIDE), WIDE)

        def rows_step(m, sums):
            rows = pl.ds(pl.multiple_of(m * WIDE, WIDE), WIDE)
            logits = dot(ia[rows, :], ta[lanes, :], ((1,), (1,)))
            root = jnp.exp(logits * half_scale)
            probs[rows, lanes] = root
            high = root * math.exp(-HIGH_SHIFT)
            high = high * high
            low = jnp.minimum(root * math.exp(LOW_SHIFT), math.exp(LOW_CAP))
            low = low * low
            row_hi[rows, :] += high[:, :ROWS] + high[:, ROWS:]
            row_lo[rows, :] += low[:, :ROWS] + low[:, ROWS:]
            return (
                sums[0] + jnp.sum(high.reshape(WIDE // 8, 8, WIDE), axis=0),
                sums[1] + jnp.sum(low.reshape(WIDE // 8, 8, WIDE), axis=0),
            )

        zero = jnp.zeros((8, WIDE), f32)
        high, low = lax.fori_loop(0, sheet * ROWS // WIDE, rows_step, (zero, zero))
        high = jnp.sum(high, axis=0, keepdims=True)
        low = jnp.sum(low, axis=0, keepdims=True)
        for j in range(WIDE // ROWS):
            at = n * (WIDE // ROWS) + j
            col_all[z, pl.ds(at, 1), :] = high[:, j * ROWS : (j + 1) * ROWS]
            col_all[z, pl.ds(8 + at, 1), :] = low[:, j * ROWS : (j + 1) * ROWS]

    def half_factor(total):
        high, low = total[0:8], total[8:16]
        small = low < math.exp(LOW_LIMIT)
        lse = jnp.where(small, jnp.log(low) - 2 * LOW_SHIFT, jnp.log(high) + 2 * HIGH_SHIFT)
        return jnp.exp(lse * -0.5) * math.sqrt(0.5)

    def weigh(tile):
        lanes = pl.ds(pl.multiple_of(tile * ROWS, ROWS), ROWS)

        def rows_step(m, carry):
            rows = pl.ds(pl.multiple_of(m * WIDE, WIDE), WIDE)
            root = probs[rows, lanes]
            by_row = root * alpha[rows, :]
            by_col = root * beta[pl.ds(tile, 1), :]
            weights[rows, lanes] = (by_row * by_row + by_col * by_col).astype(bf16)
            return carry

        lax.fori_loop(0, sheet * ROWS // WIDE, rows_step, 0)

    def text_part(j):
        flip[...] = weights[:, full(turn(z, j, nz))].T

        @pl.loop(0, geo.width // WIDE)
        def _(n):
            lanes = pl.ds(pl.multiple_of(n * WIDE, WIDE), WIDE)
            gz[j, :, lanes] = dot(flip[...], ia[:, lanes])

    def image_part(q, j):
        rows = full((yh if q else hy) * nx + turn(x, j, nx))

        @pl.loop(0, geo.width // WIDE)
        def _(n):
            lanes = pl.ds(pl.multiple_of(n * WIDE, WIDE), WIDE)
            gx[q * nx + j, :, lanes] = dot(weights[rows, :], ta[:, lanes])

    def ring_rows(d, k):
        part = (k % 2) ^ d
        return slice(part * PART, (part + 1) * PART)

    def ring_target(d, k, size):
        away = size // 2 - (k + 1) // 2
        return (sign(d) * away) % size

    def z_reduce(d, k):
        value = gz[ring_target(d, k, nz), ring_rows(d, k), :]
        if k >= 2:
            arrived(zin.at[d, k - 2], zrs_s.at[d, k - 2], zrs_r.at[d, k - 2])
            value = value + zin[d, k - 2].astype(f32)
        zout[d, k] = value.astype(bf16)
        to = place(turn(z, sign(d), nz), yh, x)
        start(zout.at[d, k], zin.at[d, k], zrs_s.at[d, k], zrs_r.at[d, k], to)

    def x_reduce(q, d, k):
        value = gx[q * nx + ring_target(d, k, nx), ring_rows(d, k), :]
        if k >= 2:
            arrived(xin.at[q, d, k - 2], xrs_s.at[q, d, k - 2], xrs_r.at[q, d, k - 2])
            value = value + xin[q, d, k - 2].astype(f32)
        xout[q, d, k] = value.astype(bf16)
        to = place(z, yh, turn(x, sign(d), nx))
        start(xout.at[q, d, k], xin.at[q, d, k], xrs_s.at[q, d, k], xrs_r.at[q, d, k], to)

    def ring_last(size):
        return [k for k in (size - 3, size - 2) if k >= 0]

    def x_total(q, c):
        value = gx[q * nx, c * PART : (c + 1) * PART, :]
        for d in range(2):
            for k in ring_last(nx):
                if (k % 2) ^ d == c:
                    arrived(xin.at[q, d, k], xrs_s.at[q, d, k], xrs_r.at[q, d, k])
                    value = value + xin[q, d, k].astype(f32)
        return value

    def z_total(c):
        value = gz[0, c * PART : (c + 1) * PART, :]
        for d in range(2):
            for k in ring_last(nz):
                if (k % 2) ^ d == c:
                    arrived(zin.at[d, k], zrs_s.at[d, k], zrs_r.at[d, k])
                    value = value + zin[d, k].astype(f32)
        return value

    def finish(total, other, unit, inverse, out, c):
        rows = slice(c * PART, (c + 1) * PART)
        grad = scale_ref[0] * (total - other.astype(f32))
        along = jnp.sum(grad * unit[rows, :], axis=-1, keepdims=True)
        out[rows, :] = (inverse[rows, :] * (grad - along * unit[rows, :])).astype(bf16)

    both = range(2)
    kz, kx = nz - 1, nx - 1
    for k in range(min(2, kz)):
        for d in both:
            z_gather(d, k)
    for k in range(min(2, kx)):
        for d in both:
            x_gather(0, d, k)
    for c in both:
        y_gather(c)
    for load in loads[2:]:
        load.wait()
    conv_terms(x_ref, g_ref, k_ref, bias_ref, gain_ref, din_ref, terms_ref, xs, gs, ks, cs, ds, bs)
    din_out = pltpu.make_async_copy(din_ref, din_hbm, load_sem.at[len(loads)])
    din_out.start()
    mate_send()

    def z_step(k):
        if k < kz:
            for d in both:
                z_gathered(d, k)
            if k + 2 < kz:
                for d in both:
                    z_gather(d, k + 2)

    def x_step(q, k):
        if k < kx:
            for d in both:
                x_gathered(q, d, k)
            if k + 2 < kx:
                for d in both:
                    x_gather(q, d, k + 2)

    z_step(0)
    x_step(0, 0)
    z_step(1)
    for c in both:
        y_gathered(c)
        for k in range(min(2, kx)):
            for d in both:
                if (k % 2) ^ d == c:
                    x_gather(1, d, k)
    mate_sum()
    y_send()
    x_step(0, 1)
    z_step(2)
    x_step(0, 2)
    y_sum()
    x_send()
    z_step(3)
    x_step(1, 0)
    z_step(4)
    x_sum()
    for k in range(1, kx):
        x_step(1, k)
    for k in range(5, kz - 1):
        z_step(k)

    @pl.loop(0, blocks - 1)
    def _(i):
        logits_block(lax.rem(late + 1 + i, blocks))

    if kz - 1 >= 5:
        z_step(kz - 1)
    z_send()
    logits_block(late)
    for m in range(sheet):
        rows = slice(m * ROWS, (m + 1) * ROWS)
        row_all[b, m : m + 1, :] = jnp.sum(row_hi[rows, :].T, axis=0, keepdims=True)
        row_all[b, 8 + m : 9 + m, :] = jnp.sum(row_lo[rows, :].T, axis=0, keepdims=True)
    for o in range(1, nz):
        start(col_all.at[z], col_all.at[z], col_s.at[o], col_r.at[o], place(turn(z, o, nz), yh, x))
    for q in both:
        for o in range(nx):
            if q or o:
                i = q * nx + o
                to = place(z, hy if q else yh, turn(x, o, nx))
                start(row_all.at[b], row_all.at[b], row_s.at[i], row_r.at[i], to)
    z_sum()
    x_spread()
    for o in range(1, nz):
        arrived(col_all.at[turn(z, -o, nz)], col_s.at[o], col_r.at[o])
    total = col_all[0]
    for o in range(1, nz):
        total = total + col_all[o]
    beta[...] = half_factor(total)
    for q in both:
        for o in range(nx):
            if q or o:
                i = q * nx + o
                arrived(row_all.at[(hy if q else yh) * nx + turn(x, -o, nx)], row_s.at[i], row_r.at[i])
    total = row_all[0]
    for o in range(1, sheet):
        total = total + row_all[o]
    factor = half_factor(total)
    for m in range(sheet):
        rows = slice(m * ROWS, (m + 1) * ROWS)
        alpha[rows, :] = jnp.broadcast_to(factor[m : m + 1, :], (ROWS, ROWS)).T

    def z_stage(k):
        if k < kz:
            for d in both:
                z_reduce(d, k)

    def x_stage(q, k):
        if k < kx:
            for d in both:
                x_reduce(q, d, k)

    def text_parts(away):
        if 0 < away < nz // 2:
            text_part(away)
            text_part(nz - away)

    def image_parts(q, away):
        if 0 < away < nx // 2:
            image_part(q, away)
            image_part(q, nx - away)

    half = nz // 2
    weigh(turn(z, half, nz))
    text_part(half)
    z_stage(0)
    if half > 1:
        weigh(turn(z, half - 1, nz))
        weigh(turn(z, -(half - 1), nz))
    text_parts(half - 1)
    z_stage(1)
    first = max(half - 1, 1)

    @pl.loop(0, 2 * first - 1)
    def _(i):
        weigh(turn(z, i - (first - 1), nz))

    image_part(0, nx // 2)
    x_stage(0, 0)
    image_parts(0, nx // 2 - 1)
    x_stage(0, 1)
    x_spread_done()
    y_spread()
    image_part(1, nx // 2)
    z_stage(2)
    image_parts(1, nx // 2 - 1)
    x_stage(0, 2)
    x_stage(1, 0)
    x_stage(1, 1)
    text_parts(half - 2)
    z_stage(3)
    image_part(0, 0)
    z_stage(4)
    for c in both:
        yout[c] = x_total(0, c).astype(bf16)
        start(yout.at[c], yin.at[c], yrs_s.at[c], yrs_r.at[c], facing)
    text_parts(half - 3)
    z_stage(5)
    x_stage(1, 2)
    y_spread_done()
    mate_spread()
    z_stage(6)
    image_part(1, 0)
    text_part(0)
    mate_spread_done()
    for row in range(KS):
        for t in range(TILES):
            kg_ref[row, :, t * LANES : (t + 1) * LANES] = fin[
                pl.ds(row * KS * TILES + t, KS, stride=TILES), :
            ]
    for t in range(TILES):
        cg_ref[:, t * LANES : (t + 1) * LANES] = fin[pl.ds(SPOTS * TILES + t, 3, stride=TILES), :]
    kg_out = pltpu.make_async_copy(kg_ref, kg_hbm, load_sem.at[len(loads) + 1])
    kg_out.start()
    for c in both:
        value = x_total(1, c)
        arrived(yin.at[c], yrs_s.at[c], yrs_r.at[c])
        finish(value + yin[c].astype(f32), ta[slot(z, c), :], ui, vi, ig_ref, c)
    for c in both:
        finish(z_total(c), ia[slot(b, c), :], ut, vt, tg_ref, c)
    din_out.wait()
    kg_out.wait()
    for moving in sent:
        moving.wait_send()


def loss_block(geo, scale, image_rows, text_rows, x, g, k, bias, gain):
    f32, bf16 = jnp.float32, jnp.bfloat16
    vmem = pltpu.VMEM
    dma = pltpu.SemaphoreType.DMA
    images, texts, width = geo.sheet * ROWS, geo.z * ROWS, geo.width
    kz, kx = geo.z - 1, geo.x - 1
    big = vmem((SPOTS * TILES, LANES), f32)
    maps = vmem((GRID, GRID, TILES * LANES), bf16)
    scratch = [
        maps, vmem((KS, KS, TILES * LANES), f32), vmem((ROWS, width), bf16), vmem((ROWS, width), bf16), maps, maps, maps,
        vmem((TILES * LANES,), bf16), vmem((TILES * LANES,), bf16), vmem((SLACK, LANES), f32),
        big, big, big, big, big, vmem((2 * TILES, LANES), f32), dma((9,)),
        vmem((images, width), bf16), vmem((texts, width), bf16),
        vmem((ROWS, width), f32), vmem((ROWS, width), f32), vmem((ROWS, 1), f32), vmem((ROWS, 1), f32),
        vmem((images, texts), f32), vmem((images, texts), bf16), vmem((ROWS, images), bf16),
        vmem((images, ROWS), f32), vmem((images, ROWS), f32), vmem((images, ROWS), f32), vmem((8, ROWS), f32),
        vmem((geo.sheet, 16, ROWS), f32), vmem((geo.z, 16, ROWS), f32),
        vmem((geo.z, ROWS, width), f32), vmem((2 * geo.x, ROWS, width), f32),
        vmem((2, kz, PART, width), bf16), vmem((2, kz, PART, width), bf16),
        vmem((2, 2, kx, PART, width), bf16), vmem((2, 2, kx, PART, width), bf16),
        vmem((2, PART, width), bf16), vmem((2, PART, width), bf16),
        vmem((geo.half, LANES), f32), vmem((geo.half, LANES), f32),
        vmem((geo.y, geo.y_rows, LANES), f32), vmem((geo.y_rows, LANES), f32),
        vmem((geo.x, geo.x_rows, LANES), f32), vmem((geo.z, geo.x_rows, LANES), f32), vmem((SLACK, LANES), f32),
        dma((2, kz)), dma((2, kz)), dma((2, 2, kx)), dma((2, 2, kx)), dma((2,)), dma((2,)),
        dma((geo.sheet,)), dma((geo.sheet,)), dma((geo.z,)), dma((geo.z,)),
        dma((2, kz)), dma((2, kz)), dma((2, 2, kx)), dma((2, 2, kx)), dma((2,)), dma((2,)),
        dma((1,)), dma((1,)), dma((geo.y,)), dma((geo.y,)), dma((geo.x,)), dma((geo.x,)), dma((geo.z,)), dma((geo.z,)),
        dma((geo.x,)), dma((geo.x,)), dma((geo.y,)), dma((geo.y,)), dma((1,)), dma((1,)),
    ]
    return pl.pallas_call(
        functools.partial(loss_kernel, geo),
        out_shape=(
            jax.ShapeDtypeStruct((ROWS, width), bf16),
            jax.ShapeDtypeStruct((ROWS, width), bf16),
            jax.ShapeDtypeStruct((3, TILES * LANES), f32),
            jax.ShapeDtypeStruct((GRID, GRID, TILES * LANES), bf16),
            jax.ShapeDtypeStruct((KS, KS, TILES * LANES), f32),
        ),
        in_specs=[pl.BlockSpec(memory_space=pltpu.SMEM)] + [pl.BlockSpec(memory_space=pltpu.HBM)] * 7,
        out_specs=[pl.BlockSpec(memory_space=pltpu.VMEM)] * 3 + [pl.BlockSpec(memory_space=pltpu.HBM)] * 2,
        scratch_shapes=scratch,
        compiler_params=pltpu.CompilerParams(
            collective_id=0, has_side_effects=True, vmem_limit_bytes=60 << 20
        ),
    )(scale.reshape(1), image_rows, text_rows, x, g, k, bias, gain)


def hand_out_kernel(*refs):
    count = (len(refs) - 2) // 3
    into, away = refs[-2], refs[-1]
    loads = [pltpu.make_async_copy(refs[i], refs[2 * count + i], into.at[i]) for i in range(count)]
    stores = [pltpu.make_async_copy(refs[2 * count + i], refs[count + i], away.at[i]) for i in range(count)]
    for moving in loads:
        moving.start()
    for load, store in zip(loads, stores):
        load.wait()
        store.start()
    for moving in stores:
        moving.wait()


def hand_out(*arrays):
    held = [pl.BlockSpec(memory_space=pltpu.HBM)] * len(arrays)
    sems = pltpu.SemaphoreType.DMA((len(arrays),))
    return pl.pallas_call(
        hand_out_kernel,
        out_shape=tuple(jax.ShapeDtypeStruct(a.shape, a.dtype) for a in arrays),
        in_specs=held,
        out_specs=held,
        scratch_shapes=[pltpu.VMEM(a.shape, a.dtype) for a in arrays] + [sems, sems],
        compiler_params=pltpu.CompilerParams(vmem_limit_bytes=60 << 20),
    )(*arrays)


def per_device(
    geo, image_embed, text_embed, logit_scale, block_input, dw_kernel, dw_bias, ln_gain, block_grad
):
    image_grad, text_grad, channel_grads, d_input, kernel_grad = hand_out(
        *loss_block(
            geo, logit_scale, image_embed[0], text_embed[0],
            block_input[0], block_grad[0], dw_kernel, dw_bias, ln_gain,
        )
    )
    return (image_grad[None], text_grad[None], d_input[None], kernel_grad, channel_grads)


def solution(mesh, geo=None):
    geo = geo or Geometry(8, 2, 4, 2, 2, 1024)
    placed = (
        P("grp", "blk", None),
        P("grp", "blk", None),
        P(),
        P(("blk", "grp"), None, None, None),
        P(),
        P(),
        P(),
        P(("blk", "grp"), None, None, None),
    )
    return jax.shard_map(
        functools.partial(per_device, geo),
        mesh=mesh,
        in_specs=placed,
        out_specs=(
            P("grp", "blk", None),
            P("grp", "blk", None),
            P(("blk", "grp"), None, None, None),
            P(),
            P(),
        ),
        check_vma=False,
    )
```

```python
import functools
import math

import jax
import jax.numpy as jnp
from jax import lax
from jax.experimental import pallas as pl
from jax.experimental.pallas import tpu as pltpu
from jax.sharding import PartitionSpec as P

GRID = 7
KS = 7
EPS = 1e-06
LANES = 128
TILES = 24
SPOTS = GRID * GRID
HALF = KS // 2


def spot_mean(value, count):
    folded = value[:, 0:8] + value[:, 8:16] + value[:, 16:24]
    folded = jnp.sum(folded, axis=1, keepdims=True)
    return jnp.sum(folded, axis=2, keepdims=True) * (1.0 / count)


def conv_terms(x_ref, g_ref, k_ref, bias_ref, gain_ref, din_ref, terms_ref, xs, gs, ks, cs, ds, bs):
    channels = TILES * LANES

    def spread(src, dst):
        for y in range(GRID):
            for t in range(TILES):
                dst[pl.ds(y * GRID * TILES + t, GRID, stride=TILES), :] = src[
                    y, :, t * LANES : (t + 1) * LANES
                ].astype(jnp.float32)

    spread(x_ref, xs)
    spread(k_ref, ks)
    spread(g_ref, gs)
    bs[0:TILES, :] = bias_ref[...].astype(jnp.float32).reshape(TILES, LANES)
    bs[TILES : 2 * TILES, :] = gain_ref[...].astype(jnp.float32).reshape(TILES, LANES)

    def rows(part, spot):
        return pl.ds(pl.multiple_of(spot * TILES + part * 8, 8), 8)

    def gather(src, part, row):
        return [src[rows(part, row * GRID + x), :] for x in range(GRID)]

    @pl.loop(0, TILES // 8)
    def _(part):
        bias = bs[pl.ds(pl.multiple_of(part * 8, 8), 8), :]
        for y in range(GRID):
            sums = [bias] * GRID
            for a in range(KS):
                if not 0 <= y + a - HALF < GRID:
                    continue
                left = gather(xs, part, y + a - HALF)
                taps = gather(ks, part, a)
                for x in range(GRID):
                    for b in range(KS):
                        if 0 <= x + b - HALF < GRID:
                            sums[x] = sums[x] + left[x + b - HALF] * taps[b]
            for x in range(GRID):
                cs[rows(part, y * GRID + x), :] = sums[x]

    gain = bs[TILES : 2 * TILES, :][None]
    dsum = jnp.zeros((TILES, LANES), jnp.float32)
    nsum = jnp.zeros((TILES, LANES), jnp.float32)
    gsum = jnp.zeros((TILES, LANES), jnp.float32)
    for y in range(GRID):
        span = slice(y * GRID * TILES, (y + 1) * GRID * TILES)
        conv = cs[span, :].reshape(GRID, TILES, LANES)
        grad = gs[span, :].reshape(GRID, TILES, LANES)
        centre = conv - spot_mean(conv, channels)
        d_normed = grad * gain
        inv = lax.rsqrt(spot_mean(centre * centre, channels) + EPS)
        normed = centre * inv
        d_conv = inv * (
            d_normed - spot_mean(d_normed, channels) - normed * spot_mean(d_normed * normed, channels)
        )
        ds[span, :] = d_conv.reshape(GRID * TILES, LANES)
        dsum = dsum + jnp.sum(d_conv, axis=0)
        nsum = nsum + jnp.sum(grad * normed, axis=0)
        gsum = gsum + jnp.sum(grad, axis=0)
    first = SPOTS * TILES
    for index, total in enumerate((dsum, nsum, gsum)):
        terms_ref[first + index * TILES : first + (index + 1) * TILES, :] = total
    first = first + 3 * TILES
    terms_ref[first:SLACK, :] = jnp.zeros((SLACK - first, LANES), jnp.float32)

    @pl.loop(0, TILES // 8)
    def _(part):
        for y in range(GRID):
            sums = [None] * GRID
            for a in range(KS):
                if not 0 <= y - a + HALF < GRID:
                    continue
                left = gather(ds, part, y - a + HALF)
                taps = gather(ks, part, a)
                for x in range(GRID):
                    for b in range(KS):
                        if 0 <= x - b + HALF < GRID:
                            term = left[x - b + HALF] * taps[b]
                            sums[x] = term if sums[x] is None else sums[x] + term
            for x in range(GRID):
                cs[rows(part, y * GRID + x), :] = sums[x]
        for a in range(KS):
            sums = [None] * KS
            for y in range(GRID):
                if not 0 <= y + a - HALF < GRID:
                    continue
                left = gather(ds, part, y)
                right = gather(xs, part, y + a - HALF)
                for b in range(KS):
                    for x in range(GRID):
                        if 0 <= x + b - HALF < GRID:
                            term = left[x] * right[x + b - HALF]
                            sums[b] = term if sums[b] is None else sums[b] + term
            for b in range(KS):
                terms_ref[rows(part, a * KS + b), :] = sums[b]

    for y in range(GRID):
        for t in range(TILES):
            din_ref[y, :, t * LANES : (t + 1) * LANES] = cs[
                pl.ds(y * GRID * TILES + t, GRID, stride=TILES), :
            ].astype(jnp.bfloat16)


ROWS = 128
PART = 64
WIDE = 256
MESH = pl.DeviceIdType.MESH
SLACK = 1280
HIGH_SHIFT = 12.0
LOW_SHIFT = 10.0
LOW_CAP = 30.0
LOW_LIMIT = 55.0


class Geometry:
    def __init__(self, z, y_hi, x, y_lo, core, width):
        self.z, self.y_hi, self.x, self.y_lo, self.core, self.width = z, y_hi, x, y_lo, core, width
        self.sheet = y_hi * x
        self.y = y_hi * y_lo
        self.half = SLACK // core
        self.y_rows = self.half // self.y
        self.x_rows = self.y_rows // x


def dot(left, right, dims=((1,), (0,))):
    return lax.dot_general(left, right, (dims, ((), ())), preferred_element_type=jnp.float32)


def loss_kernel(
    geo, scale_ref, img_hbm, txt_hbm, x_hbm, g_hbm, k_hbm, bias_hbm, gain_hbm,
    ig_ref, tg_ref, cg_ref, din_hbm, kg_hbm,
    din_ref, kg_ref, img_ref, txt_ref, x_ref, g_ref, k_ref, bias_ref, gain_ref, terms_ref, xs, gs, ks, cs, ds, bs, load_sem,
    ia, ta, ui, ut, vi, vt, probs, weights, flip, pick, row_hi, row_lo, alpha, beta, row_raw, col_raw, row_all, col_all, gz, gx,
    zout, zin, xout, xin, yout, yin, l1, hsum, l2, qsum, l3, l4, fin,
    zag_s, zag_r, xag_s, xag_r, yag_s, yag_r, row_s, row_r, col_s, col_r,
    zrs_s, zrs_r, xrs_s, xrs_r, yrs_s, yrs_r,
    s1, r1, s2, r2, s3, r3, s4, r4, s5, r5, s6, r6, s7, r7,
):
    f32, bf16 = jnp.float32, jnp.bfloat16
    nz, nx, sheet = geo.z, geo.x, geo.sheet
    blk, grp = lax.axis_index("blk"), lax.axis_index("grp")
    z, b = blk // sheet, lax.rem(blk, sheet)
    yh, x = b // nx, lax.rem(b, nx)
    yl, core = grp // geo.core, lax.rem(grp, geo.core)
    y = yh * geo.y_lo + yl
    hy = 1 - yh

    def place(z_to, yh_to, x_to):
        return {"blk": z_to * sheet + yh_to * nx + x_to, "grp": grp}

    def column(y_to):
        return {
            "blk": z * sheet + (y_to // geo.y_lo) * nx + x,
            "grp": lax.rem(y_to, geo.y_lo) * geo.core + core,
        }

    def turn(value, by, size):
        return lax.rem(value + by + size, size)

    mate = {"blk": blk, "grp": yl * geo.core + (geo.core - 1 - core)}
    facing = place(z, hy, x)
    sent = []

    def copy(src, dst, send, recv, to):
        return pltpu.make_async_remote_copy(
            src_ref=src, dst_ref=dst, send_sem=send, recv_sem=recv, device_id=to, device_id_type=MESH
        )

    def start(*args):
        moving = copy(*args)
        moving.start()
        sent.append(moving)

    def arrived(dst, send, recv):
        copy(dst, dst, send, recv, facing).wait_recv()

    barrier = pltpu.get_barrier_semaphore()
    peers = [place(turn(z, o, nz), yh, x) for o in range(1, nz)]
    for q in range(2):
        for o in range(nx):
            if q or o:
                peers.append(place(z, hy if q else yh, turn(x, o, nx)))
    for o in range(1, geo.y):
        if o != geo.y_lo:
            peers.append(column(turn(y, o, geo.y)))
    peers.append(mate)
    for peer in peers:
        pl.semaphore_signal(barrier, inc=1, device_id=peer, device_id_type=MESH)
    operands = (txt_hbm, img_hbm, x_hbm, k_hbm, g_hbm, bias_hbm, gain_hbm)
    held = (txt_ref, img_ref, x_ref, k_ref, g_ref, bias_ref, gain_ref)
    loads = [
        pltpu.make_async_copy(src, dst, load_sem.at[i]) for i, (src, dst) in enumerate(zip(operands, held))
    ]
    for load in loads:
        load.start()

    def slot(index, part):
        return pl.ds(pl.multiple_of(index * ROWS + part * PART, PART), PART)

    def full(index):
        return pl.ds(pl.multiple_of(index * ROWS, ROWS), ROWS)

    def unit_rows(raw, unit, inverse, everyone, index):
        values = raw[...].astype(f32)
        inv = lax.rsqrt(jnp.sum(values * values, axis=-1, keepdims=True) + EPS)
        scaled = values * inv
        unit[...] = scaled
        inverse[...] = inv
        everyone[full(index), :] = scaled.astype(bf16)

    row_hi[...] = jnp.zeros_like(row_hi)
    row_lo[...] = jnp.zeros_like(row_lo)
    row_raw[...] = jnp.zeros_like(row_raw)
    col_raw[...] = jnp.zeros_like(col_raw)
    loads[0].wait()
    unit_rows(txt_ref, ut, vt, ta, z)
    loads[1].wait()
    unit_rows(img_ref, ui, vi, ia, b)
    pl.semaphore_wait(barrier, len(peers))

    def sign(d):
        return 1 - 2 * d

    def z_gather(d, k):
        rows = slot(turn(z, -sign(d) * (k // 2), nz), (k % 2) ^ d)
        to = place(turn(z, sign(d), nz), yh, x)
        start(ta.at[rows], ta.at[rows], zag_s.at[d, k], zag_r.at[d, k], to)

    def z_gathered(d, k):
        rows = slot(turn(z, -sign(d) * (k // 2 + 1), nz), (k % 2) ^ d)
        arrived(ta.at[rows], zag_s.at[d, k], zag_r.at[d, k])

    def x_gather(part, d, s, facing_set=False):
        side = hy if facing_set else yh
        rows = slot(side * nx + turn(x, -sign(d) * s, nx), part)
        to = place(z, yh, turn(x, sign(d), nx))
        i = 2 if facing_set else part
        start(ia.at[rows], ia.at[rows], xag_s.at[i, d, s], xag_r.at[i, d, s], to)

    def x_gathered(part, d, s, facing_set=False):
        side = hy if facing_set else yh
        rows = slot(side * nx + turn(x, -sign(d) * (s + 1), nx), part)
        i = 2 if facing_set else part
        arrived(ia.at[rows], xag_s.at[i, d, s], xag_r.at[i, d, s])

    def y_gather(part, j):
        rows = slot(yh * nx + turn(x, j, nx), part)
        i = j + 1 if part else 0
        start(ia.at[rows], ia.at[rows], yag_s.at[i], yag_r.at[i], facing)

    def y_gathered(part, j):
        rows = slot(hy * nx + turn(x, j, nx), part)
        i = j + 1 if part else 0
        arrived(ia.at[rows], yag_s.at[i], yag_r.at[i])

    def share(first, rows):
        return pl.ds(pl.multiple_of(first, 8), rows)

    def mate_send():
        start(terms_ref.at[share((geo.core - 1 - core) * geo.half, geo.half)], l1, s1.at[0], r1.at[0], mate)

    def mate_sum():
        arrived(l1, s1.at[0], r1.at[0])
        hsum[...] = terms_ref[share(core * geo.half, geo.half), :] + l1[...]

    def y_send():
        for o in range(1, geo.y):
            to = turn(y, o, geo.y)
            start(hsum.at[share(to * geo.y_rows, geo.y_rows)], l2.at[o], s2.at[o], r2.at[o], column(to))

    def y_sum():
        total = hsum[share(y * geo.y_rows, geo.y_rows), :]
        for o in range(1, geo.y):
            arrived(l2.at[o], s2.at[o], r2.at[o])
            total = total + l2[o]
        qsum[...] = total

    def x_send():
        for o in range(1, nx):
            to = turn(x, o, nx)
            start(qsum.at[share(to * geo.x_rows, geo.x_rows)], l3.at[o], s3.at[o], r3.at[o], place(z, yh, to))

    def x_sum():
        total = qsum[share(x * geo.x_rows, geo.x_rows), :]
        for o in range(1, nx):
            arrived(l3.at[o], s3.at[o], r3.at[o])
            total = total + l3[o]
        l4[z] = total

    def z_send():
        for o in range(1, nz):
            start(l4.at[z], l4.at[z], s4.at[o], r4.at[o], place(turn(z, o, nz), yh, x))

    mine = core * geo.half + y * geo.y_rows + x * geo.x_rows

    def z_sum():
        for o in range(1, nz):
            arrived(l4.at[turn(z, -o, nz)], s4.at[o], r4.at[o])
        total = l4[0]
        for o in range(1, nz):
            total = total + l4[o]
        fin[share(mine, geo.x_rows), :] = total * (1.0 / (geo.z * geo.sheet * geo.y_lo * geo.core))

    def x_spread():
        rows = fin.at[share(mine, geo.x_rows)]
        for o in range(1, nx):
            start(rows, rows, s5.at[o], r5.at[o], place(z, yh, turn(x, o, nx)))

    def x_spread_done():
        for o in range(1, nx):
            first = core * geo.half + y * geo.y_rows + turn(x, -o, nx) * geo.x_rows
            arrived(fin.at[share(first, geo.x_rows)], s5.at[o], r5.at[o])

    def y_spread():
        rows = fin.at[share(core * geo.half + y * geo.y_rows, geo.y_rows)]
        for o in range(1, geo.y):
            start(rows, rows, s6.at[o], r6.at[o], column(turn(y, o, geo.y)))

    def y_spread_done():
        for o in range(1, geo.y):
            first = core * geo.half + turn(y, -o, geo.y) * geo.y_rows
            arrived(fin.at[share(first, geo.y_rows)], s6.at[o], r6.at[o])

    def mate_spread():
        rows = fin.at[share(core * geo.half, geo.half)]
        start(rows, rows, s7.at[0], r7.at[0], mate)

    def mate_spread_done():
        arrived(fin.at[share((geo.core - 1 - core) * geo.half, geo.half)], s7.at[0], r7.at[0])

    power = scale_ref[0] * (0.5 / math.log(2.0))
    late = turn(z, nz // 2, nz)

    def logits_block(tile, width, first, count, unroll=1):
        lanes = pl.ds(pl.multiple_of(tile * ROWS, ROWS), width)

        def rows_step(m, sums):
            rows = pl.ds(pl.multiple_of((first + m) * WIDE, WIDE), WIDE)
            logits = dot(ia[rows, :], ta[lanes, :], ((1,), (1,)))
            root = jnp.exp2(logits * power)
            probs[rows, lanes] = root
            high = root * math.exp(-HIGH_SHIFT)
            high = high * high
            low = jnp.minimum(root * math.exp(LOW_SHIFT), math.exp(LOW_CAP))
            low = low * low
            row_hi[rows, :] += sum(high[:, j : j + ROWS] for j in range(0, width, ROWS))
            row_lo[rows, :] += sum(low[:, j : j + ROWS] for j in range(0, width, ROWS))
            return (
                sums[0] + jnp.sum(high.reshape(WIDE // 8, 8, width), axis=0),
                sums[1] + jnp.sum(low.reshape(WIDE // 8, 8, width), axis=0),
            )

        zero = jnp.zeros((8, width), f32)
        high, low = lax.fori_loop(0, count, rows_step, (zero, zero), unroll=unroll)
        high = jnp.sum(high, axis=0, keepdims=True)
        low = jnp.sum(low, axis=0, keepdims=True)
        for j in range(width // ROWS):
            col_raw[pl.ds(tile + j, 1), :] += high[:, j * ROWS : (j + 1) * ROWS]
            col_raw[pl.ds(8 + tile + j, 1), :] += low[:, j * ROWS : (j + 1) * ROWS]

    def local_lse(total):
        high, low = total[0:8], total[8:16]
        small = low < math.exp(LOW_LIMIT)
        return jnp.where(small, jnp.log(low) - 2 * LOW_SHIFT, jnp.log(high) + 2 * HIGH_SHIFT)

    def half_factor(parts, count):
        peak = parts[0]
        for o in range(1, count):
            peak = jnp.maximum(peak, parts[o])
        total = jnp.exp(parts[0] - peak)
        for o in range(1, count):
            total = total + jnp.exp(parts[o] - peak)
        return jnp.exp((peak + jnp.log(total)) * -0.5) * math.sqrt(0.5)

    def weigh(tile):
        lanes = pl.ds(pl.multiple_of(tile * ROWS, ROWS), ROWS)

        def rows_step(m, carry):
            rows = pl.ds(pl.multiple_of(m * WIDE, WIDE), WIDE)
            root = probs[rows, lanes]
            by_row = root * alpha[rows, :]
            by_col = root * beta[pl.ds(tile, 1), :]
            weights[rows, lanes] = (by_row * by_row + by_col * by_col).astype(bf16)
            return carry

        lax.fori_loop(0, sheet * ROWS // WIDE, rows_step, 0)

    def text_part(*shifts):
        for i, j in enumerate(shifts):
            flip[i * ROWS : (i + 1) * ROWS, :] = weights[:, full(turn(z, j, nz))].T
        for n in range(0, geo.width, WIDE):
            part = dot(flip[: len(shifts) * ROWS, :], ia[:, n : n + WIDE])
            for i, j in enumerate(shifts):
                gz[j, :, n : n + WIDE] = part[i * ROWS : (i + 1) * ROWS]

    def image_part(*shifts):
        for i, (q, j) in enumerate(shifts):
            pick[i * ROWS : (i + 1) * ROWS, :] = weights[full((yh if q else hy) * nx + turn(x, j, nx)), :]
        for n in range(0, geo.width, WIDE):
            part = dot(pick[: len(shifts) * ROWS, :], ta[:, n : n + WIDE])
            for i, (q, j) in enumerate(shifts):
                gx[q * nx + j, :, n : n + WIDE] = part[i * ROWS : (i + 1) * ROWS]

    def ring_rows(d, k):
        part = (k % 2) ^ d
        return slice(part * PART, (part + 1) * PART)

    def ring_target(d, k, size):
        away = size // 2 - (k + 1) // 2
        return (sign(d) * away) % size

    def z_reduce(d, k):
        value = gz[ring_target(d, k, nz), ring_rows(d, k), :]
        if k >= 2:
            arrived(zin.at[d, k - 2], zrs_s.at[d, k - 2], zrs_r.at[d, k - 2])
            value = value + zin[d, k - 2].astype(f32)
        zout[d, k] = value.astype(bf16)
        to = place(turn(z, sign(d), nz), yh, x)
        start(zout.at[d, k], zin.at[d, k], zrs_s.at[d, k], zrs_r.at[d, k], to)

    def x_reduce(q, d, k):
        value = gx[q * nx + ring_target(d, k, nx), ring_rows(d, k), :]
        if k >= 2:
            arrived(xin.at[q, d, k - 2], xrs_s.at[q, d, k - 2], xrs_r.at[q, d, k - 2])
            value = value + xin[q, d, k - 2].astype(f32)
        xout[q, d, k] = value.astype(bf16)
        to = place(z, yh, turn(x, sign(d), nx))
        start(xout.at[q, d, k], xin.at[q, d, k], xrs_s.at[q, d, k], xrs_r.at[q, d, k], to)

    def ring_last(size):
        return [k for k in (size - 3, size - 2) if k >= 0]

    def x_total(q, c):
        value = gx[q * nx, c * PART : (c + 1) * PART, :]
        for d in range(2):
            for k in ring_last(nx):
                if (k % 2) ^ d == c:
                    arrived(xin.at[q, d, k], xrs_s.at[q, d, k], xrs_r.at[q, d, k])
                    value = value + xin[q, d, k].astype(f32)
        return value

    def z_total(c):
        value = gz[0, c * PART : (c + 1) * PART, :]
        for d in range(2):
            for k in ring_last(nz):
                if (k % 2) ^ d == c:
                    arrived(zin.at[d, k], zrs_s.at[d, k], zrs_r.at[d, k])
                    value = value + zin[d, k].astype(f32)
        return value

    def finish(total, other, unit, inverse, out, c):
        rows = slice(c * PART, (c + 1) * PART)
        grad = scale_ref[0] * (total - other.astype(f32))
        along = jnp.sum(grad * unit[rows, :], axis=-1, keepdims=True)
        out[rows, :] = (inverse[rows, :] * (grad - along * unit[rows, :])).astype(bf16)

    both = range(2)
    kz, kx = nz - 1, nx - 1
    for k in range(min(2, kz)):
        for d in both:
            z_gather(d, k)
    for part in (1, 0):
        for d in both:
            x_gather(part, d, 0)
    y_gather(0, 0)
    y_gather(1, 0)
    for load in loads[2:]:
        load.wait()
    conv_terms(x_ref, g_ref, k_ref, bias_ref, gain_ref, din_ref, terms_ref, xs, gs, ks, cs, ds, bs)
    din_out = pltpu.make_async_copy(din_ref, din_hbm, load_sem.at[len(loads)])
    din_out.start()
    mate_send()

    def z_step(k):
        if k < kz:
            for d in both:
                z_gathered(d, k)
            if k + 2 < kz:
                for d in both:
                    z_gather(d, k + 2)

    z_step(0)
    for d in both:
        x_gathered(1, d, 0)
    x_gather(1, 1, 1)
    y_gather(1, nx - 1)
    y_gather(1, 1)
    y_gathered(0, 0)
    for d in both:
        x_gather(0, d, 0, True)
    for d in both:
        x_gathered(0, d, 0)
    x_gather(0, 0, 1)
    z_step(1)
    mate_sum()
    y_send()
    x_gathered(1, 1, 1)
    y_gather(1, 2)
    pairs = nz * ROWS // WIDE
    count = nx * ROWS // WIDE
    lean = 2 * lax.rem(z, 2) - 1
    near = 2 * (z // 2)
    next_pair = 2 * turn(z // 2, lean, pairs)
    far_pair = 2 * turn(z // 2, -lean, pairs)
    ours, theirs = yh * count, hy * count
    z_step(2)
    for d in both:
        x_gathered(0, d, 0, True)
    x_gather(0, 0, 1, True)
    x_gathered(0, 0, 1)
    logits_block(near, WIDE, ours, count)
    z_step(3)
    logits_block(next_pair, WIDE, ours, count)
    for j in (0, nx - 1, 1):
        y_gathered(1, j)
    x_gathered(0, 0, 1, True)
    z_step(4)
    y_sum()
    x_send()
    y_gathered(1, 2)
    logits_block(near, WIDE, theirs, count)
    logits_block(next_pair, WIDE, theirs, count)
    for k in range(5, kz - 1):
        z_step(k)
    x_sum()
    logits_block(far_pair, WIDE, 0, 2 * count)
    logits_block(late + 1 - 2 * lax.rem(late, 2), ROWS, 0, 2 * count)
    z_step(kz - 1)
    logits_block(late, ROWS, 0, 2 * count, True)
    for m in range(sheet):
        rows = slice(m * ROWS, (m + 1) * ROWS)
        row_raw[m : m + 1, :] = jnp.sum(row_hi[rows, :].T, axis=0, keepdims=True)
        row_raw[8 + m : 9 + m, :] = jnp.sum(row_lo[rows, :].T, axis=0, keepdims=True)
    row_all[b] = local_lse(row_raw[...])
    col_all[z] = local_lse(col_raw[...])
    for q in both:
        for o in range(nx):
            if q or o:
                i = q * nx + o
                to = place(z, hy if q else yh, turn(x, o, nx))
                start(row_all.at[b], row_all.at[b], row_s.at[i], row_r.at[i], to)
    for o in range(1, nz):
        start(col_all.at[z], col_all.at[z], col_s.at[o], col_r.at[o], place(turn(z, o, nz), yh, x))
    z_send()
    for o in range(1, nz):
        arrived(col_all.at[turn(z, -o, nz)], col_s.at[o], col_r.at[o])
    beta[...] = half_factor(col_all, nz)
    for q in both:
        for o in range(nx):
            if q or o:
                i = q * nx + o
                arrived(row_all.at[(hy if q else yh) * nx + turn(x, -o, nx)], row_s.at[i], row_r.at[i])
    factor = half_factor(row_all, sheet)
    for m in range(sheet):
        rows = slice(m * ROWS, (m + 1) * ROWS)
        alpha[rows, :] = jnp.broadcast_to(factor[m : m + 1, :], (ROWS, ROWS)).T

    def z_stage(k):
        if k < kz:
            for d in both:
                z_reduce(d, k)

    def x_stage(q, k):
        if k < kx:
            for d in both:
                x_reduce(q, d, k)

    half = nz // 2
    weigh(turn(z, half, nz))
    text_part(half)
    z_stage(0)

    @pl.loop(0, nz - 1)
    def _(i):
        weigh(turn(z, i - (half - 1), nz))

    image_part((0, 2))
    x_stage(0, 0)
    text_part(half - 1, nz - half + 1)
    z_stage(1)
    image_part((0, 1), (0, 3))
    x_stage(0, 1)
    z_sum()
    x_spread()
    image_part((1, 2), (0, 0))
    z_stage(2)
    x_stage(0, 2)
    x_stage(1, 0)
    image_part((1, 1), (1, 3))
    x_stage(1, 1)
    text_part(half - 2, nz - half + 2)
    z_stage(3)
    x_spread_done()
    y_spread()
    z_stage(4)
    for c in both:
        yout[c] = x_total(0, c).astype(bf16)
        start(yout.at[c], yin.at[c], yrs_s.at[c], yrs_r.at[c], facing)
    text_part(half - 3, nz - half + 3)
    z_stage(5)
    x_stage(1, 2)
    y_spread_done()
    mate_spread()
    z_stage(6)
    image_part((1, 0))
    text_part(0)
    mate_spread_done()
    for row in range(KS):
        for t in range(TILES):
            kg_ref[row, :, t * LANES : (t + 1) * LANES] = fin[
                pl.ds(row * KS * TILES + t, KS, stride=TILES), :
            ]
    for t in range(TILES):
        cg_ref[:, t * LANES : (t + 1) * LANES] = fin[pl.ds(SPOTS * TILES + t, 3, stride=TILES), :]
    kg_out = pltpu.make_async_copy(kg_ref, kg_hbm, load_sem.at[len(loads) + 1])
    kg_out.start()
    for c in both:
        value = x_total(1, c)
        arrived(yin.at[c], yrs_s.at[c], yrs_r.at[c])
        finish(value + yin[c].astype(f32), ta[slot(z, c), :], ui, vi, ig_ref, c)
    for c in both:
        finish(z_total(c), ia[slot(b, c), :], ut, vt, tg_ref, c)
    din_out.wait()
    kg_out.wait()
    for moving in sent:
        moving.wait_send()


def loss_block(geo, scale, image_rows, text_rows, x, g, k, bias, gain):
    f32, bf16 = jnp.float32, jnp.bfloat16
    vmem = pltpu.VMEM
    dma = pltpu.SemaphoreType.DMA
    images, texts, width = geo.sheet * ROWS, geo.z * ROWS, geo.width
    kz, kx = geo.z - 1, geo.x - 1
    big = vmem((SPOTS * TILES, LANES), f32)
    maps = vmem((GRID, GRID, TILES * LANES), bf16)
    scratch = [
        maps, vmem((KS, KS, TILES * LANES), f32), vmem((ROWS, width), bf16), vmem((ROWS, width), bf16), maps, maps, maps,
        vmem((TILES * LANES,), bf16), vmem((TILES * LANES,), bf16), vmem((SLACK, LANES), f32),
        big, big, big, big, big, vmem((2 * TILES, LANES), f32), dma((9,)),
        vmem((images, width), bf16), vmem((texts, width), bf16),
        vmem((ROWS, width), f32), vmem((ROWS, width), f32), vmem((ROWS, 1), f32), vmem((ROWS, 1), f32),
        vmem((images, texts), f32), vmem((images, texts), bf16), vmem((2 * ROWS, images), bf16), vmem((2 * ROWS, texts), bf16),
        vmem((images, ROWS), f32), vmem((images, ROWS), f32), vmem((images, ROWS), f32), vmem((8, ROWS), f32),
        vmem((16, ROWS), f32), vmem((16, ROWS), f32),
        vmem((geo.sheet, 8, ROWS), f32), vmem((geo.z, 8, ROWS), f32),
        vmem((geo.z, ROWS, width), f32), vmem((2 * geo.x, ROWS, width), f32),
        vmem((2, kz, PART, width), bf16), vmem((2, kz, PART, width), bf16),
        vmem((2, 2, kx, PART, width), bf16), vmem((2, 2, kx, PART, width), bf16),
        vmem((2, PART, width), bf16), vmem((2, PART, width), bf16),
        vmem((geo.half, LANES), f32), vmem((geo.half, LANES), f32),
        vmem((geo.y, geo.y_rows, LANES), f32), vmem((geo.y_rows, LANES), f32),
        vmem((geo.x, geo.x_rows, LANES), f32), vmem((geo.z, geo.x_rows, LANES), f32), vmem((SLACK, LANES), f32),
        dma((2, kz)), dma((2, kz)), dma((3, 2, 2)), dma((3, 2, 2)), dma((1 + geo.x,)), dma((1 + geo.x,)),
        dma((geo.sheet,)), dma((geo.sheet,)), dma((geo.z,)), dma((geo.z,)),
        dma((2, kz)), dma((2, kz)), dma((2, 2, kx)), dma((2, 2, kx)), dma((2,)), dma((2,)),
        dma((1,)), dma((1,)), dma((geo.y,)), dma((geo.y,)), dma((geo.x,)), dma((geo.x,)), dma((geo.z,)), dma((geo.z,)),
        dma((geo.x,)), dma((geo.x,)), dma((geo.y,)), dma((geo.y,)), dma((1,)), dma((1,)),
    ]
    return pl.pallas_call(
        functools.partial(loss_kernel, geo),
        out_shape=(
            jax.ShapeDtypeStruct((ROWS, width), bf16),
            jax.ShapeDtypeStruct((ROWS, width), bf16),
            jax.ShapeDtypeStruct((3, TILES * LANES), f32),
            jax.ShapeDtypeStruct((GRID, GRID, TILES * LANES), bf16),
            jax.ShapeDtypeStruct((KS, KS, TILES * LANES), f32),
        ),
        in_specs=[pl.BlockSpec(memory_space=pltpu.SMEM)] + [pl.BlockSpec(memory_space=pltpu.HBM)] * 7,
        out_specs=[pl.BlockSpec(memory_space=pltpu.VMEM)] * 3 + [pl.BlockSpec(memory_space=pltpu.HBM)] * 2,
        scratch_shapes=scratch,
        compiler_params=pltpu.CompilerParams(
            collective_id=0, has_side_effects=True, vmem_limit_bytes=60 << 20
        ),
    )(scale.reshape(1), image_rows, text_rows, x, g, k, bias, gain)


def hand_out_kernel(*refs):
    count = (len(refs) - 2) // 3
    into, away = refs[-2], refs[-1]
    loads = [pltpu.make_async_copy(refs[i], refs[2 * count + i], into.at[i]) for i in range(count)]
    stores = [pltpu.make_async_copy(refs[2 * count + i], refs[count + i], away.at[i]) for i in range(count)]
    for moving in loads:
        moving.start()
    for load, store in zip(loads, stores):
        load.wait()
        store.start()
    for moving in stores:
        moving.wait()


def hand_out(*arrays):
    held = [pl.BlockSpec(memory_space=pltpu.HBM)] * len(arrays)
    sems = pltpu.SemaphoreType.DMA((len(arrays),))
    return pl.pallas_call(
        hand_out_kernel,
        out_shape=tuple(jax.ShapeDtypeStruct(a.shape, a.dtype) for a in arrays),
        in_specs=held,
        out_specs=held,
        scratch_shapes=[pltpu.VMEM(a.shape, a.dtype) for a in arrays] + [sems, sems],
        compiler_params=pltpu.CompilerParams(vmem_limit_bytes=60 << 20),
    )(*arrays)


def per_device(
    geo, image_embed, text_embed, logit_scale, block_input, dw_kernel, dw_bias, ln_gain, block_grad
):
    image_grad, text_grad, channel_grads, d_input, kernel_grad = hand_out(
        *loss_block(
            geo, logit_scale, image_embed[0], text_embed[0],
            block_input[0], block_grad[0], dw_kernel, dw_bias, ln_gain,
        )
    )
    return (image_grad[None], text_grad[None], d_input[None], kernel_grad, channel_grads)


def solution(mesh, geo=None):
    geo = geo or Geometry(8, 2, 4, 2, 2, 1024)
    placed = (
        P("grp", "blk", None),
        P("grp", "blk", None),
        P(),
        P(("blk", "grp"), None, None, None),
        P(),
        P(),
        P(),
        P(("blk", "grp"), None, None, None),
    )
    return jax.shard_map(
        functools.partial(per_device, geo),
        mesh=mesh,
        in_specs=placed,
        out_specs=(
            P("grp", "blk", None),
            P("grp", "blk", None),
            P(("blk", "grp"), None, None, None),
            P(),
            P(),
        ),
        check_vma=False,
    )
```

```python
import functools
import math

import jax
import jax.numpy as jnp
from jax import lax
from jax.experimental import pallas as pl
from jax.experimental.pallas import tpu as pltpu
from jax.sharding import PartitionSpec as P

GRID = 7
KS = 7
EPS = 1e-06
LANES = 128
TILES = 24
SPOTS = GRID * GRID
HALF = KS // 2


def spot_mean(value, count):
    folded = value[:, 0:8] + value[:, 8:16] + value[:, 16:24]
    folded = jnp.sum(folded, axis=1, keepdims=True)
    return jnp.sum(folded, axis=2, keepdims=True) * (1.0 / count)


def conv_terms(x_ref, g_ref, k_ref, bias_ref, gain_ref, din_ref, terms_ref, xs, gs, ks, cs, ds, bs):
    channels = TILES * LANES

    def spread(src, dst):
        for y in range(GRID):
            for t in range(TILES):
                dst[pl.ds(y * GRID * TILES + t, GRID, stride=TILES), :] = src[
                    y, :, t * LANES : (t + 1) * LANES
                ].astype(jnp.float32)

    spread(x_ref, xs)
    spread(k_ref, ks)
    spread(g_ref, gs)
    bs[0:TILES, :] = bias_ref[...].astype(jnp.float32).reshape(TILES, LANES)
    bs[TILES : 2 * TILES, :] = gain_ref[...].astype(jnp.float32).reshape(TILES, LANES)

    def rows(part, spot):
        return pl.ds(pl.multiple_of(spot * TILES + part * 8, 8), 8)

    def gather(src, part, row):
        return [src[rows(part, row * GRID + x), :] for x in range(GRID)]

    @pl.loop(0, TILES // 8)
    def _(part):
        bias = bs[pl.ds(pl.multiple_of(part * 8, 8), 8), :]
        for y in range(GRID):
            sums = [bias] * GRID
            for a in range(KS):
                if not 0 <= y + a - HALF < GRID:
                    continue
                left = gather(xs, part, y + a - HALF)
                taps = gather(ks, part, a)
                for x in range(GRID):
                    for b in range(KS):
                        if 0 <= x + b - HALF < GRID:
                            sums[x] = sums[x] + left[x + b - HALF] * taps[b]
            for x in range(GRID):
                cs[rows(part, y * GRID + x), :] = sums[x]

    gain = bs[TILES : 2 * TILES, :][None]
    dsum = jnp.zeros((TILES, LANES), jnp.float32)
    nsum = jnp.zeros((TILES, LANES), jnp.float32)
    gsum = jnp.zeros((TILES, LANES), jnp.float32)
    for y in range(GRID):
        span = slice(y * GRID * TILES, (y + 1) * GRID * TILES)
        conv = cs[span, :].reshape(GRID, TILES, LANES)
        grad = gs[span, :].reshape(GRID, TILES, LANES)
        centre = conv - spot_mean(conv, channels)
        d_normed = grad * gain
        inv = lax.rsqrt(spot_mean(centre * centre, channels) + EPS)
        normed = centre * inv
        d_conv = inv * (
            d_normed - spot_mean(d_normed, channels) - normed * spot_mean(d_normed * normed, channels)
        )
        ds[span, :] = d_conv.reshape(GRID * TILES, LANES)
        dsum = dsum + jnp.sum(d_conv, axis=0)
        nsum = nsum + jnp.sum(grad * normed, axis=0)
        gsum = gsum + jnp.sum(grad, axis=0)
    first = SPOTS * TILES
    for index, total in enumerate((dsum, nsum, gsum)):
        terms_ref[first + index * TILES : first + (index + 1) * TILES, :] = total
    first = first + 3 * TILES
    terms_ref[first:SLACK, :] = jnp.zeros((SLACK - first, LANES), jnp.float32)

    @pl.loop(0, TILES // 8)
    def _(part):
        for y in range(GRID):
            sums = [None] * GRID
            for a in range(KS):
                if not 0 <= y - a + HALF < GRID:
                    continue
                left = gather(ds, part, y - a + HALF)
                taps = gather(ks, part, a)
                for x in range(GRID):
                    for b in range(KS):
                        if 0 <= x - b + HALF < GRID:
                            term = left[x - b + HALF] * taps[b]
                            sums[x] = term if sums[x] is None else sums[x] + term
            for x in range(GRID):
                cs[rows(part, y * GRID + x), :] = sums[x]
        for a in range(KS):
            sums = [None] * KS
            for y in range(GRID):
                if not 0 <= y + a - HALF < GRID:
                    continue
                left = gather(ds, part, y)
                right = gather(xs, part, y + a - HALF)
                for b in range(KS):
                    for x in range(GRID):
                        if 0 <= x + b - HALF < GRID:
                            term = left[x] * right[x + b - HALF]
                            sums[b] = term if sums[b] is None else sums[b] + term
            for b in range(KS):
                terms_ref[rows(part, a * KS + b), :] = sums[b]

    for y in range(GRID):
        for t in range(TILES):
            din_ref[y, :, t * LANES : (t + 1) * LANES] = cs[
                pl.ds(y * GRID * TILES + t, GRID, stride=TILES), :
            ].astype(jnp.bfloat16)


ROWS = 128
PART = 64
WIDE = 256
MESH = pl.DeviceIdType.MESH
SLACK = 1280
HIGH_SHIFT = 12.0
LOW_SHIFT = 10.0
LOW_CAP = 30.0
LOW_LIMIT = 55.0


class Geometry:
    def __init__(self, z, y_hi, x, y_lo, core, width):
        self.z, self.y_hi, self.x, self.y_lo, self.core, self.width = z, y_hi, x, y_lo, core, width
        self.sheet = y_hi * x
        self.y = y_hi * y_lo
        self.half = SLACK // core
        self.y_rows = self.half // self.y
        self.x_rows = self.y_rows // x


def dot(left, right, dims=((1,), (0,))):
    return lax.dot_general(left, right, (dims, ((), ())), preferred_element_type=jnp.float32)


def loss_kernel(
    geo, scale_ref, img_hbm, txt_hbm, x_hbm, g_hbm, k_hbm, bias_hbm, gain_hbm,
    ig_ref, tg_ref, cg_ref, din_hbm, kg_hbm,
    din_ref, kg_ref, img_ref, txt_ref, x_ref, g_ref, k_ref, bias_ref, gain_ref, terms_ref, xs, gs, ks, cs, ds, bs, load_sem,
    ia, ta, ui, ut, vi, vt, probs, weights, flip, pick, row_hi, row_lo, alpha, beta, row_raw, col_raw, row_all, col_all, gz, gx,
    zout, zin, xout, xin, yout, yin, l1, hsum, l2, qsum, l3, l4, fin,
    zag_s, zag_r, xag_s, xag_r, yag_s, yag_r, row_s, row_r, col_s, col_r,
    zrs_s, zrs_r, xrs_s, xrs_r, yrs_s, yrs_r,
    s1, r1, s2, r2, s3, r3, s4, r4, s5, r5, s6, r6, s7, r7,
):
    f32, bf16 = jnp.float32, jnp.bfloat16
    nz, nx, sheet = geo.z, geo.x, geo.sheet
    blk, grp = lax.axis_index("blk"), lax.axis_index("grp")
    z, b = blk // sheet, lax.rem(blk, sheet)
    yh, x = b // nx, lax.rem(b, nx)
    yl, core = grp // geo.core, lax.rem(grp, geo.core)
    y = yh * geo.y_lo + yl
    hy = 1 - yh

    def place(z_to, yh_to, x_to):
        return {"blk": z_to * sheet + yh_to * nx + x_to, "grp": grp}

    def column(y_to):
        return {
            "blk": z * sheet + (y_to // geo.y_lo) * nx + x,
            "grp": lax.rem(y_to, geo.y_lo) * geo.core + core,
        }

    def turn(value, by, size):
        return lax.rem(value + by + size, size)

    mate = {"blk": blk, "grp": yl * geo.core + (geo.core - 1 - core)}
    facing = place(z, hy, x)
    sent = []

    def copy(src, dst, send, recv, to):
        return pltpu.make_async_remote_copy(
            src_ref=src, dst_ref=dst, send_sem=send, recv_sem=recv, device_id=to, device_id_type=MESH
        )

    def start(*args):
        moving = copy(*args)
        moving.start()
        sent.append(moving)

    def arrived(dst, send, recv):
        copy(dst, dst, send, recv, facing).wait_recv()

    barrier = pltpu.get_barrier_semaphore()
    peers = [place(turn(z, o, nz), yh, x) for o in (-1, 1)]
    peers += [place(z, yh, turn(x, o, nx)) for o in (-1, 1)]
    peers += [column(turn(y, o, geo.y)) for o in range(1, geo.y)]
    peers.append(mate)
    for peer in peers:
        pl.semaphore_signal(barrier, inc=1, device_id=peer, device_id_type=MESH)
    operands = (txt_hbm, img_hbm, x_hbm, k_hbm, g_hbm, bias_hbm, gain_hbm)
    held = (txt_ref, img_ref, x_ref, k_ref, g_ref, bias_ref, gain_ref)
    loads = [
        pltpu.make_async_copy(src, dst, load_sem.at[i]) for i, (src, dst) in enumerate(zip(operands, held))
    ]
    for load in loads:
        load.start()

    def slot(index, part):
        return pl.ds(pl.multiple_of(index * ROWS + part * PART, PART), PART)

    def full(index):
        return pl.ds(pl.multiple_of(index * ROWS, ROWS), ROWS)

    def unit_rows(raw, unit, inverse, everyone, index):
        values = raw[...].astype(f32)
        inv = lax.rsqrt(jnp.sum(values * values, axis=-1, keepdims=True) + EPS)
        scaled = values * inv
        unit[...] = scaled
        inverse[...] = inv
        everyone[full(index), :] = scaled.astype(bf16)

    row_hi[...] = jnp.zeros_like(row_hi)
    row_lo[...] = jnp.zeros_like(row_lo)
    row_raw[...] = jnp.zeros_like(row_raw)
    col_raw[...] = jnp.zeros_like(col_raw)
    loads[0].wait()
    unit_rows(txt_ref, ut, vt, ta, z)
    loads[1].wait()
    unit_rows(img_ref, ui, vi, ia, b)
    pl.semaphore_wait(barrier, len(peers))

    def sign(d):
        return 1 - 2 * d

    def z_gather(d, k):
        rows = slot(turn(z, -sign(d) * (k // 2), nz), (k % 2) ^ d)
        to = place(turn(z, sign(d), nz), yh, x)
        start(ta.at[rows], ta.at[rows], zag_s.at[d, k], zag_r.at[d, k], to)

    def z_gathered(d, k):
        rows = slot(turn(z, -sign(d) * (k // 2 + 1), nz), (k % 2) ^ d)
        arrived(ta.at[rows], zag_s.at[d, k], zag_r.at[d, k])

    def x_gather(part, d, s, facing_set=False):
        side = hy if facing_set else yh
        rows = slot(side * nx + turn(x, -sign(d) * s, nx), part)
        to = place(z, yh, turn(x, sign(d), nx))
        i = 2 if facing_set else part
        start(ia.at[rows], ia.at[rows], xag_s.at[i, d, s], xag_r.at[i, d, s], to)

    def x_gathered(part, d, s, facing_set=False):
        side = hy if facing_set else yh
        rows = slot(side * nx + turn(x, -sign(d) * (s + 1), nx), part)
        i = 2 if facing_set else part
        arrived(ia.at[rows], xag_s.at[i, d, s], xag_r.at[i, d, s])

    def y_gather(part, j):
        rows = slot(yh * nx + turn(x, j, nx), part)
        i = j + 1 if part else 0
        start(ia.at[rows], ia.at[rows], yag_s.at[i], yag_r.at[i], facing)

    def y_gathered(part, j):
        rows = slot(hy * nx + turn(x, j, nx), part)
        i = j + 1 if part else 0
        arrived(ia.at[rows], yag_s.at[i], yag_r.at[i])

    def share(first, rows):
        return pl.ds(pl.multiple_of(first, 8), rows)

    def mate_send():
        start(terms_ref.at[share((geo.core - 1 - core) * geo.half, geo.half)], l1, s1.at[0], r1.at[0], mate)

    def mate_sum():
        arrived(l1, s1.at[0], r1.at[0])
        hsum[...] = terms_ref[share(core * geo.half, geo.half), :] + l1[...]

    def y_send():
        for o in range(1, geo.y):
            to = turn(y, o, geo.y)
            start(hsum.at[share(to * geo.y_rows, geo.y_rows)], l2.at[o], s2.at[o], r2.at[o], column(to))

    def y_sum():
        total = hsum[share(y * geo.y_rows, geo.y_rows), :]
        for o in range(1, geo.y):
            arrived(l2.at[o], s2.at[o], r2.at[o])
            total = total + l2[o]
        qsum[...] = total

    def x_send():
        for o in range(1, nx):
            to = turn(x, o, nx)
            start(qsum.at[share(to * geo.x_rows, geo.x_rows)], l3.at[o], s3.at[o], r3.at[o], place(z, yh, to))

    def x_sum():
        total = qsum[share(x * geo.x_rows, geo.x_rows), :]
        for o in range(1, nx):
            arrived(l3.at[o], s3.at[o], r3.at[o])
            total = total + l3[o]
        l4[z] = total

    def z_send():
        for o in range(1, nz):
            start(l4.at[z], l4.at[z], s4.at[o], r4.at[o], place(turn(z, o, nz), yh, x))

    mine = core * geo.half + y * geo.y_rows + x * geo.x_rows

    def z_sum():
        for o in range(1, nz):
            arrived(l4.at[turn(z, -o, nz)], s4.at[o], r4.at[o])
        total = l4[0]
        for o in range(1, nz):
            total = total + l4[o]
        fin[share(mine, geo.x_rows), :] = total * (1.0 / (geo.z * geo.sheet * geo.y_lo * geo.core))

    def x_spread():
        rows = fin.at[share(mine, geo.x_rows)]
        for o in range(1, nx):
            start(rows, rows, s5.at[o], r5.at[o], place(z, yh, turn(x, o, nx)))

    def x_spread_done():
        for o in range(1, nx):
            first = core * geo.half + y * geo.y_rows + turn(x, -o, nx) * geo.x_rows
            arrived(fin.at[share(first, geo.x_rows)], s5.at[o], r5.at[o])

    def y_spread():
        rows = fin.at[share(core * geo.half + y * geo.y_rows, geo.y_rows)]
        for o in range(1, geo.y):
            start(rows, rows, s6.at[o], r6.at[o], column(turn(y, o, geo.y)))

    def y_spread_done():
        for o in range(1, geo.y):
            first = core * geo.half + turn(y, -o, geo.y) * geo.y_rows
            arrived(fin.at[share(first, geo.y_rows)], s6.at[o], r6.at[o])

    def mate_spread():
        rows = fin.at[share(core * geo.half, geo.half)]
        start(rows, rows, s7.at[0], r7.at[0], mate)

    def mate_spread_done():
        arrived(fin.at[share((geo.core - 1 - core) * geo.half, geo.half)], s7.at[0], r7.at[0])

    power = scale_ref[0] * (0.5 / math.log(2.0))
    late = turn(z, nz // 2, nz)

    def logits_block(tile, width, first, count, unroll=1):
        lanes = pl.ds(pl.multiple_of(tile * ROWS, ROWS), width)

        def rows_step(m, sums):
            rows = pl.ds(pl.multiple_of((first + m) * WIDE, WIDE), WIDE)
            logits = dot(ia[rows, :], ta[lanes, :], ((1,), (1,)))
            root = jnp.exp2(logits * power)
            probs[rows, lanes] = root
            high = root * math.exp(-HIGH_SHIFT)
            high = high * high
            low = jnp.minimum(root * math.exp(LOW_SHIFT), math.exp(LOW_CAP))
            low = low * low
            row_hi[rows, :] += sum(high[:, j : j + ROWS] for j in range(0, width, ROWS))
            row_lo[rows, :] += sum(low[:, j : j + ROWS] for j in range(0, width, ROWS))
            return (
                sums[0] + jnp.sum(high.reshape(WIDE // 8, 8, width), axis=0),
                sums[1] + jnp.sum(low.reshape(WIDE // 8, 8, width), axis=0),
            )

        zero = jnp.zeros((8, width), f32)
        high, low = lax.fori_loop(0, count, rows_step, (zero, zero), unroll=unroll)
        high = jnp.sum(high, axis=0, keepdims=True)
        low = jnp.sum(low, axis=0, keepdims=True)
        for j in range(width // ROWS):
            col_raw[pl.ds(tile + j, 1), :] += high[:, j * ROWS : (j + 1) * ROWS]
            col_raw[pl.ds(8 + tile + j, 1), :] += low[:, j * ROWS : (j + 1) * ROWS]

    def local_lse(total):
        high, low = total[0:8], total[8:16]
        small = low < math.exp(LOW_LIMIT)
        return jnp.where(small, jnp.log(low) - 2 * LOW_SHIFT, jnp.log(high) + 2 * HIGH_SHIFT)

    def half_factor(parts, count):
        peak = parts[0]
        for o in range(1, count):
            peak = jnp.maximum(peak, parts[o])
        total = jnp.exp(parts[0] - peak)
        for o in range(1, count):
            total = total + jnp.exp(parts[o] - peak)
        return jnp.exp((peak + jnp.log(total)) * -0.5) * math.sqrt(0.5)

    def weigh(tile):
        lanes = pl.ds(pl.multiple_of(tile * ROWS, ROWS), ROWS)

        def rows_step(m, carry):
            rows = pl.ds(pl.multiple_of(m * WIDE, WIDE), WIDE)
            root = probs[rows, lanes]
            by_row = root * alpha[rows, :]
            by_col = root * beta[pl.ds(tile, 1), :]
            weights[rows, lanes] = (by_row * by_row + by_col * by_col).astype(bf16)
            return carry

        lax.fori_loop(0, sheet * ROWS // WIDE, rows_step, 0)

    def text_part(*shifts):
        for i, j in enumerate(shifts):
            flip[i * ROWS : (i + 1) * ROWS, :] = weights[:, full(turn(z, j, nz))].T
        for n in range(0, geo.width, WIDE):
            part = dot(flip[: len(shifts) * ROWS, :], ia[:, n : n + WIDE])
            for i, j in enumerate(shifts):
                gz[j, :, n : n + WIDE] = part[i * ROWS : (i + 1) * ROWS]

    def image_part(*shifts):
        for i, (q, j) in enumerate(shifts):
            pick[i * ROWS : (i + 1) * ROWS, :] = weights[full((yh if q else hy) * nx + turn(x, j, nx)), :]
        for n in range(0, geo.width, WIDE):
            part = dot(pick[: len(shifts) * ROWS, :], ta[:, n : n + WIDE])
            for i, (q, j) in enumerate(shifts):
                gx[q * nx + j, :, n : n + WIDE] = part[i * ROWS : (i + 1) * ROWS]

    def ring_rows(d, k):
        part = (k % 2) ^ d
        return slice(part * PART, (part + 1) * PART)

    def ring_target(d, k, size):
        away = size // 2 - (k + 1) // 2
        return (sign(d) * away) % size

    def z_reduce(d, k):
        value = gz[ring_target(d, k, nz), ring_rows(d, k), :]
        if k >= 2:
            arrived(zin.at[d, k - 2], zrs_s.at[d, k - 2], zrs_r.at[d, k - 2])
            value = value + zin[d, k - 2].astype(f32)
        zout[d, k] = value.astype(bf16)
        to = place(turn(z, sign(d), nz), yh, x)
        start(zout.at[d, k], zin.at[d, k], zrs_s.at[d, k], zrs_r.at[d, k], to)

    def x_reduce(q, d, k):
        value = gx[q * nx + ring_target(d, k, nx), ring_rows(d, k), :]
        if k >= 2:
            arrived(xin.at[q, d, k - 2], xrs_s.at[q, d, k - 2], xrs_r.at[q, d, k - 2])
            value = value + xin[q, d, k - 2].astype(f32)
        xout[q, d, k] = value.astype(bf16)
        to = place(z, yh, turn(x, sign(d), nx))
        start(xout.at[q, d, k], xin.at[q, d, k], xrs_s.at[q, d, k], xrs_r.at[q, d, k], to)

    def ring_last(size):
        return [k for k in (size - 3, size - 2) if k >= 0]

    def x_total(q, c):
        value = gx[q * nx, c * PART : (c + 1) * PART, :]
        for d in range(2):
            for k in ring_last(nx):
                if (k % 2) ^ d == c:
                    arrived(xin.at[q, d, k], xrs_s.at[q, d, k], xrs_r.at[q, d, k])
                    value = value + xin[q, d, k].astype(f32)
        return value

    def z_total(c):
        value = gz[0, c * PART : (c + 1) * PART, :]
        for d in range(2):
            for k in ring_last(nz):
                if (k % 2) ^ d == c:
                    arrived(zin.at[d, k], zrs_s.at[d, k], zrs_r.at[d, k])
                    value = value + zin[d, k].astype(f32)
        return value

    def finish(total, other, unit, inverse, out, c):
        rows = slice(c * PART, (c + 1) * PART)
        grad = scale_ref[0] * (total - other.astype(f32))
        along = jnp.sum(grad * unit[rows, :], axis=-1, keepdims=True)
        out[rows, :] = (inverse[rows, :] * (grad - along * unit[rows, :])).astype(bf16)

    both = range(2)
    kz, kx = nz - 1, nx - 1
    for k in range(min(2, kz)):
        for d in both:
            z_gather(d, k)
    for part in (1, 0):
        for d in both:
            x_gather(part, d, 0)
    y_gather(0, 0)
    y_gather(1, 0)
    for load in loads[2:]:
        load.wait()
    conv_terms(x_ref, g_ref, k_ref, bias_ref, gain_ref, din_ref, terms_ref, xs, gs, ks, cs, ds, bs)
    din_out = pltpu.make_async_copy(din_ref, din_hbm, load_sem.at[len(loads)])
    din_out.start()
    mate_send()

    def z_step(k):
        if k < kz:
            for d in both:
                z_gathered(d, k)
            if k + 2 < kz:
                for d in both:
                    z_gather(d, k + 2)

    z_step(0)
    for d in both:
        x_gathered(1, d, 0)
    x_gather(1, 1, 1)
    y_gather(1, nx - 1)
    y_gather(1, 1)
    y_gathered(0, 0)
    for d in both:
        x_gather(0, d, 0, True)
    for d in both:
        x_gathered(0, d, 0)
    x_gather(0, 0, 1)
    z_step(1)
    mate_sum()
    y_send()
    x_gathered(1, 1, 1)
    y_gather(1, 2)
    pairs = nz * ROWS // WIDE
    count = nx * ROWS // WIDE
    lean = 2 * lax.rem(z, 2) - 1
    near = 2 * (z // 2)
    next_pair = 2 * turn(z // 2, lean, pairs)
    far_pair = 2 * turn(z // 2, -lean, pairs)
    ours, theirs = yh * count, hy * count
    z_step(2)
    for d in both:
        x_gathered(0, d, 0, True)
    x_gather(0, 0, 1, True)
    x_gathered(0, 0, 1)
    logits_block(near, WIDE, ours, count)
    z_step(3)
    logits_block(next_pair, WIDE, ours, count)
    for j in (0, nx - 1, 1):
        y_gathered(1, j)
    x_gathered(0, 0, 1, True)
    z_step(4)
    y_sum()
    x_send()
    y_gathered(1, 2)
    logits_block(near, WIDE, theirs, count)
    logits_block(next_pair, WIDE, theirs, count)
    for k in range(5, kz - 1):
        z_step(k)
    x_sum()
    logits_block(far_pair, WIDE, 0, 2 * count)
    logits_block(late + 1 - 2 * lax.rem(late, 2), ROWS, 0, 2 * count)
    z_step(kz - 1)
    logits_block(late, ROWS, 0, 2 * count, True)
    for m in range(sheet):
        rows = slice(m * ROWS, (m + 1) * ROWS)
        row_raw[m : m + 1, :] = jnp.sum(row_hi[rows, :].T, axis=0, keepdims=True)
        row_raw[8 + m : 9 + m, :] = jnp.sum(row_lo[rows, :].T, axis=0, keepdims=True)
    row_all[b] = local_lse(row_raw[...])
    col_all[z] = local_lse(col_raw[...])
    for q in both:
        for o in range(nx):
            if q or o:
                i = q * nx + o
                to = place(z, hy if q else yh, turn(x, o, nx))
                start(row_all.at[b], row_all.at[b], row_s.at[i], row_r.at[i], to)
    for o in range(1, nz):
        start(col_all.at[z], col_all.at[z], col_s.at[o], col_r.at[o], place(turn(z, o, nz), yh, x))
    z_send()
    for o in range(1, nz):
        arrived(col_all.at[turn(z, -o, nz)], col_s.at[o], col_r.at[o])
    beta[...] = half_factor(col_all, nz)
    for q in both:
        for o in range(nx):
            if q or o:
                i = q * nx + o
                arrived(row_all.at[(hy if q else yh) * nx + turn(x, -o, nx)], row_s.at[i], row_r.at[i])
    factor = half_factor(row_all, sheet)
    for m in range(sheet):
        rows = slice(m * ROWS, (m + 1) * ROWS)
        alpha[rows, :] = jnp.broadcast_to(factor[m : m + 1, :], (ROWS, ROWS)).T

    def z_stage(k):
        if k < kz:
            for d in both:
                z_reduce(d, k)

    def x_stage(q, k):
        if k < kx:
            for d in both:
                x_reduce(q, d, k)

    half = nz // 2
    weigh(turn(z, half, nz))
    text_part(half)
    z_stage(0)

    @pl.loop(0, nz - 1)
    def _(i):
        weigh(turn(z, i - (half - 1), nz))

    image_part((0, 2))
    x_stage(0, 0)
    text_part(half - 1, nz - half + 1)
    z_stage(1)
    image_part((0, 1), (0, 3))
    x_stage(0, 1)
    z_sum()
    x_spread()
    image_part((1, 2), (0, 0))
    z_stage(2)
    x_stage(0, 2)
    x_stage(1, 0)
    image_part((1, 1), (1, 3))
    x_stage(1, 1)
    text_part(half - 2, nz - half + 2)
    z_stage(3)
    x_spread_done()
    y_spread()
    z_stage(4)
    for c in both:
        yout[c] = x_total(0, c).astype(bf16)
        start(yout.at[c], yin.at[c], yrs_s.at[c], yrs_r.at[c], facing)
    text_part(half - 3, nz - half + 3)
    z_stage(5)
    x_stage(1, 2)
    y_spread_done()
    mate_spread()
    z_stage(6)
    image_part((1, 0))
    text_part(0)
    mate_spread_done()
    for row in range(KS):
        for t in range(TILES):
            kg_ref[row, :, t * LANES : (t + 1) * LANES] = fin[
                pl.ds(row * KS * TILES + t, KS, stride=TILES), :
            ]
    for t in range(TILES):
        cg_ref[:, t * LANES : (t + 1) * LANES] = fin[pl.ds(SPOTS * TILES + t, 3, stride=TILES), :]
    kg_out = pltpu.make_async_copy(kg_ref, kg_hbm, load_sem.at[len(loads) + 1])
    kg_out.start()
    for c in both:
        value = x_total(1, c)
        arrived(yin.at[c], yrs_s.at[c], yrs_r.at[c])
        finish(value + yin[c].astype(f32), ta[slot(z, c), :], ui, vi, ig_ref, c)
    for c in both:
        finish(z_total(c), ia[slot(b, c), :], ut, vt, tg_ref, c)
    din_out.wait()
    kg_out.wait()
    for moving in sent:
        moving.wait_send()


def loss_block(geo, scale, image_rows, text_rows, x, g, k, bias, gain):
    f32, bf16 = jnp.float32, jnp.bfloat16
    vmem = pltpu.VMEM
    dma = pltpu.SemaphoreType.DMA
    images, texts, width = geo.sheet * ROWS, geo.z * ROWS, geo.width
    kz, kx = geo.z - 1, geo.x - 1
    big = vmem((SPOTS * TILES, LANES), f32)
    maps = vmem((GRID, GRID, TILES * LANES), bf16)
    scratch = [
        maps, vmem((KS, KS, TILES * LANES), f32), vmem((ROWS, width), bf16), vmem((ROWS, width), bf16), maps, maps, maps,
        vmem((TILES * LANES,), bf16), vmem((TILES * LANES,), bf16), vmem((SLACK, LANES), f32),
        big, big, big, big, big, vmem((2 * TILES, LANES), f32), dma((9,)),
        vmem((images, width), bf16), vmem((texts, width), bf16),
        vmem((ROWS, width), f32), vmem((ROWS, width), f32), vmem((ROWS, 1), f32), vmem((ROWS, 1), f32),
        vmem((images, texts), f32), vmem((images, texts), bf16), vmem((2 * ROWS, images), bf16), vmem((2 * ROWS, texts), bf16),
        vmem((images, ROWS), f32), vmem((images, ROWS), f32), vmem((images, ROWS), f32), vmem((8, ROWS), f32),
        vmem((16, ROWS), f32), vmem((16, ROWS), f32),
        vmem((geo.sheet, 8, ROWS), f32), vmem((geo.z, 8, ROWS), f32),
        vmem((geo.z, ROWS, width), f32), vmem((2 * geo.x, ROWS, width), f32),
        vmem((2, kz, PART, width), bf16), vmem((2, kz, PART, width), bf16),
        vmem((2, 2, kx, PART, width), bf16), vmem((2, 2, kx, PART, width), bf16),
        vmem((2, PART, width), bf16), vmem((2, PART, width), bf16),
        vmem((geo.half, LANES), f32), vmem((geo.half, LANES), f32),
        vmem((geo.y, geo.y_rows, LANES), f32), vmem((geo.y_rows, LANES), f32),
        vmem((geo.x, geo.x_rows, LANES), f32), vmem((geo.z, geo.x_rows, LANES), f32), vmem((SLACK, LANES), f32),
        dma((2, kz)), dma((2, kz)), dma((3, 2, 2)), dma((3, 2, 2)), dma((1 + geo.x,)), dma((1 + geo.x,)),
        dma((geo.sheet,)), dma((geo.sheet,)), dma((geo.z,)), dma((geo.z,)),
        dma((2, kz)), dma((2, kz)), dma((2, 2, kx)), dma((2, 2, kx)), dma((2,)), dma((2,)),
        dma((1,)), dma((1,)), dma((geo.y,)), dma((geo.y,)), dma((geo.x,)), dma((geo.x,)), dma((geo.z,)), dma((geo.z,)),
        dma((geo.x,)), dma((geo.x,)), dma((geo.y,)), dma((geo.y,)), dma((1,)), dma((1,)),
    ]
    return pl.pallas_call(
        functools.partial(loss_kernel, geo),
        out_shape=(
            jax.ShapeDtypeStruct((ROWS, width), bf16),
            jax.ShapeDtypeStruct((ROWS, width), bf16),
            jax.ShapeDtypeStruct((3, TILES * LANES), f32),
            jax.ShapeDtypeStruct((GRID, GRID, TILES * LANES), bf16),
            jax.ShapeDtypeStruct((KS, KS, TILES * LANES), f32),
        ),
        in_specs=[pl.BlockSpec(memory_space=pltpu.SMEM)] + [pl.BlockSpec(memory_space=pltpu.HBM)] * 7,
        out_specs=[pl.BlockSpec(memory_space=pltpu.VMEM)] * 3 + [pl.BlockSpec(memory_space=pltpu.HBM)] * 2,
        scratch_shapes=scratch,
        compiler_params=pltpu.CompilerParams(
            collective_id=0, has_side_effects=True, vmem_limit_bytes=60 << 20
        ),
    )(scale.reshape(1), image_rows, text_rows, x, g, k, bias, gain)


def hand_out_kernel(*refs):
    count = (len(refs) - 2) // 3
    into, away = refs[-2], refs[-1]
    loads = [pltpu.make_async_copy(refs[i], refs[2 * count + i], into.at[i]) for i in range(count)]
    stores = [pltpu.make_async_copy(refs[2 * count + i], refs[count + i], away.at[i]) for i in range(count)]
    for moving in loads:
        moving.start()
    for load, store in zip(loads, stores):
        load.wait()
        store.start()
    for moving in stores:
        moving.wait()


def hand_out(*arrays):
    held = [pl.BlockSpec(memory_space=pltpu.HBM)] * len(arrays)
    sems = pltpu.SemaphoreType.DMA((len(arrays),))
    return pl.pallas_call(
        hand_out_kernel,
        out_shape=tuple(jax.ShapeDtypeStruct(a.shape, a.dtype) for a in arrays),
        in_specs=held,
        out_specs=held,
        scratch_shapes=[pltpu.VMEM(a.shape, a.dtype) for a in arrays] + [sems, sems],
        compiler_params=pltpu.CompilerParams(vmem_limit_bytes=60 << 20),
    )(*arrays)


def per_device(
    geo, image_embed, text_embed, logit_scale, block_input, dw_kernel, dw_bias, ln_gain, block_grad
):
    image_grad, text_grad, channel_grads, d_input, kernel_grad = hand_out(
        *loss_block(
            geo, logit_scale, image_embed[0], text_embed[0],
            block_input[0], block_grad[0], dw_kernel, dw_bias, ln_gain,
        )
    )
    return (image_grad[None], text_grad[None], d_input[None], kernel_grad, channel_grads)


def solution(mesh, geo=None):
    geo = geo or Geometry(8, 2, 4, 2, 2, 1024)
    placed = (
        P("grp", "blk", None),
        P("grp", "blk", None),
        P(),
        P(("blk", "grp"), None, None, None),
        P(),
        P(),
        P(),
        P(("blk", "grp"), None, None, None),
    )
    return jax.shard_map(
        functools.partial(per_device, geo),
        mesh=mesh,
        in_specs=placed,
        out_specs=(
            P("grp", "blk", None),
            P("grp", "blk", None),
            P(("blk", "grp"), None, None, None),
            P(),
            P(),
        ),
        check_vma=False,
    )
```

```python
import functools
import math

import jax
import jax.numpy as jnp
from jax import lax
from jax.experimental import pallas as pl
from jax.experimental.pallas import tpu as pltpu
from jax.sharding import PartitionSpec as P

GRID = 7
KS = 7
EPS = 1e-06
LANES = 128
TILES = 24
SPOTS = GRID * GRID
HALF = KS // 2


def spot_mean(value, count):
    folded = value[:, 0:8] + value[:, 8:16] + value[:, 16:24]
    folded = jnp.sum(folded, axis=1, keepdims=True)
    return jnp.sum(folded, axis=2, keepdims=True) * (1.0 / count)


def conv_terms(x_ref, g_ref, k_ref, bias_ref, gain_ref, din_ref, terms_ref, xs, gs, ks, cs, ds, bs):
    channels = TILES * LANES

    def spread(src, dst):
        for y in range(GRID):
            for t in range(TILES):
                dst[pl.ds(y * GRID * TILES + t, GRID, stride=TILES), :] = src[
                    y, :, t * LANES : (t + 1) * LANES
                ].astype(jnp.float32)

    spread(x_ref, xs)
    spread(k_ref, ks)
    spread(g_ref, gs)
    bs[0:TILES, :] = bias_ref[...].astype(jnp.float32).reshape(TILES, LANES)
    bs[TILES : 2 * TILES, :] = gain_ref[...].astype(jnp.float32).reshape(TILES, LANES)

    def rows(part, spot):
        return pl.ds(pl.multiple_of(spot * TILES + part * 8, 8), 8)

    def gather(src, part, row):
        return [src[rows(part, row * GRID + x), :] for x in range(GRID)]

    @pl.loop(0, TILES // 8)
    def _(part):
        bias = bs[pl.ds(pl.multiple_of(part * 8, 8), 8), :]
        for y in range(GRID):
            sums = [bias] * GRID
            for a in range(KS):
                if not 0 <= y + a - HALF < GRID:
                    continue
                left = gather(xs, part, y + a - HALF)
                taps = gather(ks, part, a)
                for x in range(GRID):
                    for b in range(KS):
                        if 0 <= x + b - HALF < GRID:
                            sums[x] = sums[x] + left[x + b - HALF] * taps[b]
            for x in range(GRID):
                cs[rows(part, y * GRID + x), :] = sums[x]

    gain = bs[TILES : 2 * TILES, :][None]
    dsum = jnp.zeros((TILES, LANES), jnp.float32)
    nsum = jnp.zeros((TILES, LANES), jnp.float32)
    gsum = jnp.zeros((TILES, LANES), jnp.float32)
    for y in range(GRID):
        span = slice(y * GRID * TILES, (y + 1) * GRID * TILES)
        conv = cs[span, :].reshape(GRID, TILES, LANES)
        grad = gs[span, :].reshape(GRID, TILES, LANES)
        centre = conv - spot_mean(conv, channels)
        d_normed = grad * gain
        inv = lax.rsqrt(spot_mean(centre * centre, channels) + EPS)
        normed = centre * inv
        d_conv = inv * (
            d_normed - spot_mean(d_normed, channels) - normed * spot_mean(d_normed * normed, channels)
        )
        ds[span, :] = d_conv.reshape(GRID * TILES, LANES)
        dsum = dsum + jnp.sum(d_conv, axis=0)
        nsum = nsum + jnp.sum(grad * normed, axis=0)
        gsum = gsum + jnp.sum(grad, axis=0)
    first = SPOTS * TILES
    for index, total in enumerate((dsum, nsum, gsum)):
        terms_ref[first + index * TILES : first + (index + 1) * TILES, :] = total
    first = first + 3 * TILES
    terms_ref[first:SLACK, :] = jnp.zeros((SLACK - first, LANES), jnp.float32)

    @pl.loop(0, TILES // 8)
    def _(part):
        for y in range(GRID):
            sums = [None] * GRID
            for a in range(KS):
                if not 0 <= y - a + HALF < GRID:
                    continue
                left = gather(ds, part, y - a + HALF)
                taps = gather(ks, part, a)
                for x in range(GRID):
                    for b in range(KS):
                        if 0 <= x - b + HALF < GRID:
                            term = left[x - b + HALF] * taps[b]
                            sums[x] = term if sums[x] is None else sums[x] + term
            for x in range(GRID):
                cs[rows(part, y * GRID + x), :] = sums[x]
        for a in range(KS):
            sums = [None] * KS
            for y in range(GRID):
                if not 0 <= y + a - HALF < GRID:
                    continue
                left = gather(ds, part, y)
                right = gather(xs, part, y + a - HALF)
                for b in range(KS):
                    for x in range(GRID):
                        if 0 <= x + b - HALF < GRID:
                            term = left[x] * right[x + b - HALF]
                            sums[b] = term if sums[b] is None else sums[b] + term
            for b in range(KS):
                terms_ref[rows(part, a * KS + b), :] = sums[b]

    for y in range(GRID):
        for t in range(TILES):
            din_ref[y, :, t * LANES : (t + 1) * LANES] = cs[
                pl.ds(y * GRID * TILES + t, GRID, stride=TILES), :
            ].astype(jnp.bfloat16)


ROWS = 128
PART = 64
WIDE = 256
MESH = pl.DeviceIdType.MESH
SLACK = 1280
HIGH_SHIFT = 12.0
LOW_SHIFT = 10.0
LOW_CAP = 30.0
LOW_LIMIT = 55.0


class Geometry:
    def __init__(self, z, y_hi, x, y_lo, core, width):
        self.z, self.y_hi, self.x, self.y_lo, self.core, self.width = z, y_hi, x, y_lo, core, width
        self.sheet = y_hi * x
        self.y = y_hi * y_lo
        self.half = SLACK // core
        self.y_rows = self.half // self.y
        self.x_rows = self.y_rows // x


def dot(left, right, dims=((1,), (0,))):
    return lax.dot_general(left, right, (dims, ((), ())), preferred_element_type=jnp.float32)


def loss_kernel(
    geo, scale_ref, img_hbm, txt_hbm, x_hbm, g_hbm, k_hbm, bias_hbm, gain_hbm,
    ig_ref, tg_ref, cg_ref, din_hbm, kg_hbm,
    din_ref, kg_ref, img_ref, txt_ref, x_ref, g_ref, k_ref, bias_ref, gain_ref, terms_ref, xs, gs, ks, cs, ds, bs, load_sem,
    ia, ta, ui, ut, vi, vt, probs, weights, flip, pick, row_hi, row_lo, alpha, beta, row_raw, col_raw, row_all, col_all, gz, gx,
    zout, zin, xout, xin, yout, yin, l1, hsum, l2, qsum, l3, l4, fin,
    zag_s, zag_r, xag_s, xag_r, yag_s, yag_r, row_s, row_r, col_s, col_r,
    zrs_s, zrs_r, xrs_s, xrs_r, yrs_s, yrs_r,
    s1, r1, s2, r2, s3, r3, s4, r4, s5, r5, s6, r6, s7, r7,
):
    f32, bf16 = jnp.float32, jnp.bfloat16
    nz, nx, sheet = geo.z, geo.x, geo.sheet
    blk, grp = lax.axis_index("blk"), lax.axis_index("grp")
    z, b = blk // sheet, lax.rem(blk, sheet)
    yh, x = b // nx, lax.rem(b, nx)
    yl, core = grp // geo.core, lax.rem(grp, geo.core)
    y = yh * geo.y_lo + yl
    hy = 1 - yh

    def place(z_to, yh_to, x_to):
        return {"blk": z_to * sheet + yh_to * nx + x_to, "grp": grp}

    def column(y_to):
        return {
            "blk": z * sheet + (y_to // geo.y_lo) * nx + x,
            "grp": lax.rem(y_to, geo.y_lo) * geo.core + core,
        }

    def turn(value, by, size):
        return lax.rem(value + by + size, size)

    mate = {"blk": blk, "grp": yl * geo.core + (geo.core - 1 - core)}
    facing = place(z, hy, x)
    sent = []

    def copy(src, dst, send, recv, to):
        return pltpu.make_async_remote_copy(
            src_ref=src, dst_ref=dst, send_sem=send, recv_sem=recv, device_id=to, device_id_type=MESH
        )

    def start(*args):
        moving = copy(*args)
        moving.start()
        sent.append(moving)

    def arrived(dst, send, recv):
        copy(dst, dst, send, recv, facing).wait_recv()

    barrier = pltpu.get_barrier_semaphore()
    peers = [place(turn(z, o, nz), yh, x) for o in (-1, 1)]
    peers += [place(z, yh, turn(x, o, nx)) for o in (-1, 1)]
    peers += [column(turn(y, o, geo.y)) for o in range(1, geo.y)]
    peers.append(mate)
    for peer in peers:
        pl.semaphore_signal(barrier, inc=1, device_id=peer, device_id_type=MESH)
    operands = (txt_hbm, img_hbm, x_hbm, k_hbm, g_hbm, bias_hbm, gain_hbm)
    held = (txt_ref, img_ref, x_ref, k_ref, g_ref, bias_ref, gain_ref)
    loads = [
        pltpu.make_async_copy(src, dst, load_sem.at[i]) for i, (src, dst) in enumerate(zip(operands, held))
    ]
    for load in loads:
        load.start()

    def slot(index, part):
        return pl.ds(pl.multiple_of(index * ROWS + part * PART, PART), PART)

    def full(index):
        return pl.ds(pl.multiple_of(index * ROWS, ROWS), ROWS)

    def unit_rows(raw, unit, inverse, everyone, index):
        values = raw[...].astype(f32)
        inv = lax.rsqrt(jnp.sum(values * values, axis=-1, keepdims=True) + EPS)
        scaled = values * inv
        unit[...] = scaled
        inverse[...] = inv
        everyone[full(index), :] = scaled.astype(bf16)

    row_hi[...] = jnp.zeros_like(row_hi)
    row_lo[...] = jnp.zeros_like(row_lo)
    row_raw[...] = jnp.zeros_like(row_raw)
    col_raw[...] = jnp.zeros_like(col_raw)
    loads[0].wait()
    unit_rows(txt_ref, ut, vt, ta, z)
    loads[1].wait()
    unit_rows(img_ref, ui, vi, ia, b)
    pl.semaphore_wait(barrier, len(peers))

    def sign(d):
        return 1 - 2 * d

    def z_gather(d, k):
        rows = slot(turn(z, -sign(d) * (k // 2), nz), (k % 2) ^ d)
        to = place(turn(z, sign(d), nz), yh, x)
        start(ta.at[rows], ta.at[rows], zag_s.at[d, k], zag_r.at[d, k], to)

    def z_gathered(d, k):
        rows = slot(turn(z, -sign(d) * (k // 2 + 1), nz), (k % 2) ^ d)
        arrived(ta.at[rows], zag_s.at[d, k], zag_r.at[d, k])

    def x_gather(part, d, s, facing_set=False):
        side = hy if facing_set else yh
        rows = slot(side * nx + turn(x, -sign(d) * s, nx), part)
        to = place(z, yh, turn(x, sign(d), nx))
        i = 2 if facing_set else part
        start(ia.at[rows], ia.at[rows], xag_s.at[i, d, s], xag_r.at[i, d, s], to)

    def x_gathered(part, d, s, facing_set=False):
        side = hy if facing_set else yh
        rows = slot(side * nx + turn(x, -sign(d) * (s + 1), nx), part)
        i = 2 if facing_set else part
        arrived(ia.at[rows], xag_s.at[i, d, s], xag_r.at[i, d, s])

    def y_gather(part, j):
        rows = slot(yh * nx + turn(x, j, nx), part)
        i = j + 1 if part else 0
        start(ia.at[rows], ia.at[rows], yag_s.at[i], yag_r.at[i], facing)

    def y_gathered(part, j):
        rows = slot(hy * nx + turn(x, j, nx), part)
        i = j + 1 if part else 0
        arrived(ia.at[rows], yag_s.at[i], yag_r.at[i])

    def share(first, rows):
        return pl.ds(pl.multiple_of(first, 8), rows)

    def mate_send():
        start(terms_ref.at[share((geo.core - 1 - core) * geo.half, geo.half)], l1, s1.at[0], r1.at[0], mate)

    def mate_sum():
        arrived(l1, s1.at[0], r1.at[0])
        hsum[...] = terms_ref[share(core * geo.half, geo.half), :] + l1[...]

    def y_send():
        for o in range(1, geo.y):
            to = turn(y, o, geo.y)
            start(hsum.at[share(to * geo.y_rows, geo.y_rows)], l2.at[o], s2.at[o], r2.at[o], column(to))

    def y_sum():
        total = hsum[share(y * geo.y_rows, geo.y_rows), :]
        for o in range(1, geo.y):
            arrived(l2.at[o], s2.at[o], r2.at[o])
            total = total + l2[o]
        qsum[...] = total

    def x_send():
        for o in range(1, nx):
            to = turn(x, o, nx)
            start(qsum.at[share(to * geo.x_rows, geo.x_rows)], l3.at[o], s3.at[o], r3.at[o], place(z, yh, to))

    def x_sum():
        total = qsum[share(x * geo.x_rows, geo.x_rows), :]
        for o in range(1, nx):
            arrived(l3.at[o], s3.at[o], r3.at[o])
            total = total + l3[o]
        l4[z] = total

    def z_send():
        for o in range(1, nz):
            start(l4.at[z], l4.at[z], s4.at[o], r4.at[o], place(turn(z, o, nz), yh, x))

    mine = core * geo.half + y * geo.y_rows + x * geo.x_rows

    def z_sum():
        for o in range(1, nz):
            arrived(l4.at[turn(z, -o, nz)], s4.at[o], r4.at[o])
        total = l4[0]
        for o in range(1, nz):
            total = total + l4[o]
        fin[share(mine, geo.x_rows), :] = total * (1.0 / (geo.z * geo.sheet * geo.y_lo * geo.core))

    def x_spread():
        rows = fin.at[share(mine, geo.x_rows)]
        for o in range(1, nx):
            start(rows, rows, s5.at[o], r5.at[o], place(z, yh, turn(x, o, nx)))

    def x_spread_done():
        for o in range(1, nx):
            first = core * geo.half + y * geo.y_rows + turn(x, -o, nx) * geo.x_rows
            arrived(fin.at[share(first, geo.x_rows)], s5.at[o], r5.at[o])

    def y_spread():
        rows = fin.at[share(core * geo.half + y * geo.y_rows, geo.y_rows)]
        for o in range(1, geo.y):
            start(rows, rows, s6.at[o], r6.at[o], column(turn(y, o, geo.y)))

    def y_spread_done():
        for o in range(1, geo.y):
            first = core * geo.half + turn(y, -o, geo.y) * geo.y_rows
            arrived(fin.at[share(first, geo.y_rows)], s6.at[o], r6.at[o])

    def mate_spread():
        rows = fin.at[share(core * geo.half, geo.half)]
        start(rows, rows, s7.at[0], r7.at[0], mate)

    def mate_spread_done():
        arrived(fin.at[share((geo.core - 1 - core) * geo.half, geo.half)], s7.at[0], r7.at[0])

    power = scale_ref[0] * (0.5 / math.log(2.0))
    late = turn(z, nz // 2, nz)

    def logits_block(tile, width, first, count, unroll=1):
        lanes = pl.ds(pl.multiple_of(tile * ROWS, ROWS), width)

        def rows_step(m, sums):
            rows = pl.ds(pl.multiple_of((first + m) * WIDE, WIDE), WIDE)
            logits = dot(ia[rows, :], ta[lanes, :], ((1,), (1,)))
            root = jnp.exp2(logits * power)
            probs[rows, lanes] = root
            high = root * math.exp(-HIGH_SHIFT)
            high = high * high
            low = jnp.minimum(root * math.exp(LOW_SHIFT), math.exp(LOW_CAP))
            low = low * low
            row_hi[rows, :] += sum(high[:, j : j + ROWS] for j in range(0, width, ROWS))
            row_lo[rows, :] += sum(low[:, j : j + ROWS] for j in range(0, width, ROWS))
            return (
                sums[0] + jnp.sum(high.reshape(WIDE // 8, 8, width), axis=0),
                sums[1] + jnp.sum(low.reshape(WIDE // 8, 8, width), axis=0),
            )

        zero = jnp.zeros((8, width), f32)
        high, low = lax.fori_loop(0, count, rows_step, (zero, zero), unroll=unroll)
        high = jnp.sum(high, axis=0, keepdims=True)
        low = jnp.sum(low, axis=0, keepdims=True)
        for j in range(width // ROWS):
            col_raw[pl.ds(tile + j, 1), :] += high[:, j * ROWS : (j + 1) * ROWS]
            col_raw[pl.ds(8 + tile + j, 1), :] += low[:, j * ROWS : (j + 1) * ROWS]

    def local_lse(total):
        high, low = total[0:8], total[8:16]
        small = low < math.exp(LOW_LIMIT)
        return jnp.where(small, jnp.log(low) - 2 * LOW_SHIFT, jnp.log(high) + 2 * HIGH_SHIFT)

    def half_factor(parts, count):
        peak = parts[0]
        for o in range(1, count):
            peak = jnp.maximum(peak, parts[o])
        total = jnp.exp(parts[0] - peak)
        for o in range(1, count):
            total = total + jnp.exp(parts[o] - peak)
        return jnp.exp((peak + jnp.log(total)) * -0.5) * math.sqrt(0.5)

    def weigh(tile):
        lanes = pl.ds(pl.multiple_of(tile * ROWS, ROWS), ROWS)

        def rows_step(m, carry):
            rows = pl.ds(pl.multiple_of(m * WIDE, WIDE), WIDE)
            root = probs[rows, lanes]
            by_row = root * alpha[rows, :]
            by_col = root * beta[pl.ds(tile, 1), :]
            weights[rows, lanes] = (by_row * by_row + by_col * by_col).astype(bf16)
            return carry

        lax.fori_loop(0, sheet * ROWS // WIDE, rows_step, 0)

    def text_part(*shifts):
        for i, j in enumerate(shifts):
            flip[i * ROWS : (i + 1) * ROWS, :] = weights[:, full(turn(z, j, nz))].T
        for n in range(0, geo.width, WIDE):
            part = dot(flip[: len(shifts) * ROWS, :], ia[:, n : n + WIDE])
            for i, j in enumerate(shifts):
                gz[j, :, n : n + WIDE] = part[i * ROWS : (i + 1) * ROWS]

    def image_part(*shifts):
        for i, (q, j) in enumerate(shifts):
            pick[i * ROWS : (i + 1) * ROWS, :] = weights[full((yh if q else hy) * nx + turn(x, j, nx)), :]
        for n in range(0, geo.width, WIDE):
            part = dot(pick[: len(shifts) * ROWS, :], ta[:, n : n + WIDE])
            for i, (q, j) in enumerate(shifts):
                gx[q * nx + j, :, n : n + WIDE] = part[i * ROWS : (i + 1) * ROWS]

    def ring_rows(d, k):
        part = (k % 2) ^ d
        return slice(part * PART, (part + 1) * PART)

    def ring_target(d, k, size):
        away = size // 2 - (k + 1) // 2
        return (sign(d) * away) % size

    def z_reduce(d, k):
        value = gz[ring_target(d, k, nz), ring_rows(d, k), :]
        if k >= 2:
            arrived(zin.at[d, k - 2], zrs_s.at[d, k - 2], zrs_r.at[d, k - 2])
            value = value + zin[d, k - 2].astype(f32)
        zout[d, k] = value.astype(bf16)
        to = place(turn(z, sign(d), nz), yh, x)
        start(zout.at[d, k], zin.at[d, k], zrs_s.at[d, k], zrs_r.at[d, k], to)

    def y_early(j):
        yout[1 + j] = gx[j, PART:, :].astype(bf16)
        start(yout.at[1 + j], yin.at[1 + j], yrs_s.at[1 + j], yrs_r.at[1 + j], facing)

    def y_arrived(i):
        arrived(yin.at[i], yrs_s.at[i], yrs_r.at[i])
        return yin[i].astype(f32)

    def x_reduce(q, d, k):
        target = ring_target(d, k, nx)
        value = gx[q * nx + target, ring_rows(d, k), :]
        if (k % 2) ^ d == 1:
            value = value + y_arrived(1 + target)
        if k >= 2:
            arrived(xin.at[q, d, k - 2], xrs_s.at[q, d, k - 2], xrs_r.at[q, d, k - 2])
            value = value + xin[q, d, k - 2].astype(f32)
        xout[q, d, k] = value.astype(bf16)
        to = place(z, yh, turn(x, sign(d), nx))
        start(xout.at[q, d, k], xin.at[q, d, k], xrs_s.at[q, d, k], xrs_r.at[q, d, k], to)

    def ring_last(size):
        return [k for k in (size - 3, size - 2) if k >= 0]

    def x_total(q, c):
        value = gx[q * nx, c * PART : (c + 1) * PART, :]
        for d in range(2):
            for k in ring_last(nx):
                if (k % 2) ^ d == c:
                    arrived(xin.at[q, d, k], xrs_s.at[q, d, k], xrs_r.at[q, d, k])
                    value = value + xin[q, d, k].astype(f32)
        return value

    def z_total(c):
        value = gz[0, c * PART : (c + 1) * PART, :]
        for d in range(2):
            for k in ring_last(nz):
                if (k % 2) ^ d == c:
                    arrived(zin.at[d, k], zrs_s.at[d, k], zrs_r.at[d, k])
                    value = value + zin[d, k].astype(f32)
        return value

    def finish(total, other, unit, inverse, out, c):
        rows = slice(c * PART, (c + 1) * PART)
        grad = scale_ref[0] * (total - other.astype(f32))
        along = jnp.sum(grad * unit[rows, :], axis=-1, keepdims=True)
        out[rows, :] = (inverse[rows, :] * (grad - along * unit[rows, :])).astype(bf16)

    both = range(2)
    kz, kx = nz - 1, nx - 1
    for k in range(min(2, kz)):
        for d in both:
            z_gather(d, k)
    for part in (1, 0):
        for d in both:
            x_gather(part, d, 0)
    y_gather(0, 0)
    y_gather(1, 0)
    for load in loads[2:]:
        load.wait()
    conv_terms(x_ref, g_ref, k_ref, bias_ref, gain_ref, din_ref, terms_ref, xs, gs, ks, cs, ds, bs)
    din_out = pltpu.make_async_copy(din_ref, din_hbm, load_sem.at[len(loads)])
    din_out.start()
    mate_send()

    def z_step(k):
        if k < kz:
            for d in both:
                z_gathered(d, k)
            if k + 2 < kz:
                for d in both:
                    z_gather(d, k + 2)

    z_step(0)
    for d in both:
        x_gathered(1, d, 0)
    x_gather(1, 1, 1)
    y_gather(1, nx - 1)
    y_gather(1, 1)
    y_gathered(0, 0)
    for d in both:
        x_gather(0, d, 0, True)
    for d in both:
        x_gathered(0, d, 0)
    x_gather(0, 0, 1)
    z_step(1)
    mate_sum()
    y_send()
    x_gathered(1, 1, 1)
    y_gather(1, 2)
    pairs = nz * ROWS // WIDE
    count = nx * ROWS // WIDE
    lean = 2 * lax.rem(z, 2) - 1
    near = 2 * (z // 2)
    next_pair = 2 * turn(z // 2, lean, pairs)
    far_pair = 2 * turn(z // 2, -lean, pairs)
    ours, theirs = yh * count, hy * count
    z_step(2)
    for d in both:
        x_gathered(0, d, 0, True)
    x_gather(0, 0, 1, True)
    x_gathered(0, 0, 1)
    logits_block(near, WIDE, ours, count)
    z_step(3)
    logits_block(next_pair, WIDE, ours, count)
    for j in (0, nx - 1, 1):
        y_gathered(1, j)
    x_gathered(0, 0, 1, True)
    z_step(4)
    y_sum()
    x_send()
    y_gathered(1, 2)
    logits_block(near, WIDE, theirs, count)
    logits_block(next_pair, WIDE, theirs, count)
    for k in range(5, kz - 1):
        z_step(k)
    x_sum()
    logits_block(far_pair, WIDE, 0, 2 * count)
    logits_block(late + 1 - 2 * lax.rem(late, 2), ROWS, 0, 2 * count)
    z_step(kz - 1)
    logits_block(late, ROWS, 0, 2 * count, True)
    for m in range(sheet):
        rows = slice(m * ROWS, (m + 1) * ROWS)
        row_raw[m : m + 1, :] = jnp.sum(row_hi[rows, :].T, axis=0, keepdims=True)
        row_raw[8 + m : 9 + m, :] = jnp.sum(row_lo[rows, :].T, axis=0, keepdims=True)
    row_all[b] = local_lse(row_raw[...])
    col_all[z] = local_lse(col_raw[...])
    for q in both:
        for o in range(nx):
            if q or o:
                i = q * nx + o
                to = place(z, hy if q else yh, turn(x, o, nx))
                start(row_all.at[b], row_all.at[b], row_s.at[i], row_r.at[i], to)
    for o in range(1, nz):
        start(col_all.at[z], col_all.at[z], col_s.at[o], col_r.at[o], place(turn(z, o, nz), yh, x))
    z_send()
    for o in range(1, nz):
        arrived(col_all.at[turn(z, -o, nz)], col_s.at[o], col_r.at[o])
    beta[...] = half_factor(col_all, nz)
    for q in both:
        for o in range(nx):
            if q or o:
                i = q * nx + o
                arrived(row_all.at[(hy if q else yh) * nx + turn(x, -o, nx)], row_s.at[i], row_r.at[i])
    factor = half_factor(row_all, sheet)
    for m in range(sheet):
        rows = slice(m * ROWS, (m + 1) * ROWS)
        alpha[rows, :] = jnp.broadcast_to(factor[m : m + 1, :], (ROWS, ROWS)).T

    def z_stage(k):
        if k < kz:
            for d in both:
                z_reduce(d, k)

    half = nz // 2
    weigh(turn(z, half, nz))
    text_part(half)
    z_stage(0)

    @pl.loop(0, nz - 1)
    def _(i):
        weigh(turn(z, i - (half - 1), nz))

    image_part((0, 2), (0, 3))
    x_reduce(0, 0, 0)
    x_reduce(0, 1, 1)
    y_early(2)
    y_early(3)
    text_part(half - 1, nz - half + 1)
    z_stage(1)
    z_sum()
    x_spread()
    image_part((0, 1), (0, 0))
    y_early(1)
    image_part((1, 2), (1, 3))
    x_reduce(1, 0, 0)
    x_reduce(1, 1, 1)
    z_stage(2)
    x_reduce(0, 0, 2)
    image_part((1, 1), (1, 0))
    x_spread_done()
    y_spread()
    x_reduce(1, 1, 0)
    text_part(half - 2, nz - half + 2)
    z_stage(3)
    x_reduce(1, 0, 2)
    z_stage(4)
    x_reduce(1, 0, 1)
    yout[0] = x_total(0, 0).astype(bf16)
    start(yout.at[0], yin.at[0], yrs_s.at[0], yrs_r.at[0], facing)
    y_early(0)
    text_part(half - 3, nz - half + 3)
    z_stage(5)
    x_reduce(1, 1, 2)
    y_spread_done()
    mate_spread()
    z_stage(6)
    text_part(0)
    mate_spread_done()
    for row in range(KS):
        for t in range(TILES):
            kg_ref[row, :, t * LANES : (t + 1) * LANES] = fin[
                pl.ds(row * KS * TILES + t, KS, stride=TILES), :
            ]
    for t in range(TILES):
        cg_ref[:, t * LANES : (t + 1) * LANES] = fin[pl.ds(SPOTS * TILES + t, 3, stride=TILES), :]
    kg_out = pltpu.make_async_copy(kg_ref, kg_hbm, load_sem.at[len(loads) + 1])
    kg_out.start()
    for c in both:
        value = x_total(1, c) + y_arrived(c)
        finish(value, ta[slot(z, c), :], ui, vi, ig_ref, c)
    for c in both:
        finish(z_total(c), ia[slot(b, c), :], ut, vt, tg_ref, c)
    din_out.wait()
    kg_out.wait()
    for moving in sent:
        moving.wait_send()


def loss_block(geo, scale, image_rows, text_rows, x, g, k, bias, gain):
    f32, bf16 = jnp.float32, jnp.bfloat16
    vmem = pltpu.VMEM
    dma = pltpu.SemaphoreType.DMA
    images, texts, width = geo.sheet * ROWS, geo.z * ROWS, geo.width
    kz, kx = geo.z - 1, geo.x - 1
    big = vmem((SPOTS * TILES + TILES, LANES), f32)
    maps = vmem((GRID, GRID, TILES * LANES), bf16)
    scratch = [
        maps, vmem((KS, KS, TILES * LANES), f32), vmem((ROWS, width), bf16), vmem((ROWS, width), bf16), maps, maps, maps,
        vmem((TILES * LANES,), bf16), vmem((TILES * LANES,), bf16), vmem((SLACK, LANES), f32),
        big, big, big, big, big, vmem((2 * TILES, LANES), f32), dma((9,)),
        vmem((images, width), bf16), vmem((texts, width), bf16),
        vmem((ROWS, width), f32), vmem((ROWS, width), f32), vmem((ROWS, 1), f32), vmem((ROWS, 1), f32),
        vmem((images, texts), f32), vmem((images, texts), bf16), vmem((2 * ROWS, images), bf16), vmem((2 * ROWS, texts), bf16),
        vmem((images, ROWS), f32), vmem((images, ROWS), f32), vmem((images, ROWS), f32), vmem((8, ROWS), f32),
        vmem((16, ROWS), f32), vmem((16, ROWS), f32),
        vmem((geo.sheet, 8, ROWS), f32), vmem((geo.z, 8, ROWS), f32),
        vmem((geo.z, ROWS, width), f32), vmem((2 * geo.x, ROWS, width), f32),
        vmem((2, kz, PART, width), bf16), vmem((2, kz, PART, width), bf16),
        vmem((2, 2, kx, PART, width), bf16), vmem((2, 2, kx, PART, width), bf16),
        vmem((1 + geo.x, PART, width), bf16), vmem((1 + geo.x, PART, width), bf16),
        vmem((geo.half, LANES), f32), vmem((geo.half, LANES), f32),
        vmem((geo.y, geo.y_rows, LANES), f32), vmem((geo.y_rows, LANES), f32),
        vmem((geo.x, geo.x_rows, LANES), f32), vmem((geo.z, geo.x_rows, LANES), f32), vmem((SLACK, LANES), f32),
        dma((2, kz)), dma((2, kz)), dma((3, 2, 2)), dma((3, 2, 2)), dma((1 + geo.x,)), dma((1 + geo.x,)),
        dma((geo.sheet,)), dma((geo.sheet,)), dma((geo.z,)), dma((geo.z,)),
        dma((2, kz)), dma((2, kz)), dma((2, 2, kx)), dma((2, 2, kx)), dma((1 + geo.x,)), dma((1 + geo.x,)),
        dma((1,)), dma((1,)), dma((geo.y,)), dma((geo.y,)), dma((geo.x,)), dma((geo.x,)), dma((geo.z,)), dma((geo.z,)),
        dma((geo.x,)), dma((geo.x,)), dma((geo.y,)), dma((geo.y,)), dma((1,)), dma((1,)),
    ]
    return pl.pallas_call(
        functools.partial(loss_kernel, geo),
        out_shape=(
            jax.ShapeDtypeStruct((ROWS, width), bf16),
            jax.ShapeDtypeStruct((ROWS, width), bf16),
            jax.ShapeDtypeStruct((3, TILES * LANES), f32),
            jax.ShapeDtypeStruct((GRID, GRID, TILES * LANES), bf16),
            jax.ShapeDtypeStruct((KS, KS, TILES * LANES), f32),
        ),
        in_specs=[pl.BlockSpec(memory_space=pltpu.SMEM)] + [pl.BlockSpec(memory_space=pltpu.HBM)] * 7,
        out_specs=[pl.BlockSpec(memory_space=pltpu.VMEM)] * 3 + [pl.BlockSpec(memory_space=pltpu.HBM)] * 2,
        scratch_shapes=scratch,
        compiler_params=pltpu.CompilerParams(
            collective_id=0, has_side_effects=True, vmem_limit_bytes=60 << 20
        ),
    )(scale.reshape(1), image_rows, text_rows, x, g, k, bias, gain)


def hand_out_kernel(*refs):
    count = (len(refs) - 2) // 3
    into, away = refs[-2], refs[-1]
    loads = [pltpu.make_async_copy(refs[i], refs[2 * count + i], into.at[i]) for i in range(count)]
    stores = [pltpu.make_async_copy(refs[2 * count + i], refs[count + i], away.at[i]) for i in range(count)]
    for moving in loads:
        moving.start()
    for load, store in zip(loads, stores):
        load.wait()
        store.start()
    for moving in stores:
        moving.wait()


def hand_out(*arrays):
    held = [pl.BlockSpec(memory_space=pltpu.HBM)] * len(arrays)
    sems = pltpu.SemaphoreType.DMA((len(arrays),))
    return pl.pallas_call(
        hand_out_kernel,
        out_shape=tuple(jax.ShapeDtypeStruct(a.shape, a.dtype) for a in arrays),
        in_specs=held,
        out_specs=held,
        scratch_shapes=[pltpu.VMEM(a.shape, a.dtype) for a in arrays] + [sems, sems],
        compiler_params=pltpu.CompilerParams(vmem_limit_bytes=60 << 20),
    )(*arrays)


def per_device(
    geo, image_embed, text_embed, logit_scale, block_input, dw_kernel, dw_bias, ln_gain, block_grad
):
    image_grad, text_grad, channel_grads, d_input, kernel_grad = hand_out(
        *loss_block(
            geo, logit_scale, image_embed[0], text_embed[0],
            block_input[0], block_grad[0], dw_kernel, dw_bias, ln_gain,
        )
    )
    return (image_grad[None], text_grad[None], d_input[None], kernel_grad, channel_grads)


def solution(mesh, geo=None):
    geo = geo or Geometry(8, 2, 4, 2, 2, 1024)
    placed = (
        P("grp", "blk", None),
        P("grp", "blk", None),
        P(),
        P(("blk", "grp"), None, None, None),
        P(),
        P(),
        P(),
        P(("blk", "grp"), None, None, None),
    )
    return jax.shard_map(
        functools.partial(per_device, geo),
        mesh=mesh,
        in_specs=placed,
        out_specs=(
            P("grp", "blk", None),
            P("grp", "blk", None),
            P(("blk", "grp"), None, None, None),
            P(),
            P(),
        ),
        check_vma=False,
    )
```

```python
import functools
import math

import jax
import jax.numpy as jnp
from jax import lax
from jax.experimental import pallas as pl
from jax.experimental.pallas import tpu as pltpu
from jax.sharding import PartitionSpec as P

GRID = 7
KS = 7
EPS = 1e-06
LANES = 128
TILES = 24
SPOTS = GRID * GRID
HALF = KS // 2


def spot_mean(value, count):
    folded = value[:, 0:8] + value[:, 8:16] + value[:, 16:24]
    folded = jnp.sum(folded, axis=1, keepdims=True)
    return jnp.sum(folded, axis=2, keepdims=True) * (1.0 / count)


def conv_terms(x_ref, g_ref, k_ref, bias_ref, gain_ref, din_ref, terms_ref, xs, gs, ks, cs, ds, bs):
    channels = TILES * LANES

    def spread(src, dst):
        for y in range(GRID):
            for t in range(TILES):
                dst[pl.ds(y * GRID * TILES + t, GRID, stride=TILES), :] = src[
                    y, :, t * LANES : (t + 1) * LANES
                ].astype(jnp.float32)

    spread(x_ref, xs)
    spread(k_ref, ks)
    spread(g_ref, gs)
    bs[0:TILES, :] = bias_ref[...].astype(jnp.float32).reshape(TILES, LANES)
    bs[TILES : 2 * TILES, :] = gain_ref[...].astype(jnp.float32).reshape(TILES, LANES)

    def rows(part, spot):
        return pl.ds(pl.multiple_of(spot * TILES + part * 8, 8), 8)

    def gather(src, part, row):
        return [src[rows(part, row * GRID + x), :] for x in range(GRID)]

    @pl.loop(0, TILES // 8)
    def _(part):
        bias = bs[pl.ds(pl.multiple_of(part * 8, 8), 8), :]
        for y in range(GRID):
            sums = [bias] * GRID
            for a in range(KS):
                if not 0 <= y + a - HALF < GRID:
                    continue
                left = gather(xs, part, y + a - HALF)
                taps = gather(ks, part, a)
                for x in range(GRID):
                    for b in range(KS):
                        if 0 <= x + b - HALF < GRID:
                            sums[x] = sums[x] + left[x + b - HALF] * taps[b]
            for x in range(GRID):
                cs[rows(part, y * GRID + x), :] = sums[x]

    gain = bs[TILES : 2 * TILES, :][None]
    dsum = jnp.zeros((TILES, LANES), jnp.float32)
    nsum = jnp.zeros((TILES, LANES), jnp.float32)
    gsum = jnp.zeros((TILES, LANES), jnp.float32)
    for y in range(GRID):
        span = slice(y * GRID * TILES, (y + 1) * GRID * TILES)
        conv = cs[span, :].reshape(GRID, TILES, LANES)
        grad = gs[span, :].reshape(GRID, TILES, LANES)
        centre = conv - spot_mean(conv, channels)
        d_normed = grad * gain
        inv = lax.rsqrt(spot_mean(centre * centre, channels) + EPS)
        normed = centre * inv
        d_conv = inv * (
            d_normed - spot_mean(d_normed, channels) - normed * spot_mean(d_normed * normed, channels)
        )
        ds[span, :] = d_conv.reshape(GRID * TILES, LANES)
        dsum = dsum + jnp.sum(d_conv, axis=0)
        nsum = nsum + jnp.sum(grad * normed, axis=0)
        gsum = gsum + jnp.sum(grad, axis=0)
    first = SPOTS * TILES
    for index, total in enumerate((dsum, nsum, gsum)):
        terms_ref[first + index * TILES : first + (index + 1) * TILES, :] = total
    first = first + 3 * TILES
    terms_ref[first:SLACK, :] = jnp.zeros((SLACK - first, LANES), jnp.float32)

    @pl.loop(0, TILES // 8)
    def _(part):
        for y in range(GRID):
            sums = [None] * GRID
            for a in range(KS):
                if not 0 <= y - a + HALF < GRID:
                    continue
                left = gather(ds, part, y - a + HALF)
                taps = gather(ks, part, a)
                for x in range(GRID):
                    for b in range(KS):
                        if 0 <= x - b + HALF < GRID:
                            term = left[x - b + HALF] * taps[b]
                            sums[x] = term if sums[x] is None else sums[x] + term
            for x in range(GRID):
                cs[rows(part, y * GRID + x), :] = sums[x]
        for a in range(KS):
            sums = [None] * KS
            for y in range(GRID):
                if not 0 <= y + a - HALF < GRID:
                    continue
                left = gather(ds, part, y)
                right = gather(xs, part, y + a - HALF)
                for b in range(KS):
                    for x in range(GRID):
                        if 0 <= x + b - HALF < GRID:
                            term = left[x] * right[x + b - HALF]
                            sums[b] = term if sums[b] is None else sums[b] + term
            for b in range(KS):
                terms_ref[rows(part, a * KS + b), :] = sums[b]

    for y in range(GRID):
        for t in range(TILES):
            din_ref[y, :, t * LANES : (t + 1) * LANES] = cs[
                pl.ds(y * GRID * TILES + t, GRID, stride=TILES), :
            ].astype(jnp.bfloat16)


ROWS = 128
PART = 64
WIDE = 256
MESH = pl.DeviceIdType.MESH
SLACK = 1280
HIGH_SHIFT = 12.0
LOW_SHIFT = 10.0
LOW_CAP = 30.0
LOW_LIMIT = 55.0


class Geometry:
    def __init__(self, z, y_hi, x, y_lo, core, width):
        self.z, self.y_hi, self.x, self.y_lo, self.core, self.width = z, y_hi, x, y_lo, core, width
        self.sheet = y_hi * x
        self.y = y_hi * y_lo
        self.half = SLACK // core
        self.y_rows = self.half // self.y
        self.x_rows = self.y_rows // x


def dot(left, right, dims=((1,), (0,))):
    return lax.dot_general(left, right, (dims, ((), ())), preferred_element_type=jnp.float32)


def loss_kernel(
    geo, scale_ref, img_hbm, txt_hbm, x_hbm, g_hbm, k_hbm, bias_hbm, gain_hbm,
    ig_hbm, tg_hbm, cg_hbm, din_hbm, kg_hbm, ig_ref, tg_ref, cg_ref,
    din_ref, kg_ref, img_ref, txt_ref, x_ref, g_ref, k_ref, bias_ref, gain_ref, terms_ref, xs, gs, ks, cs, ds, bs, load_sem,
    ia, ta, ui, ut, vi, vt, probs, weights, flip, pick, row_hi, row_lo, alpha, beta, row_raw, col_raw, row_all, col_all, gz, gx,
    zout, zin, xout, xin, yout, yin, l1, hsum, l2, qsum, l3, l4, fin,
    zag_s, zag_r, xag_s, xag_r, yag_s, yag_r, row_s, row_r, col_s, col_r,
    zrs_s, zrs_r, xrs_s, xrs_r, yrs_s, yrs_r,
    s1, r1, s2, r2, s3, r3, s4, r4, s5, r5, s6, r6, s7, r7,
):
    f32, bf16 = jnp.float32, jnp.bfloat16
    nz, nx, sheet = geo.z, geo.x, geo.sheet
    blk, grp = lax.axis_index("blk"), lax.axis_index("grp")
    z, b = blk // sheet, lax.rem(blk, sheet)
    yh, x = b // nx, lax.rem(b, nx)
    yl, core = grp // geo.core, lax.rem(grp, geo.core)
    y = yh * geo.y_lo + yl
    hy = 1 - yh

    def place(z_to, yh_to, x_to):
        return {"blk": z_to * sheet + yh_to * nx + x_to, "grp": grp}

    def column(y_to):
        return {
            "blk": z * sheet + (y_to // geo.y_lo) * nx + x,
            "grp": lax.rem(y_to, geo.y_lo) * geo.core + core,
        }

    def turn(value, by, size):
        return lax.rem(value + by + size, size)

    mate = {"blk": blk, "grp": yl * geo.core + (geo.core - 1 - core)}
    facing = place(z, hy, x)
    sent = []

    def copy(src, dst, send, recv, to):
        return pltpu.make_async_remote_copy(
            src_ref=src, dst_ref=dst, send_sem=send, recv_sem=recv, device_id=to, device_id_type=MESH
        )

    def start(*args):
        moving = copy(*args)
        moving.start()
        sent.append(moving)

    def arrived(dst, send, recv):
        copy(dst, dst, send, recv, facing).wait_recv()

    barrier = pltpu.get_barrier_semaphore()
    peers = [place(turn(z, o, nz), yh, x) for o in (-1, 1)]
    peers += [place(z, yh, turn(x, o, nx)) for o in (-1, 1)]
    peers += [column(turn(y, o, geo.y)) for o in range(1, geo.y)]
    peers.append(mate)
    for peer in peers:
        pl.semaphore_signal(barrier, inc=1, device_id=peer, device_id_type=MESH)
    operands = (txt_hbm, img_hbm, x_hbm, k_hbm, g_hbm, bias_hbm, gain_hbm)
    held = (txt_ref, img_ref, x_ref, k_ref, g_ref, bias_ref, gain_ref)
    loads = [
        pltpu.make_async_copy(src, dst, load_sem.at[i]) for i, (src, dst) in enumerate(zip(operands, held))
    ]
    for load in loads:
        load.start()

    def slot(index, part):
        return pl.ds(pl.multiple_of(index * ROWS + part * PART, PART), PART)

    def full(index):
        return pl.ds(pl.multiple_of(index * ROWS, ROWS), ROWS)

    def unit_rows(raw, unit, inverse, everyone, index):
        values = raw[...].astype(f32)
        inv = lax.rsqrt(jnp.sum(values * values, axis=-1, keepdims=True) + EPS)
        scaled = values * inv
        unit[...] = scaled
        inverse[...] = inv
        everyone[full(index), :] = scaled.astype(bf16)

    row_hi[...] = jnp.zeros_like(row_hi)
    row_lo[...] = jnp.zeros_like(row_lo)
    row_raw[...] = jnp.zeros_like(row_raw)
    col_raw[...] = jnp.zeros_like(col_raw)
    loads[0].wait()
    unit_rows(txt_ref, ut, vt, ta, z)
    loads[1].wait()
    unit_rows(img_ref, ui, vi, ia, b)
    pl.semaphore_wait(barrier, len(peers))

    def sign(d):
        return 1 - 2 * d

    def z_gather(d, k):
        rows = slot(turn(z, -sign(d) * (k // 2), nz), (k % 2) ^ d)
        to = place(turn(z, sign(d), nz), yh, x)
        start(ta.at[rows], ta.at[rows], zag_s.at[d, k], zag_r.at[d, k], to)

    def z_gathered(d, k):
        rows = slot(turn(z, -sign(d) * (k // 2 + 1), nz), (k % 2) ^ d)
        arrived(ta.at[rows], zag_s.at[d, k], zag_r.at[d, k])

    def x_gather(part, d, s, facing_set=False):
        side = hy if facing_set else yh
        rows = slot(side * nx + turn(x, -sign(d) * s, nx), part)
        to = place(z, yh, turn(x, sign(d), nx))
        i = 2 if facing_set else part
        start(ia.at[rows], ia.at[rows], xag_s.at[i, d, s], xag_r.at[i, d, s], to)

    def x_gathered(part, d, s, facing_set=False):
        side = hy if facing_set else yh
        rows = slot(side * nx + turn(x, -sign(d) * (s + 1), nx), part)
        i = 2 if facing_set else part
        arrived(ia.at[rows], xag_s.at[i, d, s], xag_r.at[i, d, s])

    def y_gather(part, j):
        rows = slot(yh * nx + turn(x, j, nx), part)
        i = j + 1 if part else 0
        start(ia.at[rows], ia.at[rows], yag_s.at[i], yag_r.at[i], facing)

    def y_gathered(part, j):
        rows = slot(hy * nx + turn(x, j, nx), part)
        i = j + 1 if part else 0
        arrived(ia.at[rows], yag_s.at[i], yag_r.at[i])

    def share(first, rows):
        return pl.ds(pl.multiple_of(first, 8), rows)

    def mate_send():
        start(terms_ref.at[share((geo.core - 1 - core) * geo.half, geo.half)], l1, s1.at[0], r1.at[0], mate)

    def mate_sum():
        arrived(l1, s1.at[0], r1.at[0])
        hsum[...] = terms_ref[share(core * geo.half, geo.half), :] + l1[...]

    def y_send():
        for o in range(1, geo.y):
            to = turn(y, o, geo.y)
            start(hsum.at[share(to * geo.y_rows, geo.y_rows)], l2.at[o], s2.at[o], r2.at[o], column(to))

    def y_sum():
        total = hsum[share(y * geo.y_rows, geo.y_rows), :]
        for o in range(1, geo.y):
            arrived(l2.at[o], s2.at[o], r2.at[o])
            total = total + l2[o]
        qsum[...] = total

    def x_send():
        for o in range(1, nx):
            to = turn(x, o, nx)
            start(qsum.at[share(to * geo.x_rows, geo.x_rows)], l3.at[o], s3.at[o], r3.at[o], place(z, yh, to))

    def x_sum():
        total = qsum[share(x * geo.x_rows, geo.x_rows), :]
        for o in range(1, nx):
            arrived(l3.at[o], s3.at[o], r3.at[o])
            total = total + l3[o]
        l4[z] = total

    def z_send():
        for o in range(1, nz):
            start(l4.at[z], l4.at[z], s4.at[o], r4.at[o], place(turn(z, o, nz), yh, x))

    mine = core * geo.half + y * geo.y_rows + x * geo.x_rows

    def z_sum():
        for o in range(1, nz):
            arrived(l4.at[turn(z, -o, nz)], s4.at[o], r4.at[o])
        total = l4[0]
        for o in range(1, nz):
            total = total + l4[o]
        fin[share(mine, geo.x_rows), :] = total * (1.0 / (geo.z * geo.sheet * geo.y_lo * geo.core))

    def x_spread():
        rows = fin.at[share(mine, geo.x_rows)]
        for o in range(1, nx):
            start(rows, rows, s5.at[o], r5.at[o], place(z, yh, turn(x, o, nx)))

    def x_spread_done():
        for o in range(1, nx):
            first = core * geo.half + y * geo.y_rows + turn(x, -o, nx) * geo.x_rows
            arrived(fin.at[share(first, geo.x_rows)], s5.at[o], r5.at[o])

    def y_spread():
        rows = fin.at[share(core * geo.half + y * geo.y_rows, geo.y_rows)]
        for o in range(1, geo.y):
            start(rows, rows, s6.at[o], r6.at[o], column(turn(y, o, geo.y)))

    def y_spread_done():
        for o in range(1, geo.y):
            first = core * geo.half + turn(y, -o, geo.y) * geo.y_rows
            arrived(fin.at[share(first, geo.y_rows)], s6.at[o], r6.at[o])

    def mate_spread():
        rows = fin.at[share(core * geo.half, geo.half)]
        start(rows, rows, s7.at[0], r7.at[0], mate)

    def mate_spread_done():
        arrived(fin.at[share((geo.core - 1 - core) * geo.half, geo.half)], s7.at[0], r7.at[0])

    power = scale_ref[0] * (0.5 / math.log(2.0))
    late = turn(z, nz // 2, nz)

    def logits_block(tile, width, first, count, unroll=1):
        lanes = pl.ds(pl.multiple_of(tile * ROWS, ROWS), width)

        def rows_step(m, sums):
            rows = pl.ds(pl.multiple_of((first + m) * WIDE, WIDE), WIDE)
            logits = dot(ia[rows, :], ta[lanes, :], ((1,), (1,)))
            root = jnp.exp2(logits * power)
            probs[rows, lanes] = root
            high = root * math.exp(-HIGH_SHIFT)
            high = high * high
            low = jnp.minimum(root * math.exp(LOW_SHIFT), math.exp(LOW_CAP))
            low = low * low
            row_hi[rows, :] += sum(high[:, j : j + ROWS] for j in range(0, width, ROWS))
            row_lo[rows, :] += sum(low[:, j : j + ROWS] for j in range(0, width, ROWS))
            return (
                sums[0] + jnp.sum(high.reshape(WIDE // 8, 8, width), axis=0),
                sums[1] + jnp.sum(low.reshape(WIDE // 8, 8, width), axis=0),
            )

        zero = jnp.zeros((8, width), f32)
        high, low = lax.fori_loop(0, count, rows_step, (zero, zero), unroll=unroll)
        high = jnp.sum(high, axis=0, keepdims=True)
        low = jnp.sum(low, axis=0, keepdims=True)
        for j in range(width // ROWS):
            col_raw[pl.ds(tile + j, 1), :] += high[:, j * ROWS : (j + 1) * ROWS]
            col_raw[pl.ds(8 + tile + j, 1), :] += low[:, j * ROWS : (j + 1) * ROWS]

    def local_lse(total):
        high, low = total[0:8], total[8:16]
        small = low < math.exp(LOW_LIMIT)
        return jnp.where(small, jnp.log(low) - 2 * LOW_SHIFT, jnp.log(high) + 2 * HIGH_SHIFT)

    def half_factor(parts, count):
        peak = parts[0]
        for o in range(1, count):
            peak = jnp.maximum(peak, parts[o])
        total = jnp.exp(parts[0] - peak)
        for o in range(1, count):
            total = total + jnp.exp(parts[o] - peak)
        return jnp.exp((peak + jnp.log(total)) * -0.5) * math.sqrt(0.5)

    def weigh(tile):
        lanes = pl.ds(pl.multiple_of(tile * ROWS, ROWS), ROWS)

        def rows_step(m, carry):
            rows = pl.ds(pl.multiple_of(m * WIDE, WIDE), WIDE)
            root = probs[rows, lanes]
            by_row = root * alpha[rows, :]
            by_col = root * beta[pl.ds(tile, 1), :]
            weights[rows, lanes] = (by_row * by_row + by_col * by_col).astype(bf16)
            return carry

        lax.fori_loop(0, sheet * ROWS // WIDE, rows_step, 0)

    def text_part(*shifts):
        for i, j in enumerate(shifts):
            flip[i * ROWS : (i + 1) * ROWS, :] = weights[:, full(turn(z, j, nz))].T
        for n in range(0, geo.width, WIDE):
            part = dot(flip[: len(shifts) * ROWS, :], ia[:, n : n + WIDE])
            for i, j in enumerate(shifts):
                gz[j, :, n : n + WIDE] = part[i * ROWS : (i + 1) * ROWS]

    def image_part(*shifts):
        for i, (q, j) in enumerate(shifts):
            pick[i * ROWS : (i + 1) * ROWS, :] = weights[full((yh if q else hy) * nx + turn(x, j, nx)), :]
        for n in range(0, geo.width, WIDE):
            part = dot(pick[: len(shifts) * ROWS, :], ta[:, n : n + WIDE])
            for i, (q, j) in enumerate(shifts):
                gx[q * nx + j, :, n : n + WIDE] = part[i * ROWS : (i + 1) * ROWS]

    def ring_rows(d, k):
        part = (k % 2) ^ d
        return slice(part * PART, (part + 1) * PART)

    def ring_target(d, k, size):
        away = size // 2 - (k + 1) // 2
        return (sign(d) * away) % size

    def z_reduce(d, k):
        value = gz[ring_target(d, k, nz), ring_rows(d, k), :]
        if k >= 2:
            arrived(zin.at[d, k - 2], zrs_s.at[d, k - 2], zrs_r.at[d, k - 2])
            value = value + zin[d, k - 2].astype(f32)
        zout[d, k] = value.astype(bf16)
        to = place(turn(z, sign(d), nz), yh, x)
        start(zout.at[d, k], zin.at[d, k], zrs_s.at[d, k], zrs_r.at[d, k], to)

    def y_early(j):
        yout[1 + j] = gx[j, PART:, :].astype(bf16)
        start(yout.at[1 + j], yin.at[1 + j], yrs_s.at[1 + j], yrs_r.at[1 + j], facing)

    def y_arrived(i):
        arrived(yin.at[i], yrs_s.at[i], yrs_r.at[i])
        return yin[i].astype(f32)

    def x_reduce(q, d, k):
        target = ring_target(d, k, nx)
        value = gx[q * nx + target, ring_rows(d, k), :]
        if (k % 2) ^ d == 1:
            value = value + y_arrived(1 + target)
        if k >= 2:
            arrived(xin.at[q, d, k - 2], xrs_s.at[q, d, k - 2], xrs_r.at[q, d, k - 2])
            value = value + xin[q, d, k - 2].astype(f32)
        xout[q, d, k] = value.astype(bf16)
        to = place(z, yh, turn(x, sign(d), nx))
        start(xout.at[q, d, k], xin.at[q, d, k], xrs_s.at[q, d, k], xrs_r.at[q, d, k], to)

    def ring_last(size):
        return [k for k in (size - 3, size - 2) if k >= 0]

    def x_total(q, c):
        value = gx[q * nx, c * PART : (c + 1) * PART, :]
        for d in range(2):
            for k in ring_last(nx):
                if (k % 2) ^ d == c:
                    arrived(xin.at[q, d, k], xrs_s.at[q, d, k], xrs_r.at[q, d, k])
                    value = value + xin[q, d, k].astype(f32)
        return value

    def z_total(c):
        value = gz[0, c * PART : (c + 1) * PART, :]
        for d in range(2):
            for k in ring_last(nz):
                if (k % 2) ^ d == c:
                    arrived(zin.at[d, k], zrs_s.at[d, k], zrs_r.at[d, k])
                    value = value + zin[d, k].astype(f32)
        return value

    def finish(total, other, unit, inverse, out, c):
        rows = slice(c * PART, (c + 1) * PART)
        grad = scale_ref[0] * (total - other.astype(f32))
        along = jnp.sum(grad * unit[rows, :], axis=-1, keepdims=True)
        out[rows, :] = (inverse[rows, :] * (grad - along * unit[rows, :])).astype(bf16)

    both = range(2)
    kz, kx = nz - 1, nx - 1
    for k in range(min(2, kz)):
        for d in both:
            z_gather(d, k)
    for part in (1, 0):
        for d in both:
            x_gather(part, d, 0)
    y_gather(0, 0)
    y_gather(1, 0)
    for load in loads[2:]:
        load.wait()
    conv_terms(x_ref, g_ref, k_ref, bias_ref, gain_ref, din_ref, terms_ref, xs, gs, ks, cs, ds, bs)
    din_out = pltpu.make_async_copy(din_ref, din_hbm, load_sem.at[len(loads)])
    din_out.start()
    mate_send()

    def z_step(k):
        if k < kz:
            for d in both:
                z_gathered(d, k)
            if k + 2 < kz:
                for d in both:
                    z_gather(d, k + 2)

    z_step(0)
    for d in both:
        x_gathered(1, d, 0)
    x_gather(1, 1, 1)
    y_gather(1, nx - 1)
    y_gather(1, 1)
    y_gathered(0, 0)
    for d in both:
        x_gather(0, d, 0, True)
    for d in both:
        x_gathered(0, d, 0)
    x_gather(0, 0, 1)
    z_step(1)
    mate_sum()
    y_send()
    x_gathered(1, 1, 1)
    y_gather(1, 2)
    pairs = nz * ROWS // WIDE
    count = nx * ROWS // WIDE
    lean = 2 * lax.rem(z, 2) - 1
    near = 2 * (z // 2)
    next_pair = 2 * turn(z // 2, lean, pairs)
    far_pair = 2 * turn(z // 2, -lean, pairs)
    ours, theirs = yh * count, hy * count
    z_step(2)
    for d in both:
        x_gathered(0, d, 0, True)
    x_gather(0, 0, 1, True)
    x_gathered(0, 0, 1)
    logits_block(near, WIDE, ours, count)
    z_step(3)
    logits_block(next_pair, WIDE, ours, count)
    for j in (0, nx - 1, 1):
        y_gathered(1, j)
    x_gathered(0, 0, 1, True)
    z_step(4)
    y_sum()
    x_send()
    y_gathered(1, 2)
    logits_block(near, WIDE, theirs, count)
    logits_block(next_pair, WIDE, theirs, count)
    for k in range(5, kz - 1):
        z_step(k)
    x_sum()
    logits_block(far_pair, WIDE, 0, 2 * count)
    logits_block(late + 1 - 2 * lax.rem(late, 2), ROWS, 0, 2 * count)
    z_step(kz - 1)
    logits_block(late, ROWS, 0, 2 * count, True)
    for m in range(sheet):
        rows = slice(m * ROWS, (m + 1) * ROWS)
        row_raw[m : m + 1, :] = jnp.sum(row_hi[rows, :].T, axis=0, keepdims=True)
        row_raw[8 + m : 9 + m, :] = jnp.sum(row_lo[rows, :].T, axis=0, keepdims=True)
    row_all[b] = local_lse(row_raw[...])
    col_all[z] = local_lse(col_raw[...])
    for q in both:
        for o in range(nx):
            if q or o:
                i = q * nx + o
                to = place(z, hy if q else yh, turn(x, o, nx))
                start(row_all.at[b], row_all.at[b], row_s.at[i], row_r.at[i], to)
    for o in range(1, nz):
        start(col_all.at[z], col_all.at[z], col_s.at[o], col_r.at[o], place(turn(z, o, nz), yh, x))
    z_send()
    for o in range(1, nz):
        arrived(col_all.at[turn(z, -o, nz)], col_s.at[o], col_r.at[o])
    beta[...] = half_factor(col_all, nz)
    for q in both:
        for o in range(nx):
            if q or o:
                i = q * nx + o
                arrived(row_all.at[(hy if q else yh) * nx + turn(x, -o, nx)], row_s.at[i], row_r.at[i])
    factor = half_factor(row_all, sheet)
    for m in range(sheet):
        rows = slice(m * ROWS, (m + 1) * ROWS)
        alpha[rows, :] = jnp.broadcast_to(factor[m : m + 1, :], (ROWS, ROWS)).T

    def z_stage(k):
        if k < kz:
            for d in both:
                z_reduce(d, k)

    half = nz // 2
    weigh(turn(z, half, nz))
    text_part(half)
    z_stage(0)

    @pl.loop(0, nz - 1)
    def _(i):
        weigh(turn(z, i - (half - 1), nz))

    image_part((0, 2), (0, 3))
    x_reduce(0, 0, 0)
    x_reduce(0, 1, 1)
    y_early(2)
    y_early(3)
    text_part(half - 1, nz - half + 1)
    z_stage(1)
    z_sum()
    x_spread()
    image_part((0, 1), (0, 0))
    y_early(1)
    image_part((1, 2), (1, 3))
    x_reduce(1, 0, 0)
    x_reduce(1, 1, 1)
    z_stage(2)
    x_reduce(0, 0, 2)
    image_part((1, 1), (1, 0))
    x_spread_done()
    y_spread()
    x_reduce(1, 1, 0)
    text_part(half - 2, nz - half + 2)
    z_stage(3)
    x_reduce(1, 0, 2)
    z_stage(4)
    x_reduce(1, 0, 1)
    yout[0] = x_total(0, 0).astype(bf16)
    start(yout.at[0], yin.at[0], yrs_s.at[0], yrs_r.at[0], facing)
    y_early(0)
    text_part(half - 3, nz - half + 3)
    z_stage(5)
    x_reduce(1, 1, 2)
    y_spread_done()
    mate_spread()
    z_stage(6)
    text_part(0)
    mate_spread_done()
    for row in range(KS):
        for t in range(TILES):
            kg_ref[row, :, t * LANES : (t + 1) * LANES] = fin[
                pl.ds(row * KS * TILES + t, KS, stride=TILES), :
            ]
    for t in range(TILES):
        cg_ref[:, t * LANES : (t + 1) * LANES] = fin[pl.ds(SPOTS * TILES + t, 3, stride=TILES), :]
    kg_out = pltpu.make_async_copy(kg_ref, kg_hbm, load_sem.at[len(loads) + 1])
    kg_out.start()
    cg_out = pltpu.make_async_copy(cg_ref, cg_hbm, load_sem.at[len(loads) + 2])
    cg_out.start()
    for c in both:
        value = x_total(1, c) + y_arrived(c)
        finish(value, ta[slot(z, c), :], ui, vi, ig_ref, c)
    ig_out = pltpu.make_async_copy(ig_ref, ig_hbm, load_sem.at[len(loads) + 3])
    ig_out.start()
    tg_out = []
    for c in both:
        finish(z_total(c), ia[slot(b, c), :], ut, vt, tg_ref, c)
        rows = pl.ds(c * PART, PART)
        tg_out.append(pltpu.make_async_copy(tg_ref.at[rows], tg_hbm.at[rows], load_sem.at[len(loads) + 4 + c]))
        tg_out[c].start()
    for moving in sent:
        moving.wait_send()
    for leaving in (din_out, kg_out, cg_out, ig_out, *tg_out):
        leaving.wait()


def loss_block(geo, scale, image_rows, text_rows, x, g, k, bias, gain):
    f32, bf16 = jnp.float32, jnp.bfloat16
    vmem = pltpu.VMEM
    dma = pltpu.SemaphoreType.DMA
    images, texts, width = geo.sheet * ROWS, geo.z * ROWS, geo.width
    kz, kx = geo.z - 1, geo.x - 1
    big = vmem((SPOTS * TILES + TILES, LANES), f32)
    maps = vmem((GRID, GRID, TILES * LANES), bf16)
    scratch = [
        vmem((ROWS, width), bf16), vmem((ROWS, width), bf16), vmem((3, TILES * LANES), f32),
        maps, vmem((KS, KS, TILES * LANES), f32), vmem((ROWS, width), bf16), vmem((ROWS, width), bf16), maps, maps, maps,
        vmem((TILES * LANES,), bf16), vmem((TILES * LANES,), bf16), vmem((SLACK, LANES), f32),
        big, big, big, big, big, vmem((2 * TILES, LANES), f32), dma((13,)),
        vmem((images, width), bf16), vmem((texts, width), bf16),
        vmem((ROWS, width), f32), vmem((ROWS, width), f32), vmem((ROWS, 1), f32), vmem((ROWS, 1), f32),
        vmem((images, texts), f32), vmem((images, texts), bf16), vmem((2 * ROWS, images), bf16), vmem((2 * ROWS, texts), bf16),
        vmem((images, ROWS), f32), vmem((images, ROWS), f32), vmem((images, ROWS), f32), vmem((8, ROWS), f32),
        vmem((16, ROWS), f32), vmem((16, ROWS), f32),
        vmem((geo.sheet, 8, ROWS), f32), vmem((geo.z, 8, ROWS), f32),
        vmem((geo.z, ROWS, width), f32), vmem((2 * geo.x, ROWS, width), f32),
        vmem((2, kz, PART, width), bf16), vmem((2, kz, PART, width), bf16),
        vmem((2, 2, kx, PART, width), bf16), vmem((2, 2, kx, PART, width), bf16),
        vmem((1 + geo.x, PART, width), bf16), vmem((1 + geo.x, PART, width), bf16),
        vmem((geo.half, LANES), f32), vmem((geo.half, LANES), f32),
        vmem((geo.y, geo.y_rows, LANES), f32), vmem((geo.y_rows, LANES), f32),
        vmem((geo.x, geo.x_rows, LANES), f32), vmem((geo.z, geo.x_rows, LANES), f32), vmem((SLACK, LANES), f32),
        dma((2, kz)), dma((2, kz)), dma((3, 2, 2)), dma((3, 2, 2)), dma((1 + geo.x,)), dma((1 + geo.x,)),
        dma((geo.sheet,)), dma((geo.sheet,)), dma((geo.z,)), dma((geo.z,)),
        dma((2, kz)), dma((2, kz)), dma((2, 2, kx)), dma((2, 2, kx)), dma((1 + geo.x,)), dma((1 + geo.x,)),
        dma((1,)), dma((1,)), dma((geo.y,)), dma((geo.y,)), dma((geo.x,)), dma((geo.x,)), dma((geo.z,)), dma((geo.z,)),
        dma((geo.x,)), dma((geo.x,)), dma((geo.y,)), dma((geo.y,)), dma((1,)), dma((1,)),
    ]
    return pl.pallas_call(
        functools.partial(loss_kernel, geo),
        out_shape=(
            jax.ShapeDtypeStruct((ROWS, width), bf16),
            jax.ShapeDtypeStruct((ROWS, width), bf16),
            jax.ShapeDtypeStruct((3, TILES * LANES), f32),
            jax.ShapeDtypeStruct((GRID, GRID, TILES * LANES), bf16),
            jax.ShapeDtypeStruct((KS, KS, TILES * LANES), f32),
        ),
        in_specs=[pl.BlockSpec(memory_space=pltpu.SMEM)] + [pl.BlockSpec(memory_space=pltpu.HBM)] * 7,
        out_specs=[pl.BlockSpec(memory_space=pltpu.HBM)] * 5,
        scratch_shapes=scratch,
        compiler_params=pltpu.CompilerParams(
            collective_id=0, has_side_effects=True, vmem_limit_bytes=60 << 20
        ),
    )(scale.reshape(1), image_rows, text_rows, x, g, k, bias, gain)


def hand_out_kernel(*refs):
    count = (len(refs) - 2) // 3
    into, away = refs[-2], refs[-1]
    loads = [pltpu.make_async_copy(refs[i], refs[2 * count + i], into.at[i]) for i in range(count)]
    stores = [pltpu.make_async_copy(refs[2 * count + i], refs[count + i], away.at[i]) for i in range(count)]
    for moving in loads:
        moving.start()
    for load, store in zip(loads, stores):
        load.wait()
        store.start()
    for moving in stores:
        moving.wait()


def hand_out(*arrays):
    held = [pl.BlockSpec(memory_space=pltpu.HBM)] * len(arrays)
    sems = pltpu.SemaphoreType.DMA((len(arrays),))
    return pl.pallas_call(
        hand_out_kernel,
        out_shape=tuple(jax.ShapeDtypeStruct(a.shape, a.dtype) for a in arrays),
        in_specs=held,
        out_specs=held,
        scratch_shapes=[pltpu.VMEM(a.shape, a.dtype) for a in arrays] + [sems, sems],
        compiler_params=pltpu.CompilerParams(vmem_limit_bytes=60 << 20),
    )(*arrays)


def per_device(
    geo, image_embed, text_embed, logit_scale, block_input, dw_kernel, dw_bias, ln_gain, block_grad
):
    image_grad, text_grad, channel_grads, d_input, kernel_grad = hand_out(
        *loss_block(
            geo, logit_scale, image_embed[0], text_embed[0],
            block_input[0], block_grad[0], dw_kernel, dw_bias, ln_gain,
        )
    )
    return (image_grad[None], text_grad[None], d_input[None], kernel_grad, channel_grads)


def solution(mesh, geo=None):
    geo = geo or Geometry(8, 2, 4, 2, 2, 1024)
    placed = (
        P("grp", "blk", None),
        P("grp", "blk", None),
        P(),
        P(("blk", "grp"), None, None, None),
        P(),
        P(),
        P(),
        P(("blk", "grp"), None, None, None),
    )
    return jax.shard_map(
        functools.partial(per_device, geo),
        mesh=mesh,
        in_specs=placed,
        out_specs=(
            P("grp", "blk", None),
            P("grp", "blk", None),
            P(("blk", "grp"), None, None, None),
            P(),
            P(),
        ),
        check_vma=False,
    )
```
